32 devices in a mesh: section: 2 (over y), dp: 4 (over z), tensor: 4 (over x, core).
Axes of the slice: x: 2, y: 2, z: 4, core: 2. Of those that a mesh axis runs over, the one named last changes fastest.
Arguments:
- layer_input: bfloat16 [2, 8, 512, 768], P('section', 'dp', 'tensor'), may hold values from -6 to 6
- dec_lengths: int32 [8], P('dp'), may hold values from 256 to 512, as said below
- out_cotangent: bfloat16 [8, 512, 768], P('dp', 'tensor'), may hold values from -6 to 6
- gains: float32 [2, 3, 768], P('section'), may hold values from 0.25 to 1.75
- attn_weights: bfloat16 [2, 6, 768, 768], P('section', None, None, 'tensor'), may hold values from -2.44948974 to 2.44948974
- ffn_weights: bfloat16 [2, 3, 768, 2048], P('section', None, None, 'tensor'), may hold values from -0.21875 to 0.21875
Outputs:
- block_out: bfloat16 [2, 8, 512, 768], P('section', 'dp', 'tensor')
- input_grad: bfloat16 [2, 8, 512, 768], P('section', 'dp', 'tensor')
- gain_grad: float32 [2, 3, 768], P('section')
- attn_grad: float32 [2, 6, 768, 768], P('section', None, None, 'tensor')
- ffn_grad: float32 [2, 3, 768, 2048], P('section', None, None, 'tensor')
The draws below stay inside these ranges and needn't reach their ends.
Inputs may be any that keep to these rules, and one draw needn't show every extreme that they name: `dec_lengths`: each row has either 512 or half of 512 live decoder tokens at its start; some row has 512 and some row half of 512.
All inputs are finite; a program needn't handle non-finite values.
Results may differ from the reference program's by a relative error of at most 0.03.
Values may be sent and summed in bfloat16 or wider, within the bound.
No kernel may reach another device: no remote copies, remote signals or barrier semaphores. Data moves between devices by JAX's collectives and lax.ppermute only.
A program may use at most 192 MiB of HBM per device.

```python
import jax
import jax.numpy as jnp
from jax import lax

D = 768
HEADS = 12
DH = 64
FF = 2048
SEQ = 512
BATCH = 8


def draw_dec_lengths(key, part):
    key = jax.random.fold_in(key, 11)
    first_key, second_key = jax.random.split(key)
    halves = jax.random.randint(first_key, (BATCH,), 0, 2)
    chosen = jax.random.randint(second_key, (), 0, BATCH)
    row_ids = jnp.arange(BATCH)
    halves = jnp.where(row_ids == chosen, 0, halves)
    halves = jnp.where(row_ids == (chosen + 1) % BATCH, 1, halves)
    return (SEQ - SEQ // 2 * halves).astype(jnp.int32)


def draw_attn_weights(key, part):
    key = jax.random.fold_in(key, 23)
    base = jnp.clip(jax.random.normal(key, (2, 6, D, HEADS * DH), jnp.float32), -6.0, 6.0)
    section_ids = jnp.arange(2)[:, None]
    slot_ids = jnp.arange(6)[None, :]
    outward = (slot_ids == 3) | (section_ids == 1) & (slot_ids == 5)
    scales = jnp.where(outward, 0.5 * (SEQ / (HEADS * DH)) ** 0.5, D ** (-0.5))
    return (base * scales[:, :, None, None]).astype(jnp.bfloat16)


def shard_levels(key, dims, shards, low, high):
    def one(dim, shards_of):
        heights = jax.random.uniform(jax.random.fold_in(jax.random.fold_in(key, 6), dim), (shards_of,), jnp.float32, low / len(shards), high / len(shards))
        return jnp.repeat(jnp.exp(heights), dims[dim] // shards_of).reshape((-1,) + (1,) * (len(dims) - dim - 1))

    gain = one(*shards[0])
    for cut in shards[1:]:
        gain = gain * one(*cut)
    return gain


def noise(key, shape, deviation, most, shards=(), kind=jnp.bfloat16):
    array = jax.random.normal(key, shape, jnp.float32) * deviation
    if len(shards) > 0:
        array = shard_levels(key, shape, shards, -0.22, 0.18) * array
    return jnp.clip(array, min=-most, max=most).astype(kind)


def setup_inputs(seed: int = 0) -> dict:
    arg_keys = jax.random.split(jax.random.key(seed), 7)
    layer_input = noise(arg_keys[0], (2, BATCH, SEQ, D), 1.0, 6.0, ((0, 2), (1, 4), (2, 4)))
    dec_lengths = draw_dec_lengths(jax.random.fold_in(arg_keys[6], 71), 0)
    out_cotangent = noise(arg_keys[2], (BATCH, SEQ, D), 1.0, 6.0, ((0, 4), (1, 4)))
    gains = jnp.clip(1.0 + 0.15 * jax.random.normal(arg_keys[3], (2, 3, D), jnp.float32), 0.25, 1.75)
    attn_weights = draw_attn_weights(jax.random.fold_in(arg_keys[6], 71), 0)
    ffn_weights = noise(arg_keys[5], (2, 3, D, FF), D ** -0.5, 0.21875, ((0, 2), (3, 4)))
    return {"layer_input": layer_input, "dec_lengths": dec_lengths, "out_cotangent": out_cotangent, "gains": gains, "attn_weights": attn_weights, "ffn_weights": ffn_weights}


EPSILON = 1e-06
NEGATIVE = -1e+30
HIGHEST = lax.Precision.HIGHEST

@jax.custom_vjp
def low(v):
    return lax.optimization_barrier(v.astype(jnp.bfloat16)).astype(jnp.float32)

@jax.custom_vjp
def low_back(v):
    return v

def low_keep(v):
    return (low(v), None)

def low_pass(kept, grad):
    return (grad,)

def back_keep(v):
    return (v, None)

def back_low(kept, grad):
    return (low(grad),)
low.defvjp(low_keep, low_pass)
low_back.defvjp(back_keep, back_low)

def both_ways(values):
    return low_back(low(values))

def matmul(left_side, right_side):
    return jnp.dot(left_side, right_side, precision=HIGHEST)

def normalize(values, gain_row):
    return gain_row * values * lax.rsqrt(lax.optimization_barrier(jnp.mean(values * values, axis=-1, keepdims=True)) + EPSILON)

def attention(queries, keys_in, values_in, causal):
    length = queries.shape[0]
    key_count = keys_in.shape[0]
    query_heads = queries.reshape(length, HEADS, DH)
    key_heads = keys_in.reshape(key_count, HEADS, DH)
    value_heads = values_in.reshape(key_count, HEADS, DH)
    raw_scores = jnp.einsum('qhd,khd->hqk', query_heads, key_heads, precision=HIGHEST) * DH ** (-0.5)
    if causal:
        allowed = jnp.arange(key_count)[None, :] <= jnp.arange(length)[:, None]
        raw_scores = jnp.where(allowed[None], raw_scores, NEGATIVE)
    scores = low_back(raw_scores)
    probabilities = jax.nn.softmax(scores, axis=-1)
    attended = jnp.einsum('hqk,khd->qhd', low(probabilities), value_heads, precision=HIGHEST)
    return both_ways(attended.reshape(length, HEADS * DH))

def self_block(normed, attn_set, causal):
    queries = both_ways(matmul(normed, attn_set[0]))
    keys_in = both_ways(matmul(normed, attn_set[1]))
    values_in = both_ways(matmul(normed, attn_set[2]))
    attended = attention(queries, keys_in, values_in, causal)
    return low_back(matmul(attended, attn_set[3].T))

def feed_forward(normed, ffn_set):
    gate_sum = low_back(matmul(normed, ffn_set[0]))
    up_sum = low_back(matmul(normed, ffn_set[1]))
    hidden = low(jax.nn.gelu(gate_sum) * up_sum)
    return low_back(matmul(hidden, ffn_set[2].T))

def encoder(block_in, gain_set, attn_set, ffn_set):
    after_self = block_in + self_block(low(normalize(block_in, gain_set[0])), attn_set, False)
    after_ffn = after_self + feed_forward(low(normalize(after_self, gain_set[1])), ffn_set)
    memory = low(normalize(after_ffn, gain_set[2]))
    cross_keys = both_ways(matmul(memory, attn_set[4]))
    cross_values = both_ways(matmul(memory, attn_set[5]))
    return (memory, cross_keys, cross_values)

def decoder(block_in, cross_keys, cross_values, gain_set, attn_set, ffn_set):
    after_self = block_in + self_block(low(normalize(block_in, gain_set[0])), attn_set, True)
    cross_query = both_ways(matmul(low(normalize(after_self, gain_set[1])), attn_set[4]))
    attended = attention(cross_query, cross_keys, cross_values, False)
    after_cross = after_self + low_back(matmul(attended, attn_set[5].T))
    return after_cross + feed_forward(low(normalize(after_cross, gain_set[2])), ffn_set)

def reference(layer_input, dec_lengths, out_cotangent, gains, attn_weights, ffn_weights):
    inputs = layer_input.astype(jnp.float32)
    cotangents = out_cotangent.astype(jnp.float32)
    gain_all = gains.astype(jnp.float32)
    attn_all = attn_weights.astype(jnp.float32)
    ffn_all = ffn_weights.astype(jnp.float32)
    positions = jnp.arange(SEQ, dtype=jnp.int32)

    def one_row(totals, row_data):
        encoder_in, decoder_in, length, cotangent = row_data
        live_mask = (positions < length).astype(jnp.float32)[:, None]

        def forward(encoder_x, decoder_x, gain_set, attn_set, ffn_set):
            memory, cross_keys, cross_values = encoder(encoder_x, gain_set[0], attn_set[0], ffn_set[0])
            produced = decoder(decoder_x, cross_keys, cross_values, gain_set[1], attn_set[1], ffn_set[1])
            return (memory, produced * live_mask)
        outputs, pullback = jax.vjp(forward, encoder_in, decoder_in, gain_all, attn_all, ffn_all)
        memory, produced = outputs
        grad_encoder, grad_decoder, grad_gain, grad_attn, grad_ffn = pullback((jnp.zeros(memory.shape, jnp.float32), cotangent))
        totals = (totals[0] + grad_gain, totals[1] + grad_attn, totals[2] + grad_ffn)
        return (totals, (memory, produced, grad_encoder, grad_decoder))
    begin_state = (jnp.zeros(gain_all.shape, jnp.float32), jnp.zeros(attn_all.shape, jnp.float32), jnp.zeros(ffn_all.shape, jnp.float32))
    totals, stacked = lax.scan(one_row, begin_state, (inputs[0], inputs[1], dec_lengths, cotangents))
    memory_all, produced_all, grad_encoder, grad_decoder = stacked
    block_out = jnp.stack([memory_all, produced_all]).astype(jnp.bfloat16)
    input_grad = jnp.stack([grad_encoder, grad_decoder]).astype(jnp.bfloat16)
    return (block_out, input_grad, totals[0], totals[1], totals[2])
```

```python
import functools

import jax
import jax.numpy as jnp
from jax import lax
from jax.experimental import pallas as pl
from jax.experimental.pallas import tpu as pltpu
from jax.sharding import PartitionSpec as P

DH = 64
EPSILON = 1e-06
NEGATIVE = -1e30
F32 = jnp.float32
BF16 = jnp.bfloat16
VMEM = 56 * 1024 * 1024
NT = (((1,), (1,)), ((), ()))
NN = (((1,), (0,)), ((), ()))
TN = (((0,), (0,)), ((), ()))


def mm(left, right, dims=NN):
    return lax.dot_general(left, right, dims, preferred_element_type=F32)


def params():
    return pltpu.CompilerParams(vmem_limit_bytes=VMEM)


def head_scores(q, k, allowed):
    s = mm(k, q, NT)
    return s if allowed is None else jnp.where(allowed, s, NEGATIVE)


def allowed_mask(enc, length):
    key_pos = lax.broadcasted_iota(jnp.int32, (length, length), 0)
    query_pos = lax.broadcasted_iota(jnp.int32, (length, length), 1)
    return key_pos <= query_pos + enc * length


def attend_kernel(masked, enc_ref, q_ref, kv_ref, out_ref, lse_ref, width, q0, k0, v0):
    length = q_ref.shape[0]
    allowed = allowed_mask(enc_ref[0], length) if masked else None
    for h in range(width // DH):
        lo = h * DH
        q = q_ref[:, q0 + lo : q0 + lo + DH] * BF16(DH**-0.5)
        k = kv_ref[:, k0 + lo : k0 + lo + DH]
        v = kv_ref[:, v0 + lo : v0 + lo + DH]
        s = head_scores(q, k, allowed)
        top = jnp.max(s, axis=0, keepdims=True)
        e = jnp.exp(s - top)
        total = jnp.sum(e, axis=0, keepdims=True)
        o = mm(v.T, e.astype(BF16)) * (1.0 / total)
        out_ref[:, lo : lo + DH] = o.T.astype(BF16)
        lse_ref[h : h + 1, :] = top + jnp.log(total)


def attend_back_kernel(
    masked, enc_ref, q_ref, kv_ref, lse_ref, g_ref, dq_ref, dkv_ref, width, q0, k0, v0, shared
):
    length = q_ref.shape[0]
    allowed = allowed_mask(enc_ref[0], length) if masked else None
    for h in range(width // DH):
        lo = h * DH
        q = q_ref[:, q0 + lo : q0 + lo + DH] * BF16(DH**-0.5)
        k = kv_ref[:, k0 + lo : k0 + lo + DH]
        v = kv_ref[:, v0 + lo : v0 + lo + DH]
        g = g_ref[:, lo : lo + DH]
        p = jnp.exp(head_scores(q, k, allowed) - lse_ref[h : h + 1, :])
        dp = mm(v, g, NT)
        delta = jnp.sum(p * dp, axis=0, keepdims=True)
        ds = (p * (dp - delta)).astype(BF16)
        dv = mm(p.astype(BF16), g)
        dk = mm(ds, q)
        dq = mm(k.T, ds) * (DH**-0.5)
        dq_ref[:, q0 + lo : q0 + lo + DH] = dq.T.astype(BF16)
        dkv_ref[:, k0 + lo : k0 + lo + DH] = dk.astype(BF16)
        dkv_ref[:, v0 + lo : v0 + lo + DH] = dv.astype(BF16)


def row_block(length, width):
    return pl.BlockSpec((length, width), lambda i: (i, 0))


SMEM_SPEC = pl.BlockSpec(memory_space=pltpu.SMEM)


def self_attend(enc, qkv, length):
    width = qkv.shape[1] // 3
    heads = width // DH
    rows = qkv.shape[0] // length

    def kernel(enc_ref, qkv_ref, out_ref, lse_ref):
        attend_kernel(
            True, enc_ref, qkv_ref, qkv_ref, out_ref, lse_ref.at[0], width, 0, width, 2 * width
        )

    return pl.pallas_call(
        kernel,
        grid=(rows,),
        in_specs=[SMEM_SPEC, row_block(length, 3 * width)],
        out_specs=[
            row_block(length, width),
            pl.BlockSpec((1, heads, length), lambda i: (i, 0, 0)),
        ],
        out_shape=[
            jax.ShapeDtypeStruct((rows * length, width), BF16),
            jax.ShapeDtypeStruct((rows, heads, length), F32),
        ],
        compiler_params=params(),
        name="self_attend",
    )(enc, qkv)


def cross_attend(enc, q, kv, length):
    width = q.shape[1]
    heads = width // DH
    rows = q.shape[0] // length

    def kernel(enc_ref, q_ref, kv_ref, out_ref, lse_ref):
        attend_kernel(False, enc_ref, q_ref, kv_ref, out_ref, lse_ref.at[0], width, 0, 0, width)

    return pl.pallas_call(
        kernel,
        grid=(rows,),
        in_specs=[SMEM_SPEC, row_block(length, width), row_block(length, 2 * width)],
        out_specs=[
            row_block(length, width),
            pl.BlockSpec((1, heads, length), lambda i: (i, 0, 0)),
        ],
        out_shape=[
            jax.ShapeDtypeStruct((rows * length, width), BF16),
            jax.ShapeDtypeStruct((rows, heads, length), F32),
        ],
        compiler_params=params(),
        name="cross_attend",
    )(enc, q, kv)


def self_attend_back(enc, qkv, lse, g, length):
    width = qkv.shape[1] // 3
    heads = width // DH
    rows = qkv.shape[0] // length

    def kernel(enc_ref, qkv_ref, lse_ref, g_ref, d_ref):
        attend_back_kernel(
            True, enc_ref, qkv_ref, qkv_ref, lse_ref.at[0], g_ref, d_ref, d_ref,
            width, 0, width, 2 * width, True,
        )

    return pl.pallas_call(
        kernel,
        grid=(rows,),
        in_specs=[
            SMEM_SPEC,
            row_block(length, 3 * width),
            pl.BlockSpec((1, heads, length), lambda i: (i, 0, 0)),
            row_block(length, width),
        ],
        out_specs=row_block(length, 3 * width),
        out_shape=jax.ShapeDtypeStruct((rows * length, 3 * width), BF16),
        compiler_params=params(),
        name="self_attend_back",
    )(enc, qkv, lse, g)


def cross_attend_back(enc, q, kv, lse, g, length):
    width = q.shape[1]
    heads = width // DH
    rows = q.shape[0] // length

    def kernel(enc_ref, q_ref, kv_ref, lse_ref, g_ref, dq_ref, dkv_ref):
        attend_back_kernel(
            False, enc_ref, q_ref, kv_ref, lse_ref.at[0], g_ref, dq_ref, dkv_ref,
            width, 0, 0, width, False,
        )

    return pl.pallas_call(
        kernel,
        grid=(rows,),
        in_specs=[
            SMEM_SPEC,
            row_block(length, width),
            row_block(length, 2 * width),
            pl.BlockSpec((1, heads, length), lambda i: (i, 0, 0)),
            row_block(length, width),
        ],
        out_specs=[row_block(length, width), row_block(length, 2 * width)],
        out_shape=[
            jax.ShapeDtypeStruct((rows * length, width), BF16),
            jax.ShapeDtypeStruct((rows * length, 2 * width), BF16),
        ],
        compiler_params=params(),
        name="cross_attend_back",
    )(enc, q, kv, lse, g)


def normalize(values, gain_row):
    factor = lax.rsqrt(jnp.mean(values * values, axis=-1, keepdims=True) + EPSILON)
    return (values * factor * gain_row).astype(BF16)


def normalize_back(values, gain_row, u):
    factor = lax.rsqrt(jnp.mean(values * values, axis=-1, keepdims=True) + EPSILON)
    scaled = u * gain_row
    grad_gain = jnp.sum(u * values * factor, axis=0)
    inner = jnp.mean(scaled * values, axis=-1, keepdims=True)
    return (factor * scaled - values * (factor * factor * factor * inner), grad_gain)


def gelu_parts(v):
    c = 0.7978845608028654
    inner = c * (v + 0.044715 * v * v * v)
    t = jnp.tanh(inner)
    value = 0.5 * v * (1.0 + t)
    slope = 0.5 * (1.0 + t) + 0.5 * v * (1.0 - t * t) * (c * (1.0 + 3 * 0.044715 * v * v))
    return value, slope


def on_device(layer_input, dec_lengths, out_cotangent, gains, attn_weights, ffn_weights):
    tensor = lax.axis_size("tensor")
    sections = lax.axis_size("section")
    planes = lax.axis_size("dp")
    batch, part_len, model = layer_input.shape[1:]
    groups = 2 if tensor % 2 == 0 and batch % 2 == 0 else 1
    cores = tensor // groups
    rows = batch // groups
    length = part_len * tensor
    tokens = rows * length
    width = attn_weights.shape[3]
    hidden_width = ffn_weights.shape[3]

    section = lax.axis_index("section")
    plane = lax.axis_index("dp")
    lane = lax.axis_index("tensor")
    group = lane // cores
    core = lane % cores
    enc = (section == 0).astype(jnp.int32).reshape(1)
    is_enc = section == 0

    def over_groups(value):
        return lax.ppermute(value, "tensor", [(t, (t + cores) % tensor) for t in range(tensor)])

    def over_cores(value):
        return lax.ppermute(value, "tensor", [(t, t ^ 1) for t in range(tensor)])

    def core_sum(part):
        part = part.astype(BF16)
        if cores == 1:
            return part.astype(F32)
        if cores == 2:
            return part.astype(F32) + over_cores(part).astype(F32)
        together = [[g * cores + c for c in range(cores)] for g in range(groups)]
        return lax.psum(part, "tensor", axis_index_groups=together).astype(F32)

    def pick(value, index, count):
        return lax.dynamic_slice_in_dim(value, index * count, count, 0)

    def to_rows(value):
        if groups == 1:
            blocks = value[:, None]
        else:
            mine = pick(value, group, rows)
            got = over_groups(pick(value, 1 - group, rows))
            first = group == 0
            blocks = jnp.stack([jnp.where(first, mine, got), jnp.where(first, got, mine)], 1)
        if cores == 2:
            got = over_cores(blocks)
            low = core == 0
            blocks = jnp.stack([jnp.where(low, blocks, got), jnp.where(low, got, blocks)], 2)
        elif cores > 2:
            together = [[g * cores + c for c in range(cores)] for g in range(groups)]
            blocks = lax.all_gather(blocks, "tensor", axis=2, axis_index_groups=together)
        return blocks.reshape(tokens, model)

    def from_rows(value):
        blocks = value.reshape(rows, tensor, part_len, model)
        mine = lax.dynamic_index_in_dim(blocks, lane, 1, keepdims=False)
        if groups == 1:
            return mine
        got = over_groups(
            lax.dynamic_index_in_dim(blocks, (lane + cores) % tensor, 1, keepdims=False)
        )
        first = group == 0
        return jnp.concatenate([jnp.where(first, mine, got), jnp.where(first, got, mine)], 0)

    attn = attn_weights[0]
    ffn = ffn_weights[0]
    gain = gains[0]

    own_self = jnp.concatenate([attn[0], attn[1], attn[2], attn[3]], axis=1)
    own_side = jnp.concatenate([attn[4], attn[5]], axis=1)
    x_in = to_rows(layer_input[0])
    cot_rows = to_rows(out_cotangent)
    if groups == 2:
        other_self = over_groups(own_self)
        other_ffn = [over_groups(ffn[0]), over_groups(ffn[1]), over_groups(ffn[2])]
        other_side = over_groups(own_side)
        w_self = [own_self, other_self]
        w_side = [own_side, other_side]
        w_ffn = [[ffn[0], ffn[1], ffn[2]], other_ffn]
    else:
        w_self, w_side, w_ffn = [own_self], [own_side], [[ffn[0], ffn[1], ffn[2]]]
    shares = range(groups)

    x = x_in.astype(F32)
    a0 = normalize(x, gain[0])
    qkv, att, lse = [], [], []
    part = 0.0
    for i in shares:
        qkv.append(mm(a0, w_self[i][:, : 3 * width]).astype(BF16))
        o, l = self_attend(enc, qkv[i], length)
        att.append(o)
        lse.append(l)
        part = part + mm(o, w_self[i][:, 3 * width :], NT)
    x1 = x + core_sum(part)
    a1 = normalize(x1, gain[1])

    def ffn_up(a):
        gate = [mm(a, w_ffn[i][0]) for i in shares]
        up = [mm(a, w_ffn[i][1]) for i in shares]
        hidden = [(gelu_parts(gate[i])[0] * up[i]).astype(BF16) for i in shares]
        return gate, up, hidden

    def ffn_down(hidden):
        return sum(mm(hidden[i], w_ffn[i][2], NT) for i in shares)

    def ffn_back(grad, gate, up):
        d_gate, d_up = [], []
        part = 0.0
        for i in shares:
            dh = mm(grad, w_ffn[i][2])
            value, slope = gelu_parts(gate[i])
            d_gate.append((dh * up[i] * slope).astype(BF16))
            d_up.append((dh * value).astype(BF16))
            part = part + mm(d_gate[i], w_ffn[i][0], NT) + mm(d_up[i], w_ffn[i][1], NT)
        return d_gate, d_up, part

    e_gate, e_up, e_hidden = ffn_up(a1)
    y = x1 + core_sum(ffn_down(e_hidden))
    memory = normalize(y, gain[2])
    kv = [mm(memory, w_side[i]).astype(BF16) for i in shares]
    kv = [lax.ppermute(v, "section", [(0, 1)]) for v in kv]

    cq = [mm(a1, w_side[i][:, :width]).astype(BF16) for i in shares]
    catt, clse = [], []
    part = 0.0
    for i in shares:
        o, l = cross_attend(enc, cq[i], kv[i], length)
        catt.append(o)
        clse.append(l)
        part = part + mm(o, w_side[i][:, width:], NT)
    x2 = x1 + core_sum(part)
    a2 = normalize(x2, gain[2])
    row_ids = group * rows + jnp.arange(rows)
    live = (jnp.arange(length)[None, :] < dec_lengths[row_ids][:, None]).astype(F32)
    live = live.reshape(tokens, 1)
    gy = cot_rows.astype(F32) * live
    gy_low = gy.astype(BF16)
    d_gate, d_up, d_hidden = ffn_up(a2)
    dd_gate, dd_up, part = ffn_back(gy_low, d_gate, d_up)
    da2 = core_sum(part)
    back, d_gain2 = normalize_back(x2, gain[2], da2)
    g2 = gy + back
    g2_low = g2.astype(BF16)
    dcq, dkv = [], []
    part_dec = 0.0
    for i in shares:
        dcatt = mm(g2_low, w_side[i][:, width:]).astype(BF16)
        a, b = cross_attend_back(enc, cq[i], kv[i], clse[i], dcatt, length)
        dcq.append(a)
        dkv.append(b)
        part_dec = part_dec + mm(a, w_side[i][:, :width], NT)
    dkv = [lax.ppermute(v, "section", [(1, 0)]) for v in dkv]
    dec_y = x2 + core_sum(ffn_down(d_hidden))

    part = 0.0
    for i in shares:
        part = part + mm(dkv[i], w_side[i], NT)
    dmem = core_sum(part)
    e_g, e_gain2 = normalize_back(y, gain[2], dmem)
    e_g_low = e_g.astype(BF16)
    de_gate, de_up, part_enc = ffn_back(e_g_low, e_gate, e_up)
    da1 = core_sum(jnp.where(is_enc, part_enc, part_dec))

    back, gain1 = normalize_back(x1, gain[1], da1)
    g1 = jnp.where(is_enc, e_g, g2) + back
    g1_low = g1.astype(BF16)
    dqkv = []
    part = 0.0
    for i in shares:
        datt = mm(g1_low, w_self[i][:, 3 * width :]).astype(BF16)
        dqkv.append(self_attend_back(enc, qkv[i], lse[i], datt, length))
        part = part + mm(dqkv[i], w_self[i][:, : 3 * width], NT)
    da0 = core_sum(part)
    back, gain0 = normalize_back(x, gain[0], da0)
    dx = (g1 + back).astype(BF16)

    ffn_in = jnp.where(is_enc, a1, a2)
    ffn_g = jnp.where(is_enc, e_g_low, gy_low)

    def side_grad(i):
        first = mm(jnp.where(is_enc, memory, a1), jnp.where(is_enc, dkv[i][:, :width], dcq[i]), TN)
        second = mm(
            jnp.where(is_enc, memory, g2_low), jnp.where(is_enc, dkv[i][:, width:], catt[i]), TN
        )
        return jnp.concatenate([first, second], 1).astype(BF16)

    def down_grad(i):
        return mm(ffn_g, jnp.where(is_enc, e_hidden[i], d_hidden[i]), TN).astype(BF16)

    def gate_grad(i):
        return mm(ffn_in, jnp.where(is_enc, de_gate[i], dd_gate[i]), TN).astype(BF16)

    def up_grad(i):
        return mm(ffn_in, jnp.where(is_enc, de_up[i], dd_up[i]), TN).astype(BF16)

    def self_grad(i):
        return jnp.concatenate(
            [mm(a0, dqkv[i], TN), mm(g1_low, att[i], TN)], 1
        ).astype(BF16)

    def whole(grad_of):
        mine = grad_of(0)
        if groups == 2:
            mine = (mine.astype(F32) + over_groups(grad_of(1)).astype(F32)).astype(BF16)
        return plane_sum(mine)

    def plane_sum(value):
        if planes == 1:
            return value
        half = planes // 2
        for step in range(half - 1):
            inward = [(step, step + 1), (planes - 1 - step, planes - 2 - step)]
            got = lax.ppermute(value, "dp", inward)
            value = (value.astype(F32) + got.astype(F32)).astype(BF16)
        got = lax.ppermute(value, "dp", [(half - 1, half), (half, half - 1)])
        value = (value.astype(F32) + got.astype(F32)).astype(BF16)
        for step in range(half - 1):
            left, right = half - 1 - step, half + step
            got = lax.ppermute(value, "dp", [(left, left - 1), (right, right + 1)])
            value = jnp.where((plane == left - 1) | (plane == right + 1), got, value)
        return value

    t_side = whole(side_grad)
    t_down = whole(down_grad)
    t_gate = whole(gate_grad)
    t_up = whole(up_grad)
    t_self = whole(self_grad)
    attn_grad = jnp.stack(
        [t_self[:, i * width : (i + 1) * width] for i in range(4)]
        + [t_side[:, :width], t_side[:, width:]]
    ).astype(F32)
    ffn_grad = jnp.stack([t_gate, t_up, t_down]).astype(F32)

    gain_parts = jnp.stack([gain0, gain1, jnp.where(is_enc, e_gain2, d_gain2)])
    gain_total = lax.psum(jnp.where(core == 0, gain_parts, 0.0), ("dp", "tensor"))
    out = jnp.where(is_enc, memory, (dec_y * live).astype(BF16))
    return (
        from_rows(out)[None],
        from_rows(dx)[None],
        gain_total[None],
        attn_grad[None],
        ffn_grad[None],
    )


def solution(mesh):
    in_specs = (
        P("section", "dp", "tensor", None),
        P("dp"),
        P("dp", "tensor", None),
        P("section", None, None),
        P("section", None, None, "tensor"),
        P("section", None, None, "tensor"),
    )
    out_specs = (
        P("section", "dp", "tensor", None),
        P("section", "dp", "tensor", None),
        P("section", None, None),
        P("section", None, None, "tensor"),
        P("section", None, None, "tensor"),
    )
    return jax.shard_map(
        on_device, mesh=mesh, in_specs=in_specs, out_specs=out_specs, check_vma=False
    )
```

```python
import functools

import jax
import jax.numpy as jnp
from jax import lax
from jax.experimental import pallas as pl
from jax.experimental.pallas import tpu as pltpu
from jax.sharding import PartitionSpec as P

DH = 64
EPSILON = 1e-06
NEGATIVE = -1e30
F32 = jnp.float32
BF16 = jnp.bfloat16
VMEM = 56 * 1024 * 1024
NN = (((1,), (0,)), ((), ()))
NT = (((1,), (1,)), ((), ()))
TN = (((0,), (0,)), ((), ()))


def mm(left, right, dims=NN):
    return lax.dot_general(left, right, dims, preferred_element_type=F32)


def factor_of(v):
    return lax.rsqrt(jnp.mean(v * v, axis=-1, keepdims=True) + EPSILON)


def normed(v, gain):
    return (v * factor_of(v) * gain).astype(BF16)


def normed_back(v, gain, u):
    factor = factor_of(v)
    scaled = u * gain
    grad_gain = jnp.sum(u * v * factor, axis=0, keepdims=True)
    inner = jnp.mean(scaled * v, axis=-1, keepdims=True)
    return factor * scaled - v * (factor * factor * factor * inner), grad_gain


def gelu_parts(v):
    c = 0.7978845608028654
    square = v * v
    t = jnp.tanh(v * (c + (c * 0.044715) * square))
    half = 0.5 + 0.5 * t
    slope = half + v * (half * (1.0 - t)) * (c + (3.0 * c * 0.044715) * square)
    return v * half, slope


def causal_mask(enc, length):
    key_pos = lax.broadcasted_iota(jnp.int32, (length, length), 0)
    query_pos = lax.broadcasted_iota(jnp.int32, (length, length), 1)
    return key_pos <= query_pos + enc * length


def scores(q, k, allowed):
    s = mm(k, q, NT)
    return s if allowed is None else jnp.where(allowed, s, NEGATIVE)


def attend(q_ref, q0, kv_ref, k0, v0, out_ref, lse_ref, allowed, width):
    for h in range(width // DH):
        lo = h * DH
        q = q_ref[:, q0 + lo : q0 + lo + DH] * BF16(DH**-0.5)
        k = kv_ref[:, k0 + lo : k0 + lo + DH]
        v = kv_ref[:, v0 + lo : v0 + lo + DH]
        s = scores(q, k, allowed)
        top = jnp.max(s, axis=0, keepdims=True)
        e = jnp.exp(s - top)
        total = jnp.sum(e, axis=0, keepdims=True)
        o = mm(v.T, e.astype(BF16)) * (1.0 / total)
        out_ref[:, lo : lo + DH] = o.T.astype(BF16)
        lse_ref[h : h + 1, :] = top + jnp.log(total)


def attend_back(q_ref, q0, kv_ref, k0, v0, lse_ref, grad, dq_ref, dkv_ref, allowed, width):
    for h in range(width // DH):
        lo = h * DH
        q = q_ref[:, q0 + lo : q0 + lo + DH] * BF16(DH**-0.5)
        k = kv_ref[:, k0 + lo : k0 + lo + DH]
        v = kv_ref[:, v0 + lo : v0 + lo + DH]
        g = grad[:, lo : lo + DH]
        p = jnp.exp(scores(q, k, allowed) - lse_ref[h : h + 1, :])
        dp = mm(v, g, NT)
        delta = jnp.sum(p * dp, axis=0, keepdims=True)
        ds = (p * (dp - delta)).astype(BF16)
        dkv_ref[:, v0 + lo : v0 + lo + DH] = mm(p.astype(BF16), g).astype(BF16)
        dkv_ref[:, k0 + lo : k0 + lo + DH] = mm(ds, q).astype(BF16)
        dq = mm(k.T, ds) * (DH**-0.5)
        dq_ref[:, q0 + lo : q0 + lo + DH] = dq.T.astype(BF16)


def ffn_back(a, g, weights, dgate_refs, dup_refs):
    part = None
    for (wg, wu, wd), dgate_ref, dup_ref in zip(weights, dgate_refs, dup_refs):
        value, slope = gelu_parts(mm(a, wg[...]))
        up = mm(a, wu[...])
        dh = mm(g, wd[...])
        dgate_ref[...] = (dh * up * slope).astype(BF16)
        dup_ref[...] = (dh * value).astype(BF16)
        here = mm(dgate_ref[...], wg[...], NT) + mm(dup_ref[...], wu[...], NT)
        part = here if part is None else part + here
    return part


def ffn_both(a, g, weights, hid_refs, dgate_refs, dup_refs):
    part = None
    for (wg, wu, wd), hid_ref, dgate_ref, dup_ref in zip(weights, hid_refs, dgate_refs, dup_refs):
        gate = mm(a, wg[...])
        up = mm(a, wu[...])
        dh = mm(g, wd[...])
        value, slope = gelu_parts(gate)
        hid_ref[...] = (value * up).astype(BF16)
        dgate_ref[...] = (dh * up * slope).astype(BF16)
        dup_ref[...] = (dh * value).astype(BF16)
        here = mm(dgate_ref[...], wg[...], NT) + mm(dup_ref[...], wu[...], NT)
        part = here if part is None else part + here
    return part


def after(value, *others):
    return lax.optimization_barrier((value,) + others)[0]


class Order:
    def __init__(self):
        self.tokens = []

    def place(self, value):
        return after(value, *self.tokens) if self.tokens else value

    def done(self, value):
        self.tokens = [value]

    def need(self, *values):
        self.tokens = self.tokens + list(values)


TIMES = {
    "first_norm": 2.6,
    "self_forward": 5.7,
    "ffn_first": 5.3,
    "ffn_second": 4.9,
    "memory": 3.7,
    "cross_forward": 8.2,
    "dec_ffn": 9.5,
    "cross_back": 12.3,
    "side_grads": 3.4,
    "dec_down": 3.7,
    "output": 3.4,
    "memory_back": 4.6,
    "down_grads": 3.2,
    "enc_ffn_back": 9.6,
    "pair_grads": 5.0,
    "self_back": 12.3,
    "input_back": 3.8,
    "self_grads": 3.4,
    "ffn_out": 4.0,
}
SCALE = 0.0001


def estimate(name):
    flops = int(SCALE * TIMES[name] * 1.1e9)
    return pl.CostEstimate(flops=flops, bytes_accessed=1, transcendentals=0)


class Call:
    def __init__(self, rows, length, order):
        self.rows, self.length, self.order = rows, length, order
        self.specs, self.args, self.out_specs, self.out_shapes = [], [], [], []

    def scalar(self, value):
        self.specs.append(pl.BlockSpec(memory_space=pltpu.SMEM))
        self.args.append(value)

    def tokens(self, *values):
        for value in values:
            count = value.shape[0] // self.rows
            self.specs.append(pl.BlockSpec((count, value.shape[1]), lambda i: (i, 0)))
            self.args.append(value)

    def heads(self, *values):
        for value in values:
            self.specs.append(pl.BlockSpec((None,) + value.shape[1:], lambda i: (i, 0, 0)))
            self.args.append(value)

    def whole(self, *values):
        for value in values:
            block = None
            if isinstance(value, tuple):
                value, block, at = value
            if block is None:
                block, at = value.shape, (0,) * value.ndim
            self.specs.append(pl.BlockSpec(block, lambda i, at=at: at))
            self.args.append(value)

    def out_tokens(self, width, kind, count=None):
        count = self.length if count is None else count
        self.out_specs.append(pl.BlockSpec((count, width), lambda i: (i, 0)))
        self.out_shapes.append(jax.ShapeDtypeStruct((self.rows * count, width), kind))

    def out_heads(self, heads):
        self.out_specs.append(pl.BlockSpec((None, heads, self.length), lambda i: (i, 0, 0)))
        self.out_shapes.append(jax.ShapeDtypeStruct((self.rows, heads, self.length), F32))

    def out_whole(self, shape, kind):
        self.out_specs.append(pl.BlockSpec(shape, lambda i, n=len(shape): (0,) * n))
        self.out_shapes.append(jax.ShapeDtypeStruct(shape, kind))

    def run(self, kernel, name):
        first = next(k for k, v in enumerate(self.args) if v.dtype != jnp.int32)
        self.args[first] = self.order.place(self.args[first])
        out = pl.pallas_call(
            kernel,
            grid=(self.rows,),
            in_specs=self.specs,
            out_specs=self.out_specs,
            out_shape=self.out_shapes,
            compiler_params=pltpu.CompilerParams(vmem_limit_bytes=VMEM),
            cost_estimate=estimate(name),
            name=name,
        )(*self.args)
        self.order.done(out[0])
        return out


SMEM_SPEC = pl.BlockSpec(memory_space=pltpu.SMEM)


def accumulate(ref, value):
    first = pl.program_id(0) == 0

    @pl.when(first)
    def _():
        ref[...] = value

    @pl.when(jnp.logical_not(first))
    def _():
        ref[...] += value


def on_device(layer_input, dec_lengths, out_cotangent, gains, attn_weights, ffn_weights):
    tensor = lax.axis_size("tensor")
    planes = lax.axis_size("dp")
    batch, part_len, model = layer_input.shape[1:]
    groups = 2 if tensor % 2 == 0 and batch % 2 == 0 else 1
    cores = tensor // groups
    rows = batch // groups
    length = part_len * tensor
    tokens = rows * length
    share = length // cores
    width = attn_weights.shape[3]
    hidden_width = ffn_weights.shape[3]
    heads = width // DH
    shares = range(groups)

    section = lax.axis_index("section")
    plane = lax.axis_index("dp")
    lane = lax.axis_index("tensor")
    group = lane // cores
    core = lane % cores
    is_enc = section == 0
    outer = (plane == 0) | (plane == planes - 1)
    place = jnp.stack([v.astype(jnp.int32) for v in (is_enc, core, outer, plane % 2, group)])
    group_route = [(t, (t + cores) % tensor) for t in range(tensor)]
    core_groups = [[g * cores + c for c in range(cores)] for g in range(groups)]
    next_plane = [(p, p ^ 1) for p in range(planes)]
    order = Order()

    def over_groups(value):
        return lax.ppermute(value, "tensor", group_route)

    def decoder_only(value, axis, route):
        size = lax.axis_size(axis)
        return lax.ppermute(value, ("section", axis), [(size + a, size + b) for a, b in route])

    def encoder_only(value, axis, route):
        return lax.ppermute(value, ("section", axis), route)

    def core_route(step):
        return [
            (g * cores + (c + step) % cores, g * cores + c)
            for g in range(groups)
            for c in range(cores)
        ]

    def core_swap(value):
        return [lax.ppermute(value, "tensor", core_route(k)) for k in range(1, cores)]

    def core_sum(part):
        if cores <= 2:
            return [part] + core_swap(part)
        return [lax.psum(part, "tensor", axis_index_groups=core_groups)]

    def pick(value, index, count):
        return lax.dynamic_slice_in_dim(value, index * count, count, 0)

    def move(value, axis, route, decoder):
        return decoder_only(value, axis, route) if decoder else lax.ppermute(value, axis, route)

    class Fetch:
        def __init__(self, own, at, count, *behind):
            self.halved = planes % 2 == 0 and count % 32 == 0
            if self.halved:
                count //= 2
                at = at + (plane % 2) * count
            value = lax.dynamic_slice_in_dim(own, at, count, 0)
            if behind:
                value = after(value, *behind)
            self.direct = over_groups(value)

        def forward(self, placed=True):
            if self.halved:
                if placed:
                    self.direct = order.place(self.direct)
                    order.need(self.direct)
                self.passed = lax.ppermute(self.direct, "dp", next_plane)

        def arrived(self):
            return self.passed if self.halved else self.direct

        def parts(self):
            return [self.direct, self.passed] if self.halved else [self.direct]

    def assemble(place_ref, refs, out_ref, halved):
        if len(refs) == 1:
            out_ref[...] = refs[0][...]
            return
        half = refs[0].shape[0]
        first = place_ref[3] * half if halved else 0
        second = half - first
        out_ref[pl.ds(pl.multiple_of(first, half), half), :] = refs[0][...]
        out_ref[pl.ds(pl.multiple_of(second, half), half), :] = refs[1][...]

    def to_rows(value, route_group):
        if groups == 1:
            blocks = value[:, None]
        else:
            mine = pick(value, group, rows)
            got = route_group(pick(value, 1 - group, rows))
            first = group == 0
            blocks = jnp.stack([jnp.where(first, mine, got), jnp.where(first, got, mine)], 1)
        if cores == 2:
            got = core_swap(blocks)[0]
            low = core == 0
            blocks = jnp.stack([jnp.where(low, blocks, got), jnp.where(low, got, blocks)], 2)
        elif cores > 2:
            blocks = lax.all_gather(blocks, "tensor", axis=2, axis_index_groups=core_groups)
        return blocks.reshape(tokens, model)

    def from_rows(value):
        blocks = value.reshape(rows, tensor, part_len, model)
        mine = lax.dynamic_index_in_dim(blocks, lane, 1, keepdims=False)
        if groups == 1:
            return mine
        got = over_groups(
            lax.dynamic_index_in_dim(blocks, (lane + cores) % tensor, 1, keepdims=False)
        )
        first = group == 0
        return jnp.concatenate([jnp.where(first, mine, got), jnp.where(first, got, mine)], 0)

    def split(refs, *counts):
        at, out = 0, []
        for count in counts:
            out.append(refs[at : at + count])
            at += count
        return out

    def call():
        return Call(rows, length, order)

    attn_t = attn_weights[0].transpose(0, 2, 1).reshape(6 * width, model)
    ffn = ffn_weights[0]
    gain = gains[0]

    own_self = (attn_t, (4 * width, model), (0, 0))
    own_side = (attn_t, (2 * width, model), (2, 0))
    own_ffn = [(ffn, (None, model, hidden_width), (j, 0, 0)) for j in range(3)]
    w_self, w_ffn, w_dec, w_side = [own_self], [own_ffn], [own_ffn], [own_side]
    x_parts = [pick(layer_input[0], group, rows)]
    if groups == 2:
        x_parts.append(over_groups(pick(layer_input[0], 1 - group, rows)))
        flat = ffn.reshape(3 * model, hidden_width)
        far_self = Fetch(attn_t, 0, 4 * width)
        far_pair = [Fetch(flat, k * model, model, x_parts[1]) for k in range(2)]
        half = model // 2
        far_down = [
            encoder_only(ffn[2, k * half : k * half + half], "tensor", group_route)
            for k in range(2)
        ]
    enc_side = lax.ppermute(attn_t[4 * width :], "section", [(0, 1)])
    x_parts = x_parts + [v for part in zip(*[core_swap(v) for v in x_parts]) for v in part]

    c = call()
    c.scalar(place)
    c.heads(*x_parts)
    c.whole(gain[0:1])
    c.out_tokens(model, BF16)
    c.out_tokens(model, BF16)

    def first_norm(place_ref, *refs):
        gain_ref, x_ref, a_ref = refs[-3:]
        for k, ref in enumerate(refs[:-3]):
            from_core = lax.rem(place_ref[1] + k // groups, cores)
            from_group = lax.rem(place_ref[4] + k % groups, groups)
            at = (from_group * cores + from_core) * part_len
            x_ref[pl.ds(pl.multiple_of(at, part_len), part_len), :] = ref[...]
        a_ref[...] = normed(x_ref[...].astype(F32), gain_ref[...])

    if groups == 2:
        far_self.forward(False)
        order.need(far_self.direct)
    x, a0 = c.run(first_norm, "first_norm")

    def self_forward(i, part):
        pieces = far_self.parts() if i == 1 else [w_self[i]]
        c = call()
        c.scalar(place)
        c.tokens(a0)
        c.whole(*pieces)
        if part is not None:
            c.tokens(part)
        c.out_tokens(3 * width, BF16)
        c.out_tokens(width, BF16)
        c.out_heads(heads)
        c.out_tokens(model, BF16 if i == groups - 1 else F32)
        if i == 1:
            c.out_whole((4 * width, model), BF16)

        def kernel(place_ref, a_ref, *refs):
            qkv_ref, att_ref, lse_ref, part_ref = refs[-5:-1] if i == 1 else refs[-4:]
            w_ref = refs[0]
            if i == 1:
                w_ref = refs[-1]
                assemble(place_ref, refs[: len(pieces)], w_ref, far_self.halved)
            qkv_ref[...] = mm(a_ref[...], w_ref[: 3 * width, :], NT).astype(BF16)
            allowed = causal_mask(place_ref[0], length)
            attend(
                qkv_ref, 0, qkv_ref, width, 2 * width, att_ref, lse_ref, allowed, width
            )
            out = mm(att_ref[...], w_ref[3 * width :, :])
            if part is not None:
                out = out + refs[len(pieces)][...]
            part_ref[...] = out.astype(part_ref.dtype)

        return c.run(kernel, "self_forward")

    qkv, att, lse, part = [], [], [], None
    for i in shares:
        if i == 1:
            order.need(enc_side)
            far_pair[0].forward()
            far_pair[1].forward()
        a, b, l, part, *rest = self_forward(i, part)
        w_self += rest
        qkv.append(a)
        att.append(b)
        lse.append(l)
    if groups == 2:
        part = after(part, far_down[0], far_pair[0].arrived())
    parts = core_sum(part)

    def total_of(refs):
        value = refs[0][...].astype(F32)
        for ref in refs[1:]:
            value = value + ref[...].astype(F32)
        return value

    def ffn_share(a, wg, wu, wd, hid_ref):
        value, _ = gelu_parts(mm(a, wg[...]))
        hid_ref[...] = (value * mm(a, wu[...])).astype(BF16)
        return mm(hid_ref[...], wd[...], NT)

    c = call()
    c.tokens(x, *parts)
    c.whole(gain[1:2], *w_ffn[0])
    c.out_tokens(model, F32)
    c.out_tokens(model, BF16)
    c.out_tokens(hidden_width, BF16)
    c.out_tokens(model, BF16 if groups == 1 else F32)

    def ffn_first(x_ref, *refs):
        count = len(parts)
        gain_ref, wg, wu, wd, x1_ref, a1_ref, hid_ref, part_ref = refs[count:]
        x1 = x_ref[...].astype(F32) + total_of(refs[:count])
        x1_ref[...] = x1
        a1_ref[...] = normed(x1, gain_ref[...])
        part_ref[...] = ffn_share(a1_ref[...], wg, wu, wd, hid_ref).astype(part_ref.dtype)

    x1, a1, hid, part = c.run(ffn_first, "ffn_first")
    e_hid = [hid]
    if groups == 2:
        both_sides = decoder_only(
            jnp.concatenate([attn_t[4 * width :], enc_side], 0), "tensor", group_route
        )
        pieces = [fetch.parts() for fetch in far_pair]
        c = call()
        c.scalar(place)
        c.tokens(a1, part)
        c.whole(*[v for got in pieces for v in got], *far_down)
        c.out_tokens(model, BF16)
        c.out_tokens(hidden_width, BF16)
        c.out_whole((2 * model, hidden_width), BF16)
        c.out_whole((model, hidden_width), BF16)

        def ffn_second(place_ref, a_ref, prev_ref, *refs):
            *piece_refs, down_refs, (part_ref, hid_ref, pair_ref, wd) = split(
                refs, *[len(got) for got in pieces], 2, 4
            )
            for k in range(2):
                w = pair_ref.at[k * model : (k + 1) * model]
                assemble(place_ref, piece_refs[k], w, far_pair[k].halved)
            for k, ref in enumerate(down_refs):
                wd[k * half : (k + 1) * half, :] = ref[...]
            ws = pair_ref.at[:model], pair_ref.at[model:], wd
            part_ref[...] = (prev_ref[...] + ffn_share(a_ref[...], *ws, hid_ref)).astype(BF16)

        part, hid, pair, far_down = c.run(ffn_second, "ffn_second")
        far = [(pair, (model, hidden_width), (k, 0)) for k in range(2)]
        w_dec = [own_ffn, far + [decoder_only(ffn[2], "tensor", group_route)]]
        w_ffn.append(far + [far_down])
        e_hid.append(hid)
        part = after(part, both_sides)
    parts = core_sum(part)

    c = call()
    c.scalar(place)
    c.tokens(x1, *parts)
    c.whole(gain[2:3])
    c.out_tokens(model, F32)
    c.out_tokens(model, BF16)
    c.out_tokens(model, BF16, share)

    def memory_kernel(place_ref, x1_ref, *refs):
        gain_ref, y_ref, memory_ref, mine_ref = refs[-4:]
        y = x1_ref[...] + total_of(refs[:-4])
        y_ref[...] = y
        memory_ref[...] = normed(y, gain_ref[...])
        start = pl.multiple_of(place_ref[1] * share, share)
        mine_ref[...] = memory_ref[pl.ds(start, share), :]

    if groups == 2:
        both_sides = [(both_sides, (2 * width, model), (k, 0)) for k in range(2)]
    y, memory, mem_mine = c.run(memory_kernel, "memory")
    mem_mine = lax.ppermute(mem_mine, "section", [(0, 1)])
    mem = [mem_mine] + core_swap(mem_mine)

    cot = to_rows(order.place(out_cotangent), lambda v: decoder_only(v, "tensor", group_route))
    row_ids = group * rows + jnp.arange(rows)
    live = jnp.arange(length)[None, :] < dec_lengths[row_ids][:, None]
    live = live.reshape(tokens, 1)
    gy = order.place(jnp.where(live, cot, BF16(0)))
    order.done(gy)
    w_side, w_enc = [own_side], [enc_side]
    if groups == 2:
        w_side.append(both_sides[0])
        w_enc.append(both_sides[1])
    c = call()
    c.scalar(place)
    c.tokens(a1, *mem)
    c.whole(*w_side, *w_enc)
    for i in shares:
        c.out_tokens(width, BF16)
    for i in shares:
        c.out_tokens(2 * width, BF16)
    for i in shares:
        c.out_tokens(width, BF16)
    for i in shares:
        c.out_heads(heads)
    c.out_tokens(model, BF16)

    def cross_forward(place_ref, a_ref, *refs):
        mem_refs, side, enc, cq, kv, catt, clse, (part_ref,) = split(
            refs, cores, groups, groups, groups, groups, groups, groups, 1
        )
        out = None
        for i in shares:
            cq[i][...] = mm(a_ref[...], side[i][:width, :], NT).astype(BF16)
            for j, ref in enumerate(mem_refs):
                kv[i][j * share : (j + 1) * share, :] = mm(ref[...], enc[i][...], NT).astype(BF16)
            attend(cq[i], 0, kv[i], 0, width, catt[i], clse[i], None, width)
            here = mm(catt[i][...], side[i][width:, :])
            out = here if out is None else out + here
        part_ref[...] = out.astype(BF16)

    cq, kv, catt, clse, (part,) = split(
        c.run(cross_forward, "cross_forward"), groups, groups, groups, groups, 1
    )
    parts = core_sum(part)

    c = call()
    c.tokens(x1, gy, *parts)
    c.whole(gain[2:3], *[w for ws in w_dec for w in ws])
    c.out_tokens(model, F32)
    c.out_tokens(model, BF16)
    for _ in range(3 * groups):
        c.out_tokens(hidden_width, BF16)
    c.out_tokens(model, BF16)

    def triples(refs):
        return [refs[3 * i : 3 * i + 3] for i in shares]

    def dec_ffn(x1_ref, gy_ref, *refs):
        part_refs, (gain_ref,), ws, (x2_ref, a2_ref), hid, dgate, dup, (part_ref,) = split(
            refs, len(parts), 1, 3 * groups, 2, groups, groups, groups, 1
        )
        x2 = x1_ref[...] + total_of(part_refs)
        x2_ref[...] = x2
        a2_ref[...] = normed(x2, gain_ref[...])
        part_ref[...] = ffn_both(
            a2_ref[...], gy_ref[...], triples(ws), hid, dgate, dup
        ).astype(BF16)

    (x2, a2), d_hid, d_gate, d_up, (part,) = split(
        c.run(dec_ffn, "dec_ffn"), 2, groups, groups, groups, 1
    )
    parts = core_sum(part)

    c = call()
    c.tokens(x2, gy, *parts, *cq, *kv)
    c.heads(*clse)
    c.whole(gain[2:3], *w_side, *w_enc)
    c.out_tokens(model, F32)
    c.out_tokens(model, BF16)
    c.out_whole((1, model), F32)
    for i in shares:
        c.out_tokens(width, BF16)
    c.out_tokens(2 * width * groups, BF16)
    c.out_tokens(model, BF16)
    for j in range(cores):
        c.out_tokens(model, F32 if j == 0 else BF16, share)

    def cross_back(x2_ref, gy_ref, *refs):
        (
            part_refs, cq_refs, kv_refs, lse_refs, (gain_ref,), side, enc,
            (g2_ref, low_ref, gain2_ref), dcq_refs, (dkv_ref, part_ref), mem_refs,
        ) = split(
            refs, len(parts), groups, groups, groups, 1, groups, groups, 3, groups, 2, cores
        )
        dkv_refs = [dkv_ref.at[:, 2 * width * i : 2 * width * (i + 1)] for i in shares]
        back, grad_gain = normed_back(x2_ref[...], gain_ref[...], total_of(part_refs))
        accumulate(gain2_ref, grad_gain)
        g2 = gy_ref[...].astype(F32) + back
        g2_ref[...] = g2
        low_ref[...] = g2.astype(BF16)
        out = None
        for i in shares:
            grad = mm(low_ref[...], side[i][width:, :], NT).astype(BF16)
            attend_back(
                cq_refs[i], 0, kv_refs[i], 0, width, lse_refs[i], grad,
                dcq_refs[i], dkv_refs[i], None, width,
            )
            here = mm(dcq_refs[i][...], side[i][:width, :])
            out = here if out is None else out + here
        part_ref[...] = out.astype(BF16)
        for j, ref in enumerate(mem_refs):
            total = None
            for i in shares:
                here = mm(dkv_refs[i][j * share : (j + 1) * share, :], enc[i][...])
                total = here if total is None else total + here
            ref[...] = total.astype(ref.dtype)

    (g2, g2_low, dec_gain2), dcq, (dkv, part_dec), dmem = split(
        c.run(cross_back, "cross_back"), 3, groups, 2, cores
    )
    mine = dmem[0]
    for step in range(1, cores):
        mine = mine + lax.ppermute(dmem[step], "tensor", core_route(cores - step)).astype(F32)
    mine = mine.astype(BF16)
    order.done(mine)
    mine = lax.ppermute(mine, "section", [(1, 0)])
    dmem = [mine] + core_swap(mine)
    dkv = lax.ppermute(dkv, "section", [(1, 0)])

    def products(terms, tails, counts, name):
        sizes = [[len(values) for values in term] for term in terms]
        flat = [v for term in terms for values in term for v in values] + tails
        flat[0] = order.place(flat[0])

        def product(left_refs, right_refs):
            total = None
            for j, right in enumerate(right_refs):
                spans = [(left_refs[j][...], right[...])]
                for left, value in spans:
                    here = mm(left, value, TN)
                    total = here if total is None else total + here
            return total

        def kernel(place_ref, *refs):
            outs = refs[len(flat) :]
            starts = [sum(counts[:k]) for k in range(len(counts))]

            def store(value, at):
                done = 0
                while done < value.shape[0]:
                    k = max(q for q in range(len(counts)) if starts[q] <= at + done)
                    inside = at + done - starts[k]
                    count = min(value.shape[0] - done, counts[k] - inside)
                    outs[k][inside : inside + count, :] = value[done : done + count].astype(BF16)
                    done += count

            used, at = 0, 0
            for size in sizes:
                values = split(refs[used:], *size)
                used += sum(size)
                if len(size) == 2:
                    store(product(*values), at)
                else:

                    @pl.when(place_ref[0] == 1)
                    def _(values=values, at=at):
                        store(product(*values[:2]), at)

                    @pl.when(place_ref[0] == 0)
                    def _(values=values, at=at):
                        store(product(*values[2:]), at)

                at += values[0][0].shape[1]
            for tail in refs[used : len(flat)]:
                store(tail[...], at)
                at += tail.shape[0]

        out = pl.pallas_call(
            kernel,
            in_specs=[SMEM_SPEC] + [pl.BlockSpec(memory_space=pltpu.VMEM)] * len(flat),
            out_shape=[jax.ShapeDtypeStruct((count, model), BF16) for count in counts],
            compiler_params=pltpu.CompilerParams(vmem_limit_bytes=VMEM),
            cost_estimate=estimate(name),
            name=name,
        )(place, *flat)
        order.done(out[-1])
        return list(out)

    class Sum:
        def __init__(self, own, far):
            self.value, self.got, self.at = own, far, 0
            half = planes // 2
            self.moves = [("group", group_route)] if groups == 2 else []
            if planes % 2 == 0:
                for k in range(half - 1):
                    self.moves.append(("add", [(k, k + 1), (planes - 1 - k, planes - 2 - k)]))
                self.moves.append(("add", [(half - 1, half), (half, half - 1)]))
                for k in range(half - 1):
                    left, right = half - 1 - k, half + k
                    self.moves.append(("take", [(left, left - 1), (right, right + 1)]))

        def step(self):
            if self.at == len(self.moves):
                return
            kind, route = self.moves[self.at]
            if self.got is None:
                self.got = lax.ppermute(self.value, "dp", route)
            last = self.at == len(self.moves) - 1
            if last and kind == "take":
                got = self.got
                order.need(got)
            else:
                got = order.place(self.got)
            if kind == "take":
                targets = [b for _, b in route]
                self.value = jnp.where((plane == targets[0]) | (plane == targets[1]), got, self.value)
            else:
                self.value = (self.value.astype(F32) + got.astype(F32)).astype(BF16)
            if not (last and kind == "take"):
                order.done(self.value)
            self.at += 1
            if not last:
                self.got = lax.ppermute(self.value, "dp", self.moves[self.at][1])

        def finish(self):
            while self.at < len(self.moves):
                self.step()
            if planes % 2 and planes > 1:
                self.value = lax.psum(self.value, "dp")
            return self.value

    def send_other(values):
        return [over_groups(v) for v in values] if groups == 2 else [None] * len(values)

    def side_grads(i):
        args = [order.place(memory), dkv, dcq[i], a1, catt[i], g2_low]

        def kernel(place_ref, memory_ref, dkv_ref, dcq_ref, a1_ref, catt_ref, g2_ref, out_ref):
            @pl.when(place_ref[0] == 1)
            def _():
                total = None
                for row in range(rows):
                    for j in range(cores):
                        at = row * length + lax.rem(place_ref[1] + j, cores) * share
                        right = memory_ref[pl.ds(pl.multiple_of(at, share), share), :]
                        start = row * length + j * share
                        left = dkv_ref[start : start + share, 2 * width * i : 2 * width * (i + 1)]
                        here = mm(left, right, TN)
                        total = here if total is None else total + here
                out_ref[...] = total.astype(BF16)

            @pl.when(place_ref[0] == 0)
            def _():
                out_ref[:width, :] = mm(dcq_ref[...], a1_ref[...], TN).astype(BF16)
                out_ref[width:, :] = mm(catt_ref[...], g2_ref[...], TN).astype(BF16)

        out = pl.pallas_call(
            kernel,
            in_specs=[SMEM_SPEC] + [pl.BlockSpec(memory_space=pltpu.VMEM)] * len(args),
            out_shape=jax.ShapeDtypeStruct((2 * width, model), BF16),
            compiler_params=pltpu.CompilerParams(vmem_limit_bytes=VMEM),
            cost_estimate=estimate("side_grads"),
            name="side_grads",
        )(place, *args)
        order.done(out)
        return out

    def decoder_down():
        c = call()
        c.tokens(*d_hid)
        c.whole(*[ws[2] for ws in w_dec])
        c.out_tokens(model, BF16)

        def dec_down(*refs):
            hid_refs, ws, (out_ref,) = split(refs, groups, groups, 1)
            total = None
            for hid_ref, w in zip(hid_refs, ws):
                here = mm(hid_ref[...], w[...], NT)
                total = here if total is None else total + here
            out_ref[...] = total.astype(BF16)

        return core_sum(c.run(dec_down, "dec_down")[0])

    def decoder_output(last):
        c = call()
        c.scalar(place)
        c.tokens(memory, live.astype(F32), x2, *last)
        c.out_tokens(model, BF16)

        def output(place_ref, memory_ref, live_ref, x2_ref, *refs):
            total = (x2_ref[...] + total_of(refs[:-1])) * live_ref[...]
            refs[-1][...] = jnp.where(place_ref[0] == 1, memory_ref[...], total.astype(BF16))

        return c.run(output, "output")[0]

    c = call()
    c.scalar(place)
    c.tokens(y, *dmem, gy, g2)
    c.whole(gain[2:3], dec_gain2)
    c.out_tokens(model, BF16)
    c.out_tokens(model, F32)
    c.out_whole((1, model), F32)

    def memory_back(place_ref, y_ref, *refs):
        dmem_refs, (gy_ref, g2_ref, gain_ref, old_gain, low_ref, g_ref, new_gain) = split(
            refs, cores, 7
        )

        @pl.when(place_ref[0] == 1)
        def _():
            for j, ref in enumerate(dmem_refs):
                at = lax.rem(place_ref[1] + j, cores)
                g_ref[pl.ds(pl.multiple_of(at * share, share), share), :] = ref[...].astype(F32)
            e_g, grad_gain = normed_back(y_ref[...], gain_ref[...], g_ref[...])
            accumulate(new_gain, grad_gain)
            g_ref[...] = e_g
            low_ref[...] = e_g.astype(BF16)

        @pl.when(place_ref[0] == 0)
        def _():
            low_ref[...] = gy_ref[...]
            g_ref[...] = g2_ref[...]
            new_gain[...] = old_gain[...]

    ffn_g, g_in, gain2 = c.run(memory_back, "memory_back")

    def down_grads(i):
        terms = [([e_hid[i]], [ffn_g], [d_hid[i]], [ffn_g])]
        return products(terms, [], [hidden_width // 2] * 2, "down_grads")

    far_down_grads = send_other(down_grads(1)) if groups == 2 else [None] * 2
    down_sums = [Sum(own, far) for own, far in zip(down_grads(0), far_down_grads)]

    c = call()
    c.scalar(place)
    c.tokens(ffn_g, a1, part_dec)
    c.whole(*[w for ws in w_ffn for w in ws])
    c.out_tokens(model, BF16)
    for _ in range(2 * groups):
        c.out_tokens(hidden_width, BF16)

    def enc_ffn_back(place_ref, g_ref, a1_ref, old_part, *refs):
        ws, (part_ref,), dgate, dup = split(refs, 3 * groups, 1, groups, groups)

        @pl.when(place_ref[0] == 1)
        def _():
            part_ref[...] = ffn_back(
                a1_ref[...], g_ref[...], triples(ws), dgate, dup
            ).astype(BF16)

        @pl.when(place_ref[0] == 0)
        def _():
            part_ref[...] = old_part[...]

    (part,), e_gate, e_up = split(c.run(enc_ffn_back, "enc_ffn_back"), 1, groups, groups)
    parts = core_sum(part)

    def pair_grads(i):
        terms = [
            ([e_gate[i]], [a1], [d_gate[i]], [a2]),
            ([e_up[i]], [a1], [d_up[i]], [a2]),
        ]
        return products(terms, [], [hidden_width] * 2, "pair_grads")

    def gate_up(i, which):
        return products([(
            [(e_gate, e_up)[which][i]], [a1], [(d_gate, d_up)[which][i]], [a2],
        )], [], [hidden_width], "pair_grads")

    down_sums[0].step()
    far_gate = send_other(gate_up(1, 0) if groups == 2 else [None])[0]
    gate_sum = Sum(gate_up(0, 0)[0], far_gate)
    down_sums[1].step()
    far_up = send_other(gate_up(1, 1) if groups == 2 else [None])[0]
    down_sums[0].step()

    c = call()
    c.scalar(place)
    c.tokens(x1, g_in, *parts, *qkv)
    c.heads(*lse)
    c.whole(gain[1:2], *w_self)
    c.out_tokens(model, F32)
    c.out_tokens(model, BF16)
    c.out_whole((1, model), F32)
    for i in shares:
        c.out_tokens(3 * width, BF16)
    c.out_tokens(model, BF16)

    def self_back(place_ref, x1_ref, g_ref, *refs):
        (
            part_refs, qkv_refs, lse_refs, (gain_ref,), ws, (g1_ref, low_ref, gain1_ref),
            dqkv_refs, (part_ref,),
        ) = split(refs, len(parts), groups, groups, 1, groups, 3, groups, 1)
        back, grad_gain = normed_back(x1_ref[...], gain_ref[...], total_of(part_refs))
        accumulate(gain1_ref, grad_gain)
        g1 = g_ref[...] + back
        g1_ref[...] = g1
        low_ref[...] = g1.astype(BF16)
        allowed = causal_mask(place_ref[0], length)
        out = None
        for i in shares:
            grad = mm(low_ref[...], ws[i][3 * width :, :], NT).astype(BF16)
            attend_back(
                qkv_refs[i], 0, qkv_refs[i], width, 2 * width, lse_refs[i], grad,
                dqkv_refs[i], dqkv_refs[i], allowed, width,
            )
            here = mm(dqkv_refs[i][...], ws[i][: 3 * width, :])
            out = here if out is None else out + here
        part_ref[...] = out.astype(BF16)

    (g1, g1_low, gain1), dqkv, (part,) = split(c.run(self_back, "self_back"), 3, groups, 1)
    parts = core_sum(part)
    down_sums[1].step()
    down_sums[0].step()
    gate_sum.step()
    up_sum = Sum(gate_up(0, 1)[0], far_up)
    down_sums[1].step()
    side_far = send_other([side_grads(1)] if groups == 2 else [None])[0]

    c = call()
    c.tokens(x, g1, *parts)
    c.whole(gain[0:1], gain1, gain2)
    c.out_tokens(model, BF16)
    c.out_whole((16, model), F32)

    def input_back(x_ref, g1_ref, *refs):
        gain_ref, gain1_ref, gain2_ref, dx_ref, rows_ref = refs[-5:]
        back, grad_gain = normed_back(
            x_ref[...].astype(F32), gain_ref[...], total_of(refs[:-5])
        )
        dx_ref[...] = (g1_ref[...] + back).astype(BF16)

        @pl.when(pl.program_id(0) == 0)
        def _():
            rows_ref[...] = jnp.zeros_like(rows_ref)
            rows_ref[1:2, :] = gain1_ref[...]
            rows_ref[2:3, :] = gain2_ref[...]

        rows_ref[0:1, :] += grad_gain

    dx, gain_rows = c.run(input_back, "input_back")

    def self_grads(i, counts):
        terms = [([dqkv[i]], [a0]), ([att[i]], [g1_low])]
        return products(terms, [gain_rows], counts, "self_grads")

    far_grads = [None] * 2
    if groups == 2:
        far = over_groups(self_grads(1, [4 * width + 16])[0])
        far_grads = [far[: 2 * width], far[2 * width :]]
    up_sum.step()
    side_sum = Sum(side_grads(0), side_far)
    gate_sum.step()
    first_sum, last_sum = [
        Sum(own, far) for own, far in zip(self_grads(0, [2 * width, 2 * width + 16]), far_grads)
    ]
    side_sum.step()
    down_sums[0].step()
    down_sums[1].step()
    up_sum.step()
    gate_sum.step()
    first_sum.step()
    last = decoder_down()
    side_sum.step()
    last_sum.step()
    up_sum.step()
    out = decoder_output(last)
    first_sum.step()
    gate_sum.step()
    side_sum.step()
    last_sum.step()
    up_sum.step()
    first_sum.step()
    side_sum.step()
    last_sum.step()
    ffn_sums = [gate_sum, up_sum, *down_sums]
    c = Call(1, length, order)
    for one in ffn_sums:
        c.whole(one.finish())
    c.out_whole((3, model, hidden_width), F32)

    def ffn_out(*refs):
        *ins, out_ref = refs
        for j in range(2):
            out_ref[j] = ins[j][...].astype(F32).T
        for k in range(2):
            half = hidden_width // 2
            out_ref[2, :, k * half : (k + 1) * half] = ins[2 + k][...].astype(F32).T

    ffn_grad = c.run(ffn_out, "ffn_out")[0]
    out, dx = order.place(out), order.place(dx)
    t_side, t_first, t_last = [one.finish() for one in (side_sum, first_sum, last_sum)]

    attn_grad = jnp.concatenate([t_first, t_last[: 2 * width], t_side], 0).astype(F32)
    attn_grad = attn_grad.reshape(6, width, model).transpose(0, 2, 1)
    gain_total = t_last[2 * width : 2 * width + 3].astype(F32)
    return (
        from_rows(out)[None],
        from_rows(dx)[None],
        gain_total[None],
        attn_grad[None],
        ffn_grad[None],
    )


def solution(mesh):
    in_specs = (
        P("section", "dp", "tensor", None),
        P("dp"),
        P("dp", "tensor", None),
        P("section", None, None),
        P("section", None, None, "tensor"),
        P("section", None, None, "tensor"),
    )
    out_specs = (
        P("section", "dp", "tensor", None),
        P("section", "dp", "tensor", None),
        P("section", None, None),
        P("section", None, None, "tensor"),
        P("section", None, None, "tensor"),
    )
    return jax.shard_map(
        on_device, mesh=mesh, in_specs=in_specs, out_specs=out_specs, check_vma=False
    )
```

```python
import functools

import jax
import jax.numpy as jnp
from jax import lax
from jax.experimental import pallas as pl
from jax.experimental.pallas import tpu as pltpu
from jax.sharding import PartitionSpec as P

DH = 64
EPSILON = 1e-06
NEGATIVE = -1e30
F32 = jnp.float32
BF16 = jnp.bfloat16
OPT = {'vmem': 16, 'c_sum': 0, 'c_tail': 0, 'c_mid': 0, 'c_start': 0, 'pair_after': 'in', 'u_after': 'in', 'd0_after': 'g', 'd1_after': 'g', 'pass_self': 'norm', 'pin_d0': 1, 'pin_zg': 1, 'pin_zu': 0, 'both': 'core2', 'dec_far': 'cross', 'cot': 0, 'attn_out': 1, 'lag': {'X': 2, 'A': 2, 'B': 2, 'R': 2}, 'y_after': 'none', 'self_after': 'none', 'self_direct': 0, 'both_after': 'none'}
VMEM = OPT['vmem'] * 1024 * 1024
NN = (((1,), (0,)), ((), ()))
NT = (((1,), (1,)), ((), ()))
TN = (((0,), (0,)), ((), ()))


def mm(left, right, dims=NN):
    return lax.dot_general(left, right, dims, preferred_element_type=F32)


def factor_of(v):
    return lax.rsqrt(jnp.mean(v * v, axis=-1, keepdims=True) + EPSILON)


def normed(v, gain):
    return (v * factor_of(v) * gain).astype(BF16)


def normed_back(v, gain, u):
    factor = factor_of(v)
    scaled = u * gain
    grad_gain = jnp.sum(u * v * factor, axis=0, keepdims=True)
    inner = jnp.mean(scaled * v, axis=-1, keepdims=True)
    return factor * scaled - v * (factor * factor * factor * inner), grad_gain


def gelu_parts(v):
    c = 0.7978845608028654
    square = v * v
    t = jnp.tanh(v * (c + (c * 0.044715) * square))
    half = 0.5 + 0.5 * t
    slope = half + v * (half * (1.0 - t)) * (c + (3.0 * c * 0.044715) * square)
    return v * half, slope


def causal_mask(enc, length):
    key_pos = lax.broadcasted_iota(jnp.int32, (length, length), 0)
    query_pos = lax.broadcasted_iota(jnp.int32, (length, length), 1)
    return key_pos <= query_pos + enc * length


def scores(q, k, allowed):
    s = mm(k, q, NT)
    return s if allowed is None else jnp.where(allowed, s, NEGATIVE)


def attend(q_ref, q0, kv_ref, k0, v0, out_ref, lse_ref, allowed, width):
    for h in range(width // DH):
        lo = h * DH
        q = q_ref[:, q0 + lo : q0 + lo + DH] * BF16(DH**-0.5)
        k = kv_ref[:, k0 + lo : k0 + lo + DH]
        v = kv_ref[:, v0 + lo : v0 + lo + DH]
        s = scores(q, k, allowed)
        top = jnp.max(s, axis=0, keepdims=True)
        e = jnp.exp(s - top)
        total = jnp.sum(e, axis=0, keepdims=True)
        o = mm(v.T, e.astype(BF16)) * (1.0 / total)
        out_ref[:, lo : lo + DH] = o.T.astype(BF16)
        lse_ref[h : h + 1, :] = top + jnp.log(total)


def attend_back(q_ref, q0, kv_ref, k0, v0, lse_ref, grad, dq_ref, dkv_ref, allowed, width):
    for h in range(width // DH):
        lo = h * DH
        q = q_ref[:, q0 + lo : q0 + lo + DH] * BF16(DH**-0.5)
        k = kv_ref[:, k0 + lo : k0 + lo + DH]
        v = kv_ref[:, v0 + lo : v0 + lo + DH]
        g = grad[:, lo : lo + DH]
        p = jnp.exp(scores(q, k, allowed) - lse_ref[h : h + 1, :])
        dp = mm(v, g, NT)
        delta = jnp.sum(p * dp, axis=0, keepdims=True)
        ds = (p * (dp - delta)).astype(BF16)
        dkv_ref[:, v0 + lo : v0 + lo + DH] = mm(p.astype(BF16), g).astype(BF16)
        dkv_ref[:, k0 + lo : k0 + lo + DH] = mm(ds, q).astype(BF16)
        dq = mm(k.T, ds) * (DH**-0.5)
        dq_ref[:, q0 + lo : q0 + lo + DH] = dq.T.astype(BF16)


def ffn_back(a, g, weights, dgate_refs, dup_refs):
    part = None
    for (wg, wu, wd), dgate_ref, dup_ref in zip(weights, dgate_refs, dup_refs):
        value, slope = gelu_parts(mm(a, wg[...]))
        up = mm(a, wu[...])
        dh = mm(g, wd[...])
        dgate_ref[...] = (dh * up * slope).astype(BF16)
        dup_ref[...] = (dh * value).astype(BF16)
        here = mm(dgate_ref[...], wg[...], NT) + mm(dup_ref[...], wu[...], NT)
        part = here if part is None else part + here
    return part


def ffn_both(a, g, weights, hid_refs, dgate_refs, dup_refs):
    part = None
    for (wg, wu, wd), hid_ref, dgate_ref, dup_ref in zip(weights, hid_refs, dgate_refs, dup_refs):
        gate = mm(a, wg[...])
        up = mm(a, wu[...])
        dh = mm(g, wd[...])
        value, slope = gelu_parts(gate)
        hid_ref[...] = (value * up).astype(BF16)
        dgate_ref[...] = (dh * up * slope).astype(BF16)
        dup_ref[...] = (dh * value).astype(BF16)
        here = mm(dgate_ref[...], wg[...], NT) + mm(dup_ref[...], wu[...], NT)
        part = here if part is None else part + here
    return part


def after(value, *others):
    return lax.optimization_barrier((value,) + others)[0]


class Order:
    def __init__(self):
        self.tokens = []

    def place(self, value):
        return after(value, *self.tokens) if self.tokens else value

    def done(self, value):
        self.tokens = [value]

    def need(self, *values):
        self.tokens = self.tokens + list(values)


TIMES = {
    "first_norm": 2.6,
    "self_forward": 5.7,
    "ffn_first": 5.3,
    "ffn_second": 4.9,
    "memory": 3.7,
    "cross_forward": 8.2,
    "dec_ffn": 9.5,
    "cross_back": 12.3,
    "side_grads": 3.4,
    "dec_down": 3.7,
    "output": 3.4,
    "memory_back": 4.6,
    "down_grads": 3.2,
    "enc_ffn_back": 9.6,
    "pair_grads": 5.0,
    "self_back": 12.3,
    "input_back": 3.8,
    "self_grads": 3.4,
    "ffn_out": 4.0,
    "sum_step": 0.5,
    "attn_out": 1.0,
}
SCALE = 0.0001


def estimate(name):
    tail = name in ("memory_back","down_grads","enc_ffn_back","pair_grads","self_back","side_grads","input_back","self_grads","dec_down","output","ffn_out","attn_out")
    mid = name in ("cross_forward","dec_ffn","cross_back","memory")
    scale = OPT["c_sum"] if name == "sum_step" else OPT["c_tail"] if tail else OPT["c_mid"] if mid else OPT["c_start"]
    flops = max(1, int(scale * TIMES[name] * 1.1e9))
    return pl.CostEstimate(flops=flops, bytes_accessed=1, transcendentals=0)


SMEM_SPEC = pl.BlockSpec(memory_space=pltpu.SMEM)


def whole_spec(spec):
    return spec if spec is SMEM_SPEC else pl.BlockSpec(memory_space=pltpu.VMEM)


ORDER = ['dn_o', 'X:D1', 'X:D2', 'dn_w', 'fb', 'ga_o', 'X:G', 'ga_w', 'v:D1', 'up_o', 'X:U', 'v:D2', 'up_w', 'sb', 's:D1', 'sb2', 's:D2', 'v:G', 'sd_o', 'X:S', 'sd_w', 't:D1', 'ib', 'q_o', 'X:Q1', 'X:Q2', 'q_w', 't:D2', 'v:U', 's:G', 'v:S', 'r:D1', 's:U', 'v:Q1', 'r:D2', 't:G', 's:S', 'v:Q2', 't:U', 'dd', 's:Q1', 'r:G', 't:S', 's:Q2', 'r:U', 't:Q1', 'out', 'ffo', 't:Q2']


class Call:
    def __init__(self, rows, length, order):
        self.rows, self.length, self.order = rows, length, order
        self.specs, self.args, self.out_specs, self.out_shapes = [], [], [], []
        self.in_views, self.out_views = [], []

    @property
    def views(self):
        return self.in_views + self.out_views

    def scalar(self, value):
        self.specs.append(SMEM_SPEC)
        self.args.append(value)
        self.in_views.append(None)

    def tokens(self, *values):
        for value in values:
            count = value.shape[0] // self.rows
            self.specs.append(pl.BlockSpec((count, value.shape[1]), lambda i: (i, 0)))
            self.args.append(value)
            self.in_views.append(None)

    def heads(self, *values):
        for value in values:
            self.specs.append(pl.BlockSpec((None,) + value.shape[1:], lambda i: (i, 0, 0)))
            self.args.append(value)
            self.in_views.append(0)

    def whole(self, *values):
        for value in values:
            block = None
            if isinstance(value, tuple):
                value, block, at = value
            if block is None:
                block, at = value.shape, (0,) * value.ndim
            self.specs.append(pl.BlockSpec(block, lambda i, at=at: at))
            self.args.append(value)
            view = tuple(
                k if size is None else pl.ds(k * size, size) for k, size in zip(at, block)
            )
            self.in_views.append(None if block == value.shape else view)

    def out_tokens(self, width, kind, count=None):
        count = self.length if count is None else count
        self.out_views.append(None)
        self.out_specs.append(pl.BlockSpec((count, width), lambda i: (i, 0)))
        self.out_shapes.append(jax.ShapeDtypeStruct((self.rows * count, width), kind))

    def out_heads(self, heads):
        self.out_views.append(0)
        self.out_specs.append(pl.BlockSpec((None, heads, self.length), lambda i: (i, 0, 0)))
        self.out_shapes.append(jax.ShapeDtypeStruct((self.rows, heads, self.length), F32))

    def out_whole(self, shape, kind):
        self.out_views.append(None)
        self.out_specs.append(pl.BlockSpec(shape, lambda i, n=len(shape): (0,) * n))
        self.out_shapes.append(jax.ShapeDtypeStruct(shape, kind))

    def narrowed(self, kernel):
        views = list(self.views)

        def inner(*refs):
            kernel(*[ref if view is None else ref.at[view] for ref, view in zip(refs, views)])

        return inner

    def run(self, kernel, name):
        first = next(k for k, v in enumerate(self.args) if v.dtype != jnp.int32)
        self.args[first] = self.order.place(self.args[first])
        more = {"grid": (self.rows,)}
        if self.rows == 1:
            more = {}
            self.specs = [whole_spec(spec) for spec in self.specs]
            self.out_specs = [whole_spec(spec) for spec in self.out_specs]
            kernel = self.narrowed(kernel)
        out = pl.pallas_call(
            kernel,
            in_specs=self.specs,
            out_specs=self.out_specs,
            out_shape=self.out_shapes,
            **more,
            compiler_params=pltpu.CompilerParams(vmem_limit_bytes=VMEM),
            cost_estimate=estimate(name),
            name=name,
        )(*self.args)
        self.order.done(out[0])
        return out


def accumulate(ref, value, first):

    if first is True:
        ref[...] = value
        return

    @pl.when(first)
    def _():
        ref[...] = value

    @pl.when(jnp.logical_not(first))
    def _():
        ref[...] += value


def on_device(layer_input, dec_lengths, out_cotangent, gains, attn_weights, ffn_weights):
    tensor = lax.axis_size("tensor")
    planes = lax.axis_size("dp")
    batch, part_len, model = layer_input.shape[1:]
    groups = 2 if tensor % 2 == 0 and batch % 2 == 0 else 1
    cores = tensor // groups
    rows = batch // groups
    length = part_len * tensor
    tokens = rows * length
    share = length // cores
    width = attn_weights.shape[3]
    hidden_width = ffn_weights.shape[3]
    heads = width // DH
    shares = range(groups)

    section = lax.axis_index("section")
    plane = lax.axis_index("dp")
    lane = lax.axis_index("tensor")
    group = lane // cores
    core = lane % cores
    is_enc = section == 0
    outer = (plane == 0) | (plane == planes - 1)
    place = jnp.stack([v.astype(jnp.int32) for v in (is_enc, core, outer, plane % 2, group)])
    group_route = [(t, (t + cores) % tensor) for t in range(tensor)]
    core_groups = [[g * cores + c for c in range(cores)] for g in range(groups)]
    next_plane = [(p, p ^ 1) for p in range(planes)]
    order = Order()

    def over_groups(value):
        return lax.ppermute(value, "tensor", group_route)

    def decoder_only(value, axis, route):
        size = lax.axis_size(axis)
        return lax.ppermute(value, ("section", axis), [(size + a, size + b) for a, b in route])

    def encoder_only(value, axis, route):
        return lax.ppermute(value, ("section", axis), route)

    def core_route(step):
        return [
            (g * cores + (c + step) % cores, g * cores + c)
            for g in range(groups)
            for c in range(cores)
        ]

    def core_swap(value):
        return [lax.ppermute(value, "tensor", core_route(k)) for k in range(1, cores)]

    def core_sum(part):
        if cores <= 2:
            return [part] + core_swap(part)
        return [lax.psum(part, "tensor", axis_index_groups=core_groups)]

    def pick(value, index, count):
        return lax.dynamic_slice_in_dim(value, index * count, count, 0)

    def move(value, axis, route, decoder):
        return decoder_only(value, axis, route) if decoder else lax.ppermute(value, axis, route)

    queues = {}

    def queued(link, value, transfer):
        lag = OPT["lag"].get(link, 0)
        line = queues.setdefault(link, [])
        if lag and len(line) >= lag:
            value = after(value, line[-lag])
        got = transfer(value)
        line.append(got)
        return got

    class Fetch:
        def __init__(self, own, at, count, *behind, assisted=True):
            self.halved = assisted and planes % 2 == 0 and count % 32 == 0
            if self.halved:
                count //= 2
                at = at + (plane % 2) * count
            value = lax.dynamic_slice_in_dim(own, at, count, 0)
            if behind:
                value = after(value, *behind)
            self.direct = queued("X0", value, over_groups)

        def forward(self, placed=True):
            if self.halved:
                if placed:
                    self.direct = order.place(self.direct)
                    order.need(self.direct)
                self.passed = queued("Z0", self.direct, lambda v: lax.ppermute(v, "dp", next_plane))

        def arrived(self):
            return self.passed if self.halved else self.direct

        def parts(self):
            return [self.direct, self.passed] if self.halved else [self.direct]

    def assemble(place_ref, refs, out_ref, halved):
        if len(refs) == 1:
            out_ref[...] = refs[0][...]
            return
        half = refs[0].shape[0]
        first = place_ref[3] * half if halved else 0
        second = half - first
        out_ref[pl.ds(pl.multiple_of(first, half), half), :] = refs[0][...]
        out_ref[pl.ds(pl.multiple_of(second, half), half), :] = refs[1][...]

    def to_rows(value, route_group):
        if groups == 1:
            blocks = value[:, None]
        else:
            mine = pick(value, group, rows)
            got = route_group(pick(value, 1 - group, rows))
            first = group == 0
            blocks = jnp.stack([jnp.where(first, mine, got), jnp.where(first, got, mine)], 1)
        if cores == 2:
            got = core_swap(blocks)[0]
            low = core == 0
            blocks = jnp.stack([jnp.where(low, blocks, got), jnp.where(low, got, blocks)], 2)
        elif cores > 2:
            blocks = lax.all_gather(blocks, "tensor", axis=2, axis_index_groups=core_groups)
        return blocks.reshape(tokens, model)

    def from_rows(value):
        blocks = value.reshape(rows, tensor, part_len, model)
        mine = lax.dynamic_index_in_dim(blocks, lane, 1, keepdims=False)
        if groups == 1:
            return mine
        got = over_groups(
            lax.dynamic_index_in_dim(blocks, (lane + cores) % tensor, 1, keepdims=False)
        )
        first = group == 0
        return jnp.concatenate([jnp.where(first, mine, got), jnp.where(first, got, mine)], 0)

    def split(refs, *counts):
        at, out = 0, []
        for count in counts:
            out.append(refs[at : at + count])
            at += count
        return out

    def call():
        return Call(rows, length, order)

    def first_row():
        return True if rows == 1 else pl.program_id(0) == 0

    attn_t = attn_weights[0].transpose(0, 2, 1).reshape(6 * width, model)
    ffn = ffn_weights[0]
    gain = gains[0]

    own_self = (attn_t, (4 * width, model), (0, 0))
    own_side = (attn_t, (2 * width, model), (2, 0))
    own_ffn = [(ffn, (None, model, hidden_width), (j, 0, 0)) for j in range(3)]
    w_self, w_ffn, w_dec, w_side = [own_self], [own_ffn], [own_ffn], [own_side]
    x_parts = [pick(layer_input[0], group, rows)]
    if groups == 2:
        x_parts.append(queued("X0", pick(layer_input[0], 1 - group, rows), over_groups))
        flat = ffn.reshape(3 * model, hidden_width)
        behind = {"none": [], "in": [x_parts[1]], "slice": [pick(layer_input[0], 1 - group, rows)]}
        far_self = Fetch(attn_t, 0, 4 * width, *behind[OPT["self_after"]], assisted=not OPT["self_direct"])
        far_pair = [Fetch(flat, 0, model, *{"in": [x_parts[1]], "none": [], "self": [far_self.direct]}[OPT["pair_after"]])]
        far_pair.append(Fetch(flat, model, model, *{"in": [x_parts[1]], "g": [far_pair[0].direct], "none": [], "self": [far_self.direct]}[OPT["u_after"]]))
        half = model // 2
        far_down = [ffn[2, :half], ffn[2, half:]]
        opts = {"none": [], "in": [x_parts[1]], "g": [far_pair[0].direct], "u": [far_pair[1].direct], "self": [far_self.direct]}
        for k in range(2):
            if opts[OPT["d%d_after" % k]]:
                far_down[k] = after(far_down[k], *opts[OPT["d%d_after" % k]])
        far_down = [queued("X0", v, lambda v: encoder_only(v, "tensor", group_route)) for v in far_down]
    side_out = attn_t[4 * width :]
    if OPT["y_after"] == "in":
        side_out = after(side_out, x_parts[1])
    if OPT["y_after"] == "self":
        side_out = after(side_out, far_self.direct)
    enc_side = lax.ppermute(side_out, "section", [(0, 1)])
    x_parts = x_parts + [v for part in zip(*[core_swap(v) for v in x_parts]) for v in part]

    c = call()
    c.scalar(place)
    c.heads(*x_parts)
    c.whole(gain[0:1])
    c.out_tokens(model, BF16)
    c.out_tokens(model, BF16)

    def first_norm(place_ref, *refs):
        gain_ref, x_ref, a_ref = refs[-3:]
        for k, ref in enumerate(refs[:-3]):
            from_core = lax.rem(place_ref[1] + k // groups, cores)
            from_group = lax.rem(place_ref[4] + k % groups, groups)
            at = (from_group * cores + from_core) * part_len
            x_ref[pl.ds(pl.multiple_of(at, part_len), part_len), :] = ref[...]
        a_ref[...] = normed(x_ref[...].astype(F32), gain_ref[...])

    if groups == 2:
        if OPT["pass_self"] != "cluster":
            far_self.forward(False)
        if OPT["pass_self"] == "norm":
            order.need(far_self.direct)
    x, a0 = c.run(first_norm, "first_norm")

    if OPT['cot'] == 0:
        cot = to_rows(out_cotangent, lambda v: decoder_only(v, "tensor", group_route))
        row_ids = group * rows + jnp.arange(rows)
        live = jnp.arange(length)[None, :] < dec_lengths[row_ids][:, None]
        live = live.reshape(tokens, 1)
        gy = jnp.where(live, cot, BF16(0))

    def self_forward(i, part):
        pieces = far_self.parts() if i == 1 else [w_self[i]]
        made = i == 1 and len(pieces) > 1
        if i == 1 and not made:
            w_self.append(pieces[0])
        c = call()
        c.scalar(place)
        c.tokens(a0)
        c.whole(*pieces)
        if part is not None:
            c.tokens(part)
        c.out_tokens(3 * width, BF16)
        c.out_tokens(width, BF16)
        c.out_heads(heads)
        c.out_tokens(model, BF16 if i == groups - 1 else F32)
        if made:
            c.out_whole((4 * width, model), BF16)

        def kernel(place_ref, a_ref, *refs):
            qkv_ref, att_ref, lse_ref, part_ref = refs[-5:-1] if made else refs[-4:]
            w_ref = refs[0]
            if made:
                w_ref = refs[-1]
                assemble(place_ref, refs[: len(pieces)], w_ref, far_self.halved)
            qkv_ref[...] = mm(a_ref[...], w_ref[: 3 * width, :], NT).astype(BF16)
            allowed = causal_mask(place_ref[0], length)
            attend(
                qkv_ref, 0, qkv_ref, width, 2 * width, att_ref, lse_ref, allowed, width
            )
            out = mm(att_ref[...], w_ref[3 * width :, :])
            if part is not None:
                out = out + refs[len(pieces)][...]
            part_ref[...] = out.astype(part_ref.dtype)

        return c.run(kernel, "self_forward")

    qkv, att, lse, part = [], [], [], None
    for i in shares:
        if i == 1:
            order.need(enc_side)
            if OPT['cot'] == 0:
                order.need(gy)
            if OPT["self_direct"] == 3:
                order.need(far_self.arrived())
            elif OPT["pass_self"] == "cluster":
                for fetch in far_pair if OPT["self_direct"] else (far_self, *far_pair):
                    if OPT["self_direct"] == 2 and fetch is far_pair[1]:
                        continue
                    fetch.forward()
                    order.done(fetch.direct)
                order.need(far_self.arrived())
            else:
                far_pair[0].forward()
                far_pair[1].forward()
        a, b, l, part, *rest = self_forward(i, part)
        w_self += rest
        qkv.append(a)
        att.append(b)
        lse.append(l)
    if groups == 2 and OPT["self_direct"] == 2 and OPT["pass_self"] == "cluster":
        far_pair[1].forward()
        order.done(far_pair[1].direct)
        part = order.place(part)
    if groups == 2 and OPT["self_direct"] != 3:
        pins = ([far_down[0]] if OPT["pin_d0"] else []) + ([far_pair[0].arrived()] if OPT["pin_zg"] else []) + ([far_pair[1].arrived()] if OPT["pin_zu"] else [])
        if pins:
            part = after(part, *pins)
    parts = core_sum(part)

    def total_of(refs):
        value = refs[0][...].astype(F32)
        for ref in refs[1:]:
            value = value + ref[...].astype(F32)
        return value

    def ffn_share(a, wg, wu, wd, hid_ref):
        value, _ = gelu_parts(mm(a, wg[...]))
        hid_ref[...] = (value * mm(a, wu[...])).astype(BF16)
        return mm(hid_ref[...], wd[...], NT)

    if OPT['cot'] in (2, 3, 5, 6, 8):
        cot = to_rows({2: lambda: after(out_cotangent, parts[0]), 3: lambda: out_cotangent, 5: lambda: after(out_cotangent, a0), 6: lambda: after(out_cotangent, a0), 8: lambda: after(out_cotangent, far_pair[1].direct)}[OPT['cot']](), lambda v: decoder_only(v, "tensor", group_route))
        row_ids = group * rows + jnp.arange(rows)
        live = jnp.arange(length)[None, :] < dec_lengths[row_ids][:, None]
        live = live.reshape(tokens, 1)
        gy = jnp.where(live, cot, BF16(0))

    if OPT['cot'] == 5:
        order.need(gy)
    c = call()
    c.tokens(x, *parts)
    c.whole(gain[1:2], *w_ffn[0])
    c.out_tokens(model, F32)
    c.out_tokens(model, BF16)
    c.out_tokens(hidden_width, BF16)
    c.out_tokens(model, BF16 if groups == 1 else F32)

    def ffn_first(x_ref, *refs):
        count = len(parts)
        gain_ref, wg, wu, wd, x1_ref, a1_ref, hid_ref, part_ref = refs[count:]
        x1 = x_ref[...].astype(F32) + total_of(refs[:count])
        x1_ref[...] = x1
        a1_ref[...] = normed(x1, gain_ref[...])
        part_ref[...] = ffn_share(a1_ref[...], wg, wu, wd, hid_ref).astype(part_ref.dtype)

    x1, a1, hid, part = c.run(ffn_first, "ffn_first")
    if OPT["cot"] in (2, 3, 6, 8):
        order.need(gy)
    e_hid = [hid]
    if groups == 2 and OPT["self_direct"] == 3:
        for fetch in far_pair:
            fetch.forward()
            order.done(fetch.direct)
    if groups == 2:
        both_sides = decoder_only(
            after(
                jnp.concatenate([attn_t[4 * width :], enc_side], 0),
                *{"none": [], "self": [far_self.direct], "g": [far_pair[0].direct], "u": [far_pair[1].direct]}[OPT["both_after"]],
            ) if OPT["both_after"] != "none" else jnp.concatenate([attn_t[4 * width :], enc_side], 0), "tensor", group_route
        )
        pieces = [fetch.parts() for fetch in far_pair]
        c = call()
        c.scalar(place)
        c.tokens(a1, part)
        c.whole(*[v for got in pieces for v in got], *far_down)
        c.out_tokens(model, BF16)
        c.out_tokens(hidden_width, BF16)
        c.out_whole((2 * model, hidden_width), BF16)
        c.out_whole((model, hidden_width), BF16)

        def ffn_second(place_ref, a_ref, prev_ref, *refs):
            *piece_refs, down_refs, (part_ref, hid_ref, pair_ref, wd) = split(
                refs, *[len(got) for got in pieces], 2, 4
            )
            for k in range(2):
                w = pair_ref.at[k * model : (k + 1) * model]
                assemble(place_ref, piece_refs[k], w, far_pair[k].halved)
            for k, ref in enumerate(down_refs):
                wd[k * half : (k + 1) * half, :] = ref[...]
            ws = pair_ref.at[:model], pair_ref.at[model:], wd
            part_ref[...] = (prev_ref[...] + ffn_share(a_ref[...], *ws, hid_ref)).astype(BF16)

        part, hid, pair, far_down = c.run(ffn_second, "ffn_second")
        far = [(pair, (model, hidden_width), (k, 0)) for k in range(2)]
        dec_far = decoder_only(ffn[2], "tensor", group_route)
        w_dec = [own_ffn, far + [dec_far]]
        w_ffn.append(far + [far_down])
        e_hid.append(hid)
        if OPT["both"] == "core2":
            part = after(part, both_sides)
    parts = core_sum(part)

    c = call()
    c.scalar(place)
    c.tokens(x1, *parts)
    c.whole(gain[2:3])
    c.out_tokens(model, F32)
    c.out_tokens(model, BF16)
    c.out_tokens(model, BF16, share)

    def memory_kernel(place_ref, x1_ref, *refs):
        gain_ref, y_ref, memory_ref, mine_ref = refs[-4:]
        y = x1_ref[...] + total_of(refs[:-4])
        y_ref[...] = y
        memory_ref[...] = normed(y, gain_ref[...])
        start = pl.multiple_of(place_ref[1] * share, share)
        mine_ref[...] = memory_ref[pl.ds(start, share), :]

    if groups == 2:
        if OPT["both"] == "memory":
            order.need(both_sides)
        if OPT["dec_far"] == "memory":
            order.need(dec_far)
        if OPT["both"] == "cross":
            both_raw = both_sides
        both_sides = [(both_sides, (2 * width, model), (k, 0)) for k in range(2)]
    y, memory, mem_mine = c.run(memory_kernel, "memory")
    mem_mine = lax.ppermute(mem_mine, "section", [(0, 1)])
    mem = [mem_mine] + core_swap(mem_mine)

    if OPT['cot'] in (1, 4, 7):
        cot = to_rows(after(out_cotangent, far_pair[1].direct) if OPT['cot'] == 7 else order.place(out_cotangent), lambda v: decoder_only(v, "tensor", group_route))
        row_ids = group * rows + jnp.arange(rows)
        live = jnp.arange(length)[None, :] < dec_lengths[row_ids][:, None]
        live = live.reshape(tokens, 1)
        gy = jnp.where(live, cot, BF16(0))

        if OPT['cot'] in (4, 7):
            gy = order.place(gy)
            order.done(gy)
    w_side, w_enc = [own_side], [enc_side]
    if groups == 2:
        w_side.append(both_sides[0])
        w_enc.append(both_sides[1])
    c = call()
    c.scalar(place)
    c.tokens(a1, *mem)
    c.whole(*w_side, *w_enc)
    for i in shares:
        c.out_tokens(width, BF16)
    for i in shares:
        c.out_tokens(2 * width, BF16)
    for i in shares:
        c.out_tokens(width, BF16)
    for i in shares:
        c.out_heads(heads)
    c.out_tokens(model, BF16)

    def cross_forward(place_ref, a_ref, *refs):
        mem_refs, side, enc, cq, kv, catt, clse, (part_ref,) = split(
            refs, cores, groups, groups, groups, groups, groups, groups, 1
        )
        out = None
        for i in shares:
            cq[i][...] = mm(a_ref[...], side[i][:width, :], NT).astype(BF16)
            for j, ref in enumerate(mem_refs):
                kv[i][j * share : (j + 1) * share, :] = mm(ref[...], enc[i][...], NT).astype(BF16)
            attend(cq[i], 0, kv[i], 0, width, catt[i], clse[i], None, width)
            here = mm(catt[i][...], side[i][width:, :])
            out = here if out is None else out + here
        part_ref[...] = out.astype(BF16)

    if groups == 2:
        if OPT["dec_far"] == "cross":
            order.need(dec_far)
        if OPT["both"] == "cross":
            order.need(both_raw)
    cq, kv, catt, clse, (part,) = split(
        c.run(cross_forward, "cross_forward"), groups, groups, groups, groups, 1
    )
    parts = core_sum(part)

    c = call()
    c.tokens(x1, gy, *parts)
    c.whole(gain[2:3], *[w for ws in w_dec for w in ws])
    c.out_tokens(model, F32)
    c.out_tokens(model, BF16)
    for _ in range(3 * groups):
        c.out_tokens(hidden_width, BF16)
    c.out_tokens(model, BF16)

    def triples(refs):
        return [refs[3 * i : 3 * i + 3] for i in shares]

    def dec_ffn(x1_ref, gy_ref, *refs):
        part_refs, (gain_ref,), ws, (x2_ref, a2_ref), hid, dgate, dup, (part_ref,) = split(
            refs, len(parts), 1, 3 * groups, 2, groups, groups, groups, 1
        )
        x2 = x1_ref[...] + total_of(part_refs)
        x2_ref[...] = x2
        a2_ref[...] = normed(x2, gain_ref[...])
        part_ref[...] = ffn_both(
            a2_ref[...], gy_ref[...], triples(ws), hid, dgate, dup
        ).astype(BF16)

    (x2, a2), d_hid, d_gate, d_up, (part,) = split(
        c.run(dec_ffn, "dec_ffn"), 2, groups, groups, groups, 1
    )
    parts = core_sum(part)

    c = call()
    c.tokens(x2, gy, *parts, *cq, *kv)
    c.heads(*clse)
    c.whole(gain[2:3], *w_side, *w_enc)
    c.out_tokens(model, F32)
    c.out_tokens(model, BF16)
    c.out_whole((1, model), F32)
    for i in shares:
        c.out_tokens(width, BF16)
    c.out_tokens(2 * width * groups, BF16)
    c.out_tokens(model, BF16)
    for j in range(cores):
        c.out_tokens(model, F32 if j == 0 else BF16, share)

    def cross_back(x2_ref, gy_ref, *refs):
        (
            part_refs, cq_refs, kv_refs, lse_refs, (gain_ref,), side, enc,
            (g2_ref, low_ref, gain2_ref), dcq_refs, (dkv_ref, part_ref), mem_refs,
        ) = split(
            refs, len(parts), groups, groups, groups, 1, groups, groups, 3, groups, 2, cores
        )
        dkv_refs = [dkv_ref.at[:, 2 * width * i : 2 * width * (i + 1)] for i in shares]
        back, grad_gain = normed_back(x2_ref[...], gain_ref[...], total_of(part_refs))
        accumulate(gain2_ref, grad_gain, first_row())
        g2 = gy_ref[...].astype(F32) + back
        g2_ref[...] = g2
        low_ref[...] = g2.astype(BF16)
        out = None
        for i in shares:
            grad = mm(low_ref[...], side[i][width:, :], NT).astype(BF16)
            attend_back(
                cq_refs[i], 0, kv_refs[i], 0, width, lse_refs[i], grad,
                dcq_refs[i], dkv_refs[i], None, width,
            )
            here = mm(dcq_refs[i][...], side[i][:width, :])
            out = here if out is None else out + here
        part_ref[...] = out.astype(BF16)
        for j, ref in enumerate(mem_refs):
            total = None
            for i in shares:
                here = mm(dkv_refs[i][j * share : (j + 1) * share, :], enc[i][...])
                total = here if total is None else total + here
            ref[...] = total.astype(ref.dtype)

    (g2, g2_low, dec_gain2), dcq, (dkv, part_dec), dmem = split(
        c.run(cross_back, "cross_back"), 3, groups, 2, cores
    )
    mine = dmem[0]
    for step in range(1, cores):
        mine = mine + lax.ppermute(dmem[step], "tensor", core_route(cores - step)).astype(F32)
    mine = mine.astype(BF16)
    order.done(mine)
    mine = lax.ppermute(mine, "section", [(1, 0)])
    dmem = [mine] + core_swap(mine)
    kept = {}
    if "yk" not in ORDER:
        kept["dkv"] = lax.ppermute(dkv, "section", [(1, 0)])

    chunk = 4 * width // 3

    def products(terms, tails, counts, name):
        sizes = [[len(values) for values in term] for term in terms]
        flat = [v for term in terms for values in term for v in values] + tails
        flat[0] = order.place(flat[0])

        def product(left_refs, right_refs):
            total = None
            for j, right in enumerate(right_refs):
                spans = [(left_refs[j][...], right[...])]
                for left, value in spans:
                    here = mm(left, value, TN)
                    total = here if total is None else total + here
            return total

        def kernel(place_ref, *refs):
            outs = refs[len(flat) :]
            starts = [sum(counts[:k]) for k in range(len(counts))]

            def store(value, at):
                done = 0
                while done < value.shape[0]:
                    k = max(q for q in range(len(counts)) if starts[q] <= at + done)
                    inside = at + done - starts[k]
                    count = min(value.shape[0] - done, counts[k] - inside)
                    outs[k][inside : inside + count, :] = value[done : done + count].astype(BF16)
                    done += count

            used, at = 0, 0
            for size in sizes:
                values = split(refs[used:], *size)
                used += sum(size)
                if len(size) == 2:
                    store(product(*values), at)
                else:

                    @pl.when(place_ref[0] == 1)
                    def _(values=values, at=at):
                        store(product(*values[:2]), at)

                    @pl.when(place_ref[0] == 0)
                    def _(values=values, at=at):
                        store(product(*values[2:]), at)

                at += values[0][0].shape[1]
            for tail in refs[used : len(flat)]:
                store(tail[...], at)
                at += tail.shape[0]

        out = pl.pallas_call(
            kernel,
            in_specs=[SMEM_SPEC] + [pl.BlockSpec(memory_space=pltpu.VMEM)] * len(flat),
            out_shape=[jax.ShapeDtypeStruct((count, model), BF16) for count in counts],
            compiler_params=pltpu.CompilerParams(vmem_limit_bytes=VMEM),
            cost_estimate=estimate(name),
            name=name,
        )(place, *flat)
        order.done(out[-1])
        return list(out)

    def add_kernel(value, got):
        def kernel(value_ref, got_ref, out_ref):
            total = value_ref[...].astype(F32) + got_ref[...].astype(F32)
            out_ref[...] = total.astype(BF16)

        c = Call(1, length, order)
        c.whole(value, got)
        c.out_whole(value.shape, BF16)
        return c.run(kernel, "sum_step")[0]

    class Sum:
        def __init__(self):
            self.got, self.at = None, 0
            half = planes // 2
            self.moves = [("group", group_route)] if groups == 2 else []
            if planes % 2 == 0:
                for k in range(half - 1):
                    self.moves.append(("add", [(k, k + 1), (planes - 1 - k, planes - 2 - k)]))
                self.moves.append(("add", [(half - 1, half), (half, half - 1)]))
                for k in range(half - 1):
                    left, right = half - 1 - k, half + k
                    self.moves.append(("take", [(left, left - 1), (right, right + 1)]))

        def send(self):
            if groups == 2:
                self.got = queued("X", self.other, over_groups)

        def step(self):
            if self.at == len(self.moves):
                return
            kind, route = self.moves[self.at]
            if self.got is None:
                self.got = lax.ppermute(self.value, "dp", route)
            names = "XABR" if groups == 2 and planes == 4 else "X" * 100
            last = self.at == len(self.moves) - 1
            if last and kind == "take":
                got = self.got
                order.need(got)
            else:
                got = order.place(self.got)
            if kind == "take":
                targets = [b for _, b in route]
                self.value = jnp.where((plane == targets[0]) | (plane == targets[1]), got, self.value)
            else:
                self.value = add_kernel(self.value, got)
            if not (last and kind == "take"):
                order.done(self.value)
            self.at += 1
            if not last:
                route = self.moves[self.at][1]
                self.got = queued(names[self.at], self.value, lambda v: lax.ppermute(v, "dp", route))

        def finish(self):
            while self.at < len(self.moves):
                self.step()
            if planes % 2 and planes > 1:
                self.value = lax.psum(self.value, "dp")
            return self.value

    sums = {}

    def add_products(names, arrays, own):
        for name, array in zip(names, arrays):
            one = sums.setdefault(name, Sum())
            if own:
                one.value = array
            else:
                one.other = array

    def side_grads(i):
        args = [order.place(memory), kept["dkv"], dcq[i], a1, catt[i], g2_low]

        def kernel(place_ref, memory_ref, dkv_ref, dcq_ref, a1_ref, catt_ref, g2_ref, *out_refs):
            @pl.when(place_ref[0] == 1)
            def _():
                total = None
                for row in range(rows):
                    for j in range(cores):
                        at = row * length + lax.rem(place_ref[1] + j, cores) * share
                        right = memory_ref[pl.ds(pl.multiple_of(at, share), share), :]
                        start = row * length + j * share
                        left = dkv_ref[start : start + share, 2 * width * i : 2 * width * (i + 1)]
                        here = mm(left, right, TN)
                        total = here if total is None else total + here
                out_refs[0][...] = total.astype(BF16)

            @pl.when(place_ref[0] == 0)
            def _():
                out_refs[0][:width, :] = mm(dcq_ref[...], a1_ref[...], TN).astype(BF16)
                out_refs[0][width:, :] = mm(catt_ref[...], g2_ref[...], TN).astype(BF16)

        out = pl.pallas_call(
            kernel,
            in_specs=[SMEM_SPEC] + [pl.BlockSpec(memory_space=pltpu.VMEM)] * len(args),
            out_shape=[jax.ShapeDtypeStruct((2 * width, model), BF16)],
            compiler_params=pltpu.CompilerParams(vmem_limit_bytes=VMEM),
            cost_estimate=estimate("side_grads"),
            name="side_grads",
        )(place, *args)
        order.done(out[-1])
        return out

    def decoder_down():
        c = call()
        c.tokens(*d_hid)
        c.whole(*[ws[2] for ws in w_dec])
        c.out_tokens(model, BF16)

        def dec_down(*refs):
            hid_refs, ws, (out_ref,) = split(refs, groups, groups, 1)
            total = None
            for hid_ref, w in zip(hid_refs, ws):
                here = mm(hid_ref[...], w[...], NT)
                total = here if total is None else total + here
            out_ref[...] = total.astype(BF16)

        return core_sum(c.run(dec_down, "dec_down")[0])

    def decoder_output(last):
        c = call()
        c.scalar(place)
        c.tokens(memory, live.astype(F32), x2, *last)
        c.out_tokens(model, BF16)

        def output(place_ref, memory_ref, live_ref, x2_ref, *refs):
            total = (x2_ref[...] + total_of(refs[:-1])) * live_ref[...]
            refs[-1][...] = jnp.where(place_ref[0] == 1, memory_ref[...], total.astype(BF16))

        return c.run(output, "output")[0]

    c = call()
    c.scalar(place)
    c.tokens(y, *dmem, gy, g2)
    c.whole(gain[2:3], dec_gain2)
    c.out_tokens(model, BF16)
    c.out_tokens(model, F32)
    c.out_whole((1, model), F32)

    def memory_back(place_ref, y_ref, *refs):
        dmem_refs, (gy_ref, g2_ref, gain_ref, old_gain, low_ref, g_ref, new_gain) = split(
            refs, cores, 7
        )

        @pl.when(place_ref[0] == 1)
        def _():
            for j, ref in enumerate(dmem_refs):
                at = lax.rem(place_ref[1] + j, cores)
                g_ref[pl.ds(pl.multiple_of(at * share, share), share), :] = ref[...].astype(F32)
            e_g, grad_gain = normed_back(y_ref[...], gain_ref[...], g_ref[...])
            accumulate(new_gain, grad_gain, first_row())
            g_ref[...] = e_g
            low_ref[...] = e_g.astype(BF16)

        @pl.when(place_ref[0] == 0)
        def _():
            low_ref[...] = gy_ref[...]
            g_ref[...] = g2_ref[...]
            new_gain[...] = old_gain[...]

    ffn_g, g_in, gain2 = c.run(memory_back, "memory_back")

    def down_grads(i):
        terms = [([e_hid[i]], [ffn_g], [d_hid[i]], [ffn_g])]
        return products(terms, [], [hidden_width // 2] * 2, "down_grads")

    kept["g_in"] = g_in

    def ffn_back_step():
        global_parts = encoder_ffn_back()
        kept["parts"] = core_sum(global_parts)

    def encoder_ffn_back():
        c = call()
        c.scalar(place)
        c.tokens(ffn_g, a1, part_dec)
        c.whole(*[w for ws in w_ffn for w in ws])
        c.out_tokens(model, BF16)
        for _ in range(2 * groups):
            c.out_tokens(hidden_width, BF16)

        def enc_ffn_back(place_ref, g_ref, a1_ref, old_part, *refs):
            ws, (part_ref,), dgate, dup = split(refs, 3 * groups, 1, groups, groups)

            @pl.when(place_ref[0] == 1)
            def _():
                part_ref[...] = ffn_back(
                    a1_ref[...], g_ref[...], triples(ws), dgate, dup
                ).astype(BF16)

            @pl.when(place_ref[0] == 0)
            def _():
                part_ref[...] = old_part[...]

        (part,), kept["gate"], kept["up"] = split(c.run(enc_ffn_back, "enc_ffn_back"), 1, groups, groups)

        def pair_grads(i):
            terms = [
                ([e_gate[i]], [a1], [d_gate[i]], [a2]),
                ([e_up[i]], [a1], [d_up[i]], [a2]),
            ]
            return products(terms, [], [hidden_width] * 2, "pair_grads")
        return part

    def gate_up(i, which):
        return products([(
            [kept[("gate", "up")[which]][i]], [a1], [(d_gate, d_up)[which][i]], [a2],
        )], [], [hidden_width], "pair_grads")

    def self_back(i):
        c = call()
        c.scalar(place)
        if i == 0:
            c.tokens(x1, kept["g_in"], *kept["parts"])
        else:
            c.tokens(kept["g1_low"], kept["part"])
        c.tokens(qkv[i])
        c.heads(lse[i])
        if i == 0:
            c.whole(gain[1:2])
        c.whole(w_self[i])
        if i == 0:
            c.out_tokens(model, F32)
            c.out_tokens(model, BF16)
            c.out_whole((1, model), F32)
        c.out_tokens(3 * width, BF16)
        c.out_tokens(model, BF16 if i == groups - 1 else F32)

        def kernel(place_ref, *refs):
            if i == 0:
                (
                    (x1_ref, g_ref), part_refs, (qkv_ref, lse_ref, gain_ref, w_ref),
                    (g1_ref, low_ref, gain1_ref, d_ref, part_ref),
                ) = split(refs, 2, len(kept["parts"]), 4, 5)
                back, grad_gain = normed_back(x1_ref[...], gain_ref[...], total_of(part_refs))
                accumulate(gain1_ref, grad_gain, first_row())
                g1 = g_ref[...] + back
                g1_ref[...] = g1
                low_ref[...] = g1.astype(BF16)
            else:
                low_ref, prev_ref, qkv_ref, lse_ref, w_ref, d_ref, part_ref = refs
            allowed = causal_mask(place_ref[0], length)
            grad = mm(low_ref[...], w_ref[3 * width :, :], NT).astype(BF16)
            attend_back(
                qkv_ref, 0, qkv_ref, width, 2 * width, lse_ref, grad, d_ref, d_ref, allowed, width
            )
            out = mm(d_ref[...], w_ref[: 3 * width, :])
            if i > 0:
                out = out + prev_ref[...]
            part_ref[...] = out.astype(part_ref.dtype)

        *first, d, kept["part"] = c.run(kernel, "self_back")
        if i == 0:
            kept["g1"], kept["g1_low"], kept["gain1"] = first
        kept.setdefault("dqkv", []).append(d)
        if i == groups - 1:
            kept["parts"] = core_sum(kept["part"])

    def input_back_step():
        c = call()
        c.tokens(x, kept["g1"], *kept["parts"])
        c.whole(gain[0:1], kept["gain1"], gain2)
        c.out_tokens(model, BF16)
        c.out_whole((16, model), F32)

        def input_back(x_ref, g1_ref, *refs):
            gain_ref, gain1_ref, gain2_ref, dx_ref, rows_ref = refs[-5:]
            back, grad_gain = normed_back(
                x_ref[...].astype(F32), gain_ref[...], total_of(refs[:-5])
            )
            dx_ref[...] = (g1_ref[...] + back).astype(BF16)

            accumulate(rows_ref.at[0:1], grad_gain, first_row())
            rows_ref[1:2, :] = gain1_ref[...]
            rows_ref[2:3, :] = gain2_ref[...]
            rows_ref[3:, :] = jnp.zeros((13, model), F32)

        kept["dx"], kept["gains"] = c.run(input_back, "input_back")

    self_counts = [2 * width, 2 * width + 16]

    def self_grads(i):
        terms = [([kept["dqkv"][i]], [a0]), ([att[i]], [kept["g1_low"]])]
        return products(terms, [kept["gains"]], self_counts, "self_grads")


    families = {
        "dn": (["D1", "D2"], down_grads),
        "ga": (["G"], lambda i: gate_up(i, 0)),
        "up": (["U"], lambda i: gate_up(i, 1)),
        "sd": (["S"], side_grads),
        "q": (["Q1", "Q2"], self_grads),
    }

    def ffn_out_step():
        values = [sums[name].finish() for name in ("G", "U", "D1", "D2")]
        c = Call(1, length, order)
        c.whole(*values)
        c.out_whole((3, model, hidden_width), F32)

        def ffn_out(*refs):
            *ins, out_ref = refs
            half = hidden_width // 2
            for k in range(2):
                out_ref[k] = ins[k][...].astype(F32).T
                out_ref[2, :, k * half : (k + 1) * half] = ins[2 + k][...].astype(F32).T

        kept["ffn"] = c.run(ffn_out, "ffn_out")[0]

    def output_step():
        kept["out"] = decoder_output(kept["last"])

    def down_step():
        kept["last"] = decoder_down()

    def send_dkv():
        kept["dkv"] = lax.ppermute(order.place(dkv), "section", [(1, 0)])

    def spread_out(name):
        kept[name + "_rows"] = from_rows(order.place(kept[name]))

    single = {
        "yk": send_dkv,
        "fo": lambda: spread_out("out"),
        "fd": lambda: spread_out("dx"),
        "fb": ffn_back_step,
        "sb": lambda: self_back(0),
        "sb2": lambda: self_back(1) if groups == 2 else None,
        "ib": input_back_step,
        "dd": down_step,
        "out": output_step,
        "ffo": ffn_out_step,
    }
    for step in ORDER:
        kind, _, what = step.partition(":")
        if what:
            if kind == "X":
                sums[what].send()
            else:
                sums[what].step()
        elif kind in single:
            single[kind]()
        else:
            family, _, whose = kind.partition("_")
            names, grads = families[family]
            if whose == "w":
                add_products(names, grads(0), True)
            elif groups == 2:
                add_products(names, grads(1), False)
    if "fo" not in ORDER:
        spread_out("out")
    if "fd" not in ORDER:
        spread_out("dx")
    if OPT["attn_out"]:
        total = {name: sums[name].finish() for name in ("Q1", "Q2", "S")}
        gain_total = total["Q2"][2 * width : 2 * width + 3].astype(F32)
        c = Call(1, length, order)
        c.whole(total["Q1"], total["Q2"], total["S"])
        c.out_whole((6 * width, model), F32)

        def attn_out(first_ref, second_ref, side_ref, out_ref):
            for k, ref in enumerate((first_ref, second_ref, side_ref)):
                at = 2 * width * k
                out_ref[at : at + 2 * width, :] = ref[: 2 * width, :].astype(F32)

        attn_grad = c.run(attn_out, "attn_out")[0]
    else:
        total = {name: one.finish() for name, one in sums.items()}
        t_self = jnp.concatenate([total["Q1"], total["Q2"]], 0)

        attn_grad = jnp.concatenate([t_self[: 4 * width], total["S"]], 0).astype(F32)
        gain_total = t_self[4 * width : 4 * width + 3].astype(F32)
    attn_grad = attn_grad.reshape(6, width, model).transpose(0, 2, 1)
    return (
        kept["out_rows"][None],
        kept["dx_rows"][None],
        gain_total[None],
        attn_grad[None],
        kept["ffn"][None],
    )


def solution(mesh):
    in_specs = (
        P("section", "dp", "tensor", None),
        P("dp"),
        P("dp", "tensor", None),
        P("section", None, None),
        P("section", None, None, "tensor"),
        P("section", None, None, "tensor"),
    )
    out_specs = (
        P("section", "dp", "tensor", None),
        P("section", "dp", "tensor", None),
        P("section", None, None),
        P("section", None, None, "tensor"),
        P("section", None, None, "tensor"),
    )
    return jax.shard_map(
        on_device, mesh=mesh, in_specs=in_specs, out_specs=out_specs, check_vma=False
    )
```

```python
from types import SimpleNamespace
import jax
import jax.numpy as jnp
from jax import lax
from jax.experimental import pallas as pl
from jax.experimental.pallas import tpu as pltpu
from jax.sharding import PartitionSpec as P
DH = 64
EPSILON = 1e-06
NEGATIVE = -1e+30
F32 = jnp.float32
BF16 = jnp.bfloat16
VMEM = 16 * 1024 * 1024
NN = (((1,), (0,)), ((), ()))
NT = (((1,), (1,)), ((), ()))
TN = (((0,), (0,)), ((), ()))

def mm(left, right, dims=NN):
    return lax.dot_general(left, right, dims, preferred_element_type=F32)

def factor_of(v):
    return lax.rsqrt(jnp.mean(v * v, axis=-1, keepdims=True) + EPSILON)

def normed(v, gain):
    return (v * factor_of(v) * gain).astype(BF16)

def normed_back(v, gain, u):
    factor = factor_of(v)
    scaled = u * gain
    grad_gain = jnp.sum(u * v * factor, axis=0, keepdims=True)
    inner = jnp.mean(scaled * v, axis=-1, keepdims=True)
    return (factor * scaled - v * (factor * factor * factor * inner), grad_gain)

def gelu_parts(v):
    c = 0.7978845608028654
    square = v * v
    t = jnp.tanh(v * (c + c * 0.044715 * square))
    half = 0.5 + 0.5 * t
    slope = half + v * (half * (1.0 - t)) * (c + 3.0 * c * 0.044715 * square)
    return (v * half, slope)

def causal_mask(enc, length):
    key_pos = lax.broadcasted_iota(jnp.int32, (length, length), 0)
    query_pos = lax.broadcasted_iota(jnp.int32, (length, length), 1)
    return key_pos <= query_pos + enc * length

def scores(q, k, allowed):
    s = mm(k, q, NT)
    return s if allowed is None else jnp.where(allowed, s, NEGATIVE)

def attend(q_ref, q0, kv_ref, k0, v0, out_ref, lse_ref, allowed, width):
    for h in range(width // DH):
        lo = h * DH
        q = q_ref[:, q0 + lo:q0 + lo + DH] * BF16(DH ** (-0.5))
        k = kv_ref[:, k0 + lo:k0 + lo + DH]
        v = kv_ref[:, v0 + lo:v0 + lo + DH]
        s = scores(q, k, allowed)
        top = jnp.max(s, axis=0, keepdims=True)
        e = jnp.exp(s - top)
        total = jnp.sum(e, axis=0, keepdims=True)
        o = mm(v.T, e.astype(BF16)) * (1.0 / total)
        out_ref[:, lo:lo + DH] = o.T.astype(BF16)
        lse_ref[h:h + 1, :] = top + jnp.log(total)

def attend_back(q_ref, q0, kv_ref, k0, v0, lse_ref, grad, dq_ref, dkv_ref, allowed, width):
    for h in range(width // DH):
        lo = h * DH
        q = q_ref[:, q0 + lo:q0 + lo + DH] * BF16(DH ** (-0.5))
        k = kv_ref[:, k0 + lo:k0 + lo + DH]
        v = kv_ref[:, v0 + lo:v0 + lo + DH]
        g = grad[:, lo:lo + DH]
        p = jnp.exp(scores(q, k, allowed) - lse_ref[h:h + 1, :])
        dp = mm(v, g, NT)
        delta = jnp.sum(p * dp, axis=0, keepdims=True)
        ds = (p * (dp - delta)).astype(BF16)
        dkv_ref[:, v0 + lo:v0 + lo + DH] = mm(p.astype(BF16), g).astype(BF16)
        dkv_ref[:, k0 + lo:k0 + lo + DH] = mm(ds, q).astype(BF16)
        dq = mm(k.T, ds) * DH ** (-0.5)
        dq_ref[:, q0 + lo:q0 + lo + DH] = dq.T.astype(BF16)

def ffn_back(a, g, weights, dgate_refs, dup_refs):
    part = None
    for (wg, wu, wd), dgate_ref, dup_ref in zip(weights, dgate_refs, dup_refs):
        value, slope = gelu_parts(mm(a, wg[...]))
        up = mm(a, wu[...])
        dh = mm(g, wd[...])
        dgate_ref[...] = (dh * up * slope).astype(BF16)
        dup_ref[...] = (dh * value).astype(BF16)
        here = mm(dgate_ref[...], wg[...], NT) + mm(dup_ref[...], wu[...], NT)
        part = here if part is None else part + here
    return part

def ffn_both(a, g, weights, hid_refs, dgate_refs, dup_refs):
    part = None
    for (wg, wu, wd), hid_ref, dgate_ref, dup_ref in zip(weights, hid_refs, dgate_refs, dup_refs):
        gate = mm(a, wg[...])
        up = mm(a, wu[...])
        dh = mm(g, wd[...])
        value, slope = gelu_parts(gate)
        hid_ref[...] = (value * up).astype(BF16)
        dgate_ref[...] = (dh * up * slope).astype(BF16)
        dup_ref[...] = (dh * value).astype(BF16)
        here = mm(dgate_ref[...], wg[...], NT) + mm(dup_ref[...], wu[...], NT)
        part = here if part is None else part + here
    return part

def after(value, *others):
    return lax.optimization_barrier((value,) + others)[0]
LAG = {'X': 2, 'A': 2, 'B': 2, 'R': 2}

class Order:

    def __init__(self):
        self.tokens = []

    def place(self, value):
        return after(value, *self.tokens) if self.tokens else value

    def done(self, value):
        self.tokens = [value]

    def need(self, *values):
        self.tokens = self.tokens + list(values)
COST = pl.CostEstimate(flops=1, bytes_accessed=1, transcendentals=0)
SMEM_SPEC = pl.BlockSpec(memory_space=pltpu.SMEM)

def whole_spec(spec):
    return spec if spec is SMEM_SPEC else pl.BlockSpec(memory_space=pltpu.VMEM)

class Call:

    def __init__(self, rows, length, order):
        self.rows, self.length, self.order = (rows, length, order)
        self.specs, self.args, self.out_specs, self.out_shapes = ([], [], [], [])
        self.in_views, self.out_views = ([], [])

    @property
    def views(self):
        return self.in_views + self.out_views

    def scalar(self, value):
        self.specs.append(SMEM_SPEC)
        self.args.append(value)
        self.in_views.append(None)

    def tokens(self, *values):
        for value in values:
            count = value.shape[0] // self.rows
            self.specs.append(pl.BlockSpec((count, value.shape[1]), lambda i: (i, 0)))
            self.args.append(value)
            self.in_views.append(None)

    def heads(self, *values):
        for value in values:
            self.specs.append(pl.BlockSpec((None,) + value.shape[1:], lambda i: (i, 0, 0)))
            self.args.append(value)
            self.in_views.append(0)

    def whole(self, *values):
        for value in values:
            block = None
            if isinstance(value, tuple):
                value, block, at = value
            if block is None:
                block, at = (value.shape, (0,) * value.ndim)
            self.specs.append(pl.BlockSpec(block, lambda i, at=at: at))
            self.args.append(value)
            view = tuple((k if size is None else pl.ds(k * size, size) for k, size in zip(at, block)))
            self.in_views.append(None if block == value.shape else view)

    def out_tokens(self, width, kind, count=None):
        count = self.length if count is None else count
        self.out_views.append(None)
        self.out_specs.append(pl.BlockSpec((count, width), lambda i: (i, 0)))
        self.out_shapes.append(jax.ShapeDtypeStruct((self.rows * count, width), kind))

    def out_heads(self, heads):
        self.out_views.append(0)
        self.out_specs.append(pl.BlockSpec((None, heads, self.length), lambda i: (i, 0, 0)))
        self.out_shapes.append(jax.ShapeDtypeStruct((self.rows, heads, self.length), F32))

    def out_whole(self, shape, kind):
        self.out_views.append(None)
        self.out_specs.append(pl.BlockSpec(shape, lambda i, n=len(shape): (0,) * n))
        self.out_shapes.append(jax.ShapeDtypeStruct(shape, kind))

    def narrowed(self, kernel):
        views = list(self.views)

        def inner(*refs):
            kernel(*[ref if view is None else ref.at[view] for ref, view in zip(refs, views)])
        return inner

    def run(self, kernel, name):
        first = next((k for k, v in enumerate(self.args) if v.dtype != jnp.int32))
        self.args[first] = self.order.place(self.args[first])
        more = {'grid': (self.rows,)}
        if self.rows == 1:
            more = {}
            self.specs = [whole_spec(spec) for spec in self.specs]
            self.out_specs = [whole_spec(spec) for spec in self.out_specs]
            kernel = self.narrowed(kernel)
        out = pl.pallas_call(kernel, in_specs=self.specs, out_specs=self.out_specs, out_shape=self.out_shapes, **more, compiler_params=pltpu.CompilerParams(vmem_limit_bytes=VMEM), cost_estimate=COST, name=name)(*self.args)
        self.order.done(out[0])
        return out

def accumulate(ref, value, first):
    if first is True:
        ref[...] = value
        return

    @pl.when(first)
    def _():
        ref[...] = value

    @pl.when(jnp.logical_not(first))
    def _():
        ref[...] += value

def on_device(layer_input, dec_lengths, out_cotangent, gains, attn_weights, ffn_weights):
    tensor = lax.axis_size('tensor')
    planes = lax.axis_size('dp')
    batch, part_len, model = layer_input.shape[1:]
    groups = 2 if tensor % 2 == 0 and batch % 2 == 0 else 1
    cores = tensor // groups
    rows = batch // groups
    length = part_len * tensor
    tokens = rows * length
    share = length // cores
    width = attn_weights.shape[3]
    hidden_width = ffn_weights.shape[3]
    heads = width // DH
    shares = range(groups)
    section = lax.axis_index('section')
    plane = lax.axis_index('dp')
    lane = lax.axis_index('tensor')
    group = lane // cores
    core = lane % cores
    is_enc = section == 0
    outer = (plane == 0) | (plane == planes - 1)
    place = jnp.stack([v.astype(jnp.int32) for v in (is_enc, core, outer, plane % 2, group)])
    group_route = [(t, (t + cores) % tensor) for t in range(tensor)]
    core_groups = [[g * cores + c for c in range(cores)] for g in range(groups)]
    next_plane = [(p, p ^ 1) for p in range(planes)]
    order = Order()

    def over_groups(value):
        return lax.ppermute(value, 'tensor', group_route)

    def decoder_only(value, axis, route):
        size = lax.axis_size(axis)
        return lax.ppermute(value, ('section', axis), [(size + a, size + b) for a, b in route])

    def encoder_only(value, axis, route):
        return lax.ppermute(value, ('section', axis), route)

    def core_route(step):
        return [(g * cores + (c + step) % cores, g * cores + c) for g in range(groups) for c in range(cores)]

    def core_swap(value):
        return [lax.ppermute(value, 'tensor', core_route(k)) for k in range(1, cores)]

    def core_sum(part):
        if cores <= 2:
            return [part] + core_swap(part)
        return [lax.psum(part, 'tensor', axis_index_groups=core_groups)]

    def pick(value, index, count):
        return lax.dynamic_slice_in_dim(value, index * count, count, 0)

    def move(value, axis, route, decoder):
        return decoder_only(value, axis, route) if decoder else lax.ppermute(value, axis, route)
    queues = {}

    def queued(link, value, transfer):
        lag = LAG.get(link, 0)
        line = queues.setdefault(link, [])
        if lag and len(line) >= lag:
            value = after(value, line[-lag])
        got = transfer(value)
        line.append(got)
        return got

    class Fetch:

        def __init__(self, own, at, count, *behind, assisted=True):
            self.halved = assisted and planes % 2 == 0 and (count % 32 == 0)
            if self.halved:
                count //= 2
                at = at + plane % 2 * count
            value = lax.dynamic_slice_in_dim(own, at, count, 0)
            if behind:
                value = after(value, *behind)
            self.direct = queued('X0', value, over_groups)

        def forward(self, placed=True):
            if self.halved:
                if placed:
                    self.direct = order.place(self.direct)
                    order.need(self.direct)
                self.passed = queued('Z0', self.direct, lambda v: lax.ppermute(v, 'dp', next_plane))

        def arrived(self):
            return self.passed if self.halved else self.direct

        def parts(self):
            return [self.direct, self.passed] if self.halved else [self.direct]

    def assemble(place_ref, refs, out_ref, halved):
        if len(refs) == 1:
            out_ref[...] = refs[0][...]
            return
        half = refs[0].shape[0]
        first = place_ref[3] * half if halved else 0
        second = half - first
        out_ref[pl.ds(pl.multiple_of(first, half), half), :] = refs[0][...]
        out_ref[pl.ds(pl.multiple_of(second, half), half), :] = refs[1][...]

    def to_rows(value, route_group, placed=False):
        if groups == 1:
            blocks = value[:, None]
        else:
            mine = pick(value, group, rows)
            got = early_cot if placed else route_group(pick(value, 1 - group, rows))
            if placed:
                got = order.place(got)
            first = group == 0
            blocks = jnp.stack([jnp.where(first, mine, got), jnp.where(first, got, mine)], 1)
        if cores == 2:
            got = core_swap(blocks)[0]
            low = core == 0
            blocks = jnp.stack([jnp.where(low, blocks, got), jnp.where(low, got, blocks)], 2)
        elif cores > 2:
            blocks = lax.all_gather(blocks, 'tensor', axis=2, axis_index_groups=core_groups)
        return blocks.reshape(tokens, model)

    def from_rows(value):
        blocks = value.reshape(rows, tensor, part_len, model)
        mine = lax.dynamic_index_in_dim(blocks, lane, 1, keepdims=False)
        if groups == 1:
            return mine
        got = over_groups(lax.dynamic_index_in_dim(blocks, (lane + cores) % tensor, 1, keepdims=False))
        first = group == 0
        return jnp.concatenate([jnp.where(first, mine, got), jnp.where(first, got, mine)], 0)

    def split(refs, *counts):
        at, out = (0, [])
        for count in counts:
            out.append(refs[at:at + count])
            at += count
        return out

    def call():
        return Call(rows, length, order)

    def first_row():
        return True if rows == 1 else pl.program_id(0) == 0
    attn_t = attn_weights[0].transpose(0, 2, 1).reshape(6 * width, model)
    ffn = ffn_weights[0]
    gain = gains[0]
    own_self = (attn_t, (4 * width, model), (0, 0))
    own_side = (attn_t, (2 * width, model), (2, 0))
    own_ffn = [(ffn, (None, model, hidden_width), (j, 0, 0)) for j in range(3)]
    w_self, w_ffn, w_dec, w_side = ([own_self], [own_ffn], [own_ffn], [own_side])
    x_parts = [pick(layer_input[0], group, rows)]
    if groups == 2:
        x_parts.append(queued('X0', pick(layer_input[0], 1 - group, rows), over_groups))
        flat = ffn.reshape(3 * model, hidden_width)
        behind = {'none': [], 'in': [x_parts[1]], 'slice': [pick(layer_input[0], 1 - group, rows)]}
        far_self = Fetch(attn_t, 0, 4 * width, *behind['slice'], assisted=True)
        far_pair = [Fetch(flat, 0, model, x_parts[1])]
        far_pair.append(Fetch(flat, model, model, x_parts[1]))
        half = model // 2
        far_down = [ffn[2, :half], ffn[2, half:]]
        far_down[0] = after(far_down[0], far_pair[0].direct)
        far_down[1] = after(far_down[1], far_pair[0].direct)
        far_down = [queued('X0', v, lambda v: encoder_only(v, 'tensor', group_route)) for v in far_down]
    side_out = attn_t[4 * width:]
    side_out = after(side_out, x_parts[1])
    enc_side = lax.ppermute(side_out, 'section', [(0, 1)])
    x_parts = x_parts + [v for part in zip(*[core_swap(v) for v in x_parts]) for v in part]
    c = call()
    c.scalar(place)
    c.heads(*x_parts)
    c.whole(gain[0:1])
    c.out_tokens(model, BF16)
    c.out_tokens(model, BF16)

    def first_norm(place_ref, *refs):
        gain_ref, x_ref, a_ref = refs[-3:]
        for k, ref in enumerate(refs[:-3]):
            from_core = lax.rem(place_ref[1] + k // groups, cores)
            from_group = lax.rem(place_ref[4] + k % groups, groups)
            at = (from_group * cores + from_core) * part_len
            x_ref[pl.ds(pl.multiple_of(at, part_len), part_len), :] = ref[...]
        a_ref[...] = normed(x_ref[...].astype(F32), gain_ref[...])
    if groups == 2:
        far_self.forward(False)
        order.need(far_self.direct)
    x, a0 = c.run(first_norm, 'first_norm')
    cot = to_rows(out_cotangent, lambda v: decoder_only(v, 'tensor', group_route))
    row_ids = group * rows + jnp.arange(rows)
    live = jnp.arange(length)[None, :] < dec_lengths[row_ids][:, None]
    live = live.reshape(tokens, 1)
    gy = jnp.where(live, cot, BF16(0))
    early_cot = None

    def self_forward(i, part):
        pieces = far_self.parts() if i == 1 else [w_self[i]]
        made = i == 1 and len(pieces) > 1
        if i == 1 and (not made):
            w_self.append(pieces[0])
        c = call()
        c.scalar(place)
        c.tokens(a0)
        c.whole(*pieces)
        if part is not None:
            c.tokens(part)
        c.out_tokens(3 * width, BF16)
        c.out_tokens(width, BF16)
        c.out_heads(heads)
        c.out_tokens(model, BF16 if i == groups - 1 else F32)
        if made:
            c.out_whole((4 * width, model), BF16)

        def kernel(place_ref, a_ref, *refs):
            qkv_ref, att_ref, lse_ref, part_ref = refs[-5:-1] if made else refs[-4:]
            w_ref = refs[0]
            if made:
                w_ref = refs[-1]
                assemble(place_ref, refs[:len(pieces)], w_ref, far_self.halved)
            qkv_ref[...] = mm(a_ref[...], w_ref[:3 * width, :], NT).astype(BF16)
            allowed = causal_mask(place_ref[0], length)
            attend(qkv_ref, 0, qkv_ref, width, 2 * width, att_ref, lse_ref, allowed, width)
            out = mm(att_ref[...], w_ref[3 * width:, :])
            if part is not None:
                out = out + refs[len(pieces)][...]
            part_ref[...] = out.astype(part_ref.dtype)
        return c.run(kernel, 'self_forward')
    qkv, att, lse, part = ([], [], [], None)
    for i in shares:
        if i == 1:
            order.need(enc_side)
            order.need(gy)
            far_pair[0].forward()
            far_pair[1].forward()
        a, b, l, part, *rest = self_forward(i, part)
        w_self += rest
        qkv.append(a)
        att.append(b)
        lse.append(l)
    if groups == 2:
        pins = [] + [far_pair[0].arrived()] + []
        if pins:
            part = after(part, *pins)
    parts = core_sum(part)

    def total_of(refs):
        value = refs[0][...].astype(F32)
        for ref in refs[1:]:
            value = value + ref[...].astype(F32)
        return value

    def ffn_share(a, wg, wu, wd, hid_ref):
        value, _ = gelu_parts(mm(a, wg[...]))
        hid_ref[...] = (value * mm(a, wu[...])).astype(BF16)
        return mm(hid_ref[...], wd[...], NT)
    c = call()
    c.tokens(x, *parts)
    c.whole(gain[1:2], *w_ffn[0])
    c.out_tokens(model, F32)
    c.out_tokens(model, BF16)
    c.out_tokens(hidden_width, BF16)
    c.out_tokens(model, BF16 if groups == 1 else F32)

    def ffn_first(x_ref, *refs):
        count = len(parts)
        gain_ref, wg, wu, wd, x1_ref, a1_ref, hid_ref, part_ref = refs[count:]
        x1 = x_ref[...].astype(F32) + total_of(refs[:count])
        x1_ref[...] = x1
        a1_ref[...] = normed(x1, gain_ref[...])
        part_ref[...] = ffn_share(a1_ref[...], wg, wu, wd, hid_ref).astype(part_ref.dtype)
    x1, a1, hid, part = c.run(ffn_first, 'ffn_first')
    e_hid = [hid]
    if groups == 2:
        both_sides = decoder_only(jnp.concatenate([attn_t[4 * width:], enc_side], 0), 'tensor', group_route)
        pieces = [fetch.parts() for fetch in far_pair]
        c = call()
        c.scalar(place)
        c.tokens(a1, part)
        c.whole(*[v for got in pieces for v in got], *far_down)
        c.out_tokens(model, BF16)
        c.out_tokens(hidden_width, BF16)
        c.out_whole((2 * model, hidden_width), BF16)
        c.out_whole((model, hidden_width), BF16)

        def ffn_second(place_ref, a_ref, prev_ref, *refs):
            *piece_refs, down_refs, (part_ref, hid_ref, pair_ref, wd) = split(refs, *[len(got) for got in pieces], 2, 4)
            for k in range(2):
                w = pair_ref.at[k * model:(k + 1) * model]
                assemble(place_ref, piece_refs[k], w, far_pair[k].halved)
            for k, ref in enumerate(down_refs):
                wd[k * half:(k + 1) * half, :] = ref[...]
            ws = (pair_ref.at[:model], pair_ref.at[model:], wd)
            part_ref[...] = (prev_ref[...] + ffn_share(a_ref[...], *ws, hid_ref)).astype(BF16)
        part, hid, pair, far_down = c.run(ffn_second, 'ffn_second')
        far = [(pair, (model, hidden_width), (k, 0)) for k in range(2)]
        dec_far = decoder_only(ffn[2], 'tensor', group_route)
        w_dec = [own_ffn, far + [dec_far]]
        w_ffn.append(far + [far_down])
        e_hid.append(hid)
        part = after(part, both_sides)
    parts = core_sum(part)
    c = call()
    c.scalar(place)
    c.tokens(x1, *parts)
    c.whole(gain[2:3])
    c.out_tokens(model, F32)
    c.out_tokens(model, BF16)
    c.out_tokens(model, BF16, share)

    def memory_kernel(place_ref, x1_ref, *refs):
        gain_ref, y_ref, memory_ref, mine_ref = refs[-4:]
        y = x1_ref[...] + total_of(refs[:-4])
        y_ref[...] = y
        memory_ref[...] = normed(y, gain_ref[...])
        start = pl.multiple_of(place_ref[1] * share, share)
        mine_ref[...] = memory_ref[pl.ds(start, share), :]
    if groups == 2:
        both_sides = [(both_sides, (2 * width, model), (k, 0)) for k in range(2)]
    y, memory, mem_mine = c.run(memory_kernel, 'memory')
    mem_mine = lax.ppermute(mem_mine, 'section', [(0, 1)])
    mem = [mem_mine] + core_swap(mem_mine)
    w_side, w_enc = ([own_side], [enc_side])
    if groups == 2:
        w_side.append(both_sides[0])
        w_enc.append(both_sides[1])
    c = call()
    c.scalar(place)
    c.tokens(a1, *mem)
    c.whole(*w_side, *w_enc)
    for i in shares:
        c.out_tokens(width, BF16)
    for i in shares:
        c.out_tokens(2 * width, BF16)
    for i in shares:
        c.out_tokens(width, BF16)
    for i in shares:
        c.out_heads(heads)
    c.out_tokens(model, BF16)

    def cross_forward(place_ref, a_ref, *refs):
        mem_refs, side, enc, cq, kv, catt, clse, (part_ref,) = split(refs, cores, groups, groups, groups, groups, groups, groups, 1)
        out = None
        for i in shares:
            cq[i][...] = mm(a_ref[...], side[i][:width, :], NT).astype(BF16)
            for j, ref in enumerate(mem_refs):
                kv[i][j * share:(j + 1) * share, :] = mm(ref[...], enc[i][...], NT).astype(BF16)
            attend(cq[i], 0, kv[i], 0, width, catt[i], clse[i], None, width)
            here = mm(catt[i][...], side[i][width:, :])
            out = here if out is None else out + here
        part_ref[...] = out.astype(BF16)
    cq, kv, catt, clse, (part,) = split(c.run(cross_forward, 'cross_forward'), groups, groups, groups, groups, 1)
    if groups == 2:
        part = after(part, dec_far)
    parts = core_sum(part)
    c = call()
    c.tokens(x1, gy, *parts)
    c.whole(gain[2:3], *[w for ws in w_dec for w in ws])
    c.out_tokens(model, F32)
    c.out_tokens(model, BF16)
    for _ in range(3 * groups):
        c.out_tokens(hidden_width, BF16)
    c.out_tokens(model, BF16)

    def triples(refs):
        return [refs[3 * i:3 * i + 3] for i in shares]

    def dec_ffn(x1_ref, gy_ref, *refs):
        part_refs, (gain_ref,), ws, (x2_ref, a2_ref), hid, dgate, dup, (part_ref,) = split(refs, len(parts), 1, 3 * groups, 2, groups, groups, groups, 1)
        x2 = x1_ref[...] + total_of(part_refs)
        x2_ref[...] = x2
        a2_ref[...] = normed(x2, gain_ref[...])
        part_ref[...] = ffn_both(a2_ref[...], gy_ref[...], triples(ws), hid, dgate, dup).astype(BF16)
    (x2, a2), d_hid, d_gate, d_up, (part,) = split(c.run(dec_ffn, 'dec_ffn'), 2, groups, groups, groups, 1)
    parts = core_sum(part)
    c = call()
    c.tokens(x2, gy, *parts, *cq, *kv)
    c.heads(*clse)
    c.whole(gain[2:3], *w_side, *w_enc)
    c.out_tokens(model, F32)
    c.out_tokens(model, BF16)
    c.out_whole((1, model), F32)
    for i in shares:
        c.out_tokens(width, BF16)
    c.out_tokens(2 * width * groups, BF16)
    c.out_tokens(model, BF16)
    for j in range(cores):
        c.out_tokens(model, F32 if j == 0 else BF16, share)

    def cross_back(x2_ref, gy_ref, *refs):
        part_refs, cq_refs, kv_refs, lse_refs, (gain_ref,), side, enc, (g2_ref, low_ref, gain2_ref), dcq_refs, (dkv_ref, part_ref), mem_refs = split(refs, len(parts), groups, groups, groups, 1, groups, groups, 3, groups, 2, cores)
        dkv_refs = [dkv_ref.at[:, 2 * width * i:2 * width * (i + 1)] for i in shares]
        back, grad_gain = normed_back(x2_ref[...], gain_ref[...], total_of(part_refs))
        accumulate(gain2_ref, grad_gain, first_row())
        g2 = gy_ref[...].astype(F32) + back
        g2_ref[...] = g2
        low_ref[...] = g2.astype(BF16)
        out = None
        for i in shares:
            grad = mm(low_ref[...], side[i][width:, :], NT).astype(BF16)
            attend_back(cq_refs[i], 0, kv_refs[i], 0, width, lse_refs[i], grad, dcq_refs[i], dkv_refs[i], None, width)
            here = mm(dcq_refs[i][...], side[i][:width, :])
            out = here if out is None else out + here
        part_ref[...] = out.astype(BF16)
        for j, ref in enumerate(mem_refs):
            total = None
            for i in shares:
                here = mm(dkv_refs[i][j * share:(j + 1) * share, :], enc[i][...])
                total = here if total is None else total + here
            ref[...] = total.astype(ref.dtype)
    (g2, g2_low, dec_gain2), dcq, (dkv, part_dec), dmem = split(c.run(cross_back, 'cross_back'), 3, groups, 2, cores)
    mine = dmem[0]
    for step in range(1, cores):
        mine = mine + lax.ppermute(dmem[step], 'tensor', core_route(cores - step)).astype(F32)
    mine = mine.astype(BF16)
    order.done(mine)
    mine = lax.ppermute(mine, 'section', [(1, 0)])
    dmem = [mine] + core_swap(mine)
    kept = SimpleNamespace(dqkv=[])
    kept.dkv = lax.ppermute(dkv, 'section', [(1, 0)])
    chunk = 4 * width // 3

    def products(terms, tails, counts, name):
        sizes = [[len(values) for values in term] for term in terms]
        flat = [v for term in terms for values in term for v in values] + tails
        flat[0] = order.place(flat[0])

        def product(left_refs, right_refs):
            total = None
            for j, right in enumerate(right_refs):
                spans = [(left_refs[j][...], right[...])]
                for left, value in spans:
                    here = mm(left, value, TN)
                    total = here if total is None else total + here
            return total

        def kernel(place_ref, *refs):
            outs = refs[len(flat):]
            starts = [sum(counts[:k]) for k in range(len(counts))]

            def store(value, at):
                done = 0
                while done < value.shape[0]:
                    k = max((q for q in range(len(counts)) if starts[q] <= at + done))
                    inside = at + done - starts[k]
                    count = min(value.shape[0] - done, counts[k] - inside)
                    outs[k][inside:inside + count, :] = value[done:done + count].astype(BF16)
                    done += count
            used, at = (0, 0)
            for size in sizes:
                values = split(refs[used:], *size)
                used += sum(size)
                if len(size) == 2:
                    store(product(*values), at)
                else:

                    @pl.when(place_ref[0] == 1)
                    def _(values=values, at=at):
                        store(product(*values[:2]), at)

                    @pl.when(place_ref[0] == 0)
                    def _(values=values, at=at):
                        store(product(*values[2:]), at)
                at += values[0][0].shape[1]
            for tail in refs[used:len(flat)]:
                store(tail[...], at)
                at += tail.shape[0]
        out = pl.pallas_call(kernel, in_specs=[SMEM_SPEC] + [pl.BlockSpec(memory_space=pltpu.VMEM)] * len(flat), out_shape=[jax.ShapeDtypeStruct((count, model), BF16) for count in counts], compiler_params=pltpu.CompilerParams(vmem_limit_bytes=VMEM), cost_estimate=COST, name=name)(place, *flat)
        order.done(out[-1])
        return list(out)

    def add_kernel(value, got):

        def kernel(value_ref, got_ref, out_ref):
            total = value_ref[...].astype(F32) + got_ref[...].astype(F32)
            out_ref[...] = total.astype(BF16)
        c = Call(1, length, order)
        c.whole(value, got)
        c.out_whole(value.shape, BF16)
        return c.run(kernel, 'sum_step')[0]

    class Sum:

        def __init__(self):
            self.got, self.at = (None, 0)
            half = planes // 2
            self.moves = [('group', group_route)] if groups == 2 else []
            if planes % 2 == 0:
                for k in range(half - 1):
                    self.moves.append(('add', [(k, k + 1), (planes - 1 - k, planes - 2 - k)]))
                self.moves.append(('add', [(half - 1, half), (half, half - 1)]))
                for k in range(half - 1):
                    left, right = (half - 1 - k, half + k)
                    self.moves.append(('take', [(left, left - 1), (right, right + 1)]))

        def send(self):
            if groups == 2:
                self.got = queued('X', self.other, over_groups)

        def step(self):
            if self.at == len(self.moves):
                return
            kind, route = self.moves[self.at]
            if self.got is None:
                self.got = lax.ppermute(self.value, 'dp', route)
            names = 'XABR' if groups == 2 and planes == 4 else 'X' * 100
            last = self.at == len(self.moves) - 1
            if last and kind == 'take':
                got = self.got
                order.need(got)
            else:
                got = order.place(self.got)
            if kind == 'take':
                targets = [b for _, b in route]
                self.value = jnp.where((plane == targets[0]) | (plane == targets[1]), got, self.value)
            else:
                self.value = add_kernel(self.value, got)
            if not (last and kind == 'take'):
                order.done(self.value)
            self.at += 1
            if not last:
                route = self.moves[self.at][1]
                self.got = queued(names[self.at], self.value, lambda v: lax.ppermute(v, 'dp', route))

        def finish(self):
            while self.at < len(self.moves):
                self.step()
            if planes % 2 and planes > 1:
                self.value = lax.psum(self.value, 'dp')
            return self.value
    sum_d1, sum_d2, sum_g, sum_u, sum_s, sum_q1, sum_q2 = [Sum() for _ in range(7)]

    def side_grads(i):
        args = [order.place(memory), kept.dkv, dcq[i], a1, catt[i], g2_low]

        def kernel(place_ref, memory_ref, dkv_ref, dcq_ref, a1_ref, catt_ref, g2_ref, *out_refs):

            @pl.when(place_ref[0] == 1)
            def _():
                total = None
                for row in range(rows):
                    for j in range(cores):
                        at = row * length + lax.rem(place_ref[1] + j, cores) * share
                        right = memory_ref[pl.ds(pl.multiple_of(at, share), share), :]
                        start = row * length + j * share
                        left = dkv_ref[start:start + share, 2 * width * i:2 * width * (i + 1)]
                        here = mm(left, right, TN)
                        total = here if total is None else total + here
                out_refs[0][...] = total.astype(BF16)

            @pl.when(place_ref[0] == 0)
            def _():
                out_refs[0][:width, :] = mm(dcq_ref[...], a1_ref[...], TN).astype(BF16)
                out_refs[0][width:, :] = mm(catt_ref[...], g2_ref[...], TN).astype(BF16)
        out = pl.pallas_call(kernel, in_specs=[SMEM_SPEC] + [pl.BlockSpec(memory_space=pltpu.VMEM)] * len(args), out_shape=[jax.ShapeDtypeStruct((2 * width, model), BF16)], compiler_params=pltpu.CompilerParams(vmem_limit_bytes=VMEM), cost_estimate=COST, name='side_grads')(place, *args)
        order.done(out[-1])
        return out

    def decoder_down():
        c = call()
        c.tokens(*d_hid)
        c.whole(*[ws[2] for ws in w_dec])
        c.out_tokens(model, BF16)

        def dec_down(*refs):
            hid_refs, ws, (out_ref,) = split(refs, groups, groups, 1)
            total = None
            for hid_ref, w in zip(hid_refs, ws):
                here = mm(hid_ref[...], w[...], NT)
                total = here if total is None else total + here
            out_ref[...] = total.astype(BF16)
        return core_sum(c.run(dec_down, 'dec_down')[0])

    def decoder_output(last):
        c = call()
        c.scalar(place)
        c.tokens(memory, live.astype(F32), x2, *last)
        c.out_tokens(model, BF16)

        def output(place_ref, memory_ref, live_ref, x2_ref, *refs):
            total = (x2_ref[...] + total_of(refs[:-1])) * live_ref[...]
            refs[-1][...] = jnp.where(place_ref[0] == 1, memory_ref[...], total.astype(BF16))
        return c.run(output, 'output')[0]
    c = call()
    c.scalar(place)
    c.tokens(y, *dmem, gy, g2)
    c.whole(gain[2:3], dec_gain2)
    c.out_tokens(model, BF16)
    c.out_tokens(model, F32)
    c.out_whole((1, model), F32)

    def memory_back(place_ref, y_ref, *refs):
        dmem_refs, (gy_ref, g2_ref, gain_ref, old_gain, low_ref, g_ref, new_gain) = split(refs, cores, 7)

        @pl.when(place_ref[0] == 1)
        def _():
            for j, ref in enumerate(dmem_refs):
                at = lax.rem(place_ref[1] + j, cores)
                g_ref[pl.ds(pl.multiple_of(at * share, share), share), :] = ref[...].astype(F32)
            e_g, grad_gain = normed_back(y_ref[...], gain_ref[...], g_ref[...])
            accumulate(new_gain, grad_gain, first_row())
            g_ref[...] = e_g
            low_ref[...] = e_g.astype(BF16)

        @pl.when(place_ref[0] == 0)
        def _():
            low_ref[...] = gy_ref[...]
            g_ref[...] = g2_ref[...]
            new_gain[...] = old_gain[...]
    ffn_g, g_in, gain2 = c.run(memory_back, 'memory_back')

    def down_grads(i):
        terms = [([e_hid[i]], [ffn_g], [d_hid[i]], [ffn_g])]
        return products(terms, [], [hidden_width // 2] * 2, 'down_grads')
    kept.g_in = g_in

    def ffn_back_step():
        global_parts = encoder_ffn_back()
        kept.parts = core_sum(global_parts)

    def encoder_ffn_back():
        c = call()
        c.scalar(place)
        c.tokens(ffn_g, a1, part_dec)
        c.whole(*[w for ws in w_ffn for w in ws])
        c.out_tokens(model, BF16)
        for _ in range(2 * groups):
            c.out_tokens(hidden_width, BF16)

        def enc_ffn_back(place_ref, g_ref, a1_ref, old_part, *refs):
            ws, (part_ref,), dgate, dup = split(refs, 3 * groups, 1, groups, groups)

            @pl.when(place_ref[0] == 1)
            def _():
                part_ref[...] = ffn_back(a1_ref[...], g_ref[...], triples(ws), dgate, dup).astype(BF16)

            @pl.when(place_ref[0] == 0)
            def _():
                part_ref[...] = old_part[...]
        (part,), kept.gate, kept.up = split(c.run(enc_ffn_back, 'enc_ffn_back'), 1, groups, groups)

        def pair_grads(i):
            terms = [([e_gate[i]], [a1], [d_gate[i]], [a2]), ([e_up[i]], [a1], [d_up[i]], [a2])]
            return products(terms, [], [hidden_width] * 2, 'pair_grads')
        return part

    def gate_up(i, which):
        return products([([(kept.gate, kept.up)[which][i]], [a1], [(d_gate, d_up)[which][i]], [a2])], [], [hidden_width], 'pair_grads')

    def self_back(i):
        c = call()
        c.scalar(place)
        if i == 0:
            c.tokens(x1, kept.g_in, *kept.parts)
        else:
            c.tokens(kept.g1_low, kept.part)
        c.tokens(qkv[i])
        c.heads(lse[i])
        if i == 0:
            c.whole(gain[1:2])
        c.whole(w_self[i])
        if i == 0:
            c.out_tokens(model, F32)
            c.out_tokens(model, BF16)
            c.out_whole((1, model), F32)
        c.out_tokens(3 * width, BF16)
        c.out_tokens(model, BF16 if i == groups - 1 else F32)

        def kernel(place_ref, *refs):
            if i == 0:
                (x1_ref, g_ref), part_refs, (qkv_ref, lse_ref, gain_ref, w_ref), (g1_ref, low_ref, gain1_ref, d_ref, part_ref) = split(refs, 2, len(kept.parts), 4, 5)
                back, grad_gain = normed_back(x1_ref[...], gain_ref[...], total_of(part_refs))
                accumulate(gain1_ref, grad_gain, first_row())
                g1 = g_ref[...] + back
                g1_ref[...] = g1
                low_ref[...] = g1.astype(BF16)
            else:
                low_ref, prev_ref, qkv_ref, lse_ref, w_ref, d_ref, part_ref = refs
            allowed = causal_mask(place_ref[0], length)
            grad = mm(low_ref[...], w_ref[3 * width:, :], NT).astype(BF16)
            attend_back(qkv_ref, 0, qkv_ref, width, 2 * width, lse_ref, grad, d_ref, d_ref, allowed, width)
            out = mm(d_ref[...], w_ref[:3 * width, :])
            if i > 0:
                out = out + prev_ref[...]
            part_ref[...] = out.astype(part_ref.dtype)
        *first, d, kept.part = c.run(kernel, 'self_back')
        if i == 0:
            kept.g1, kept.g1_low, kept.gain1 = first
        kept.dqkv.append(d)
        if i == groups - 1:
            kept.parts = core_sum(kept.part)

    def input_back_step():
        c = call()
        c.tokens(x, kept.g1, *kept.parts)
        c.whole(gain[0:1], kept.gain1, gain2)
        c.out_tokens(model, BF16)
        c.out_whole((16, model), F32)

        def input_back(x_ref, g1_ref, *refs):
            gain_ref, gain1_ref, gain2_ref, dx_ref, rows_ref = refs[-5:]
            back, grad_gain = normed_back(x_ref[...].astype(F32), gain_ref[...], total_of(refs[:-5]))
            dx_ref[...] = (g1_ref[...] + back).astype(BF16)
            accumulate(rows_ref.at[0:1], grad_gain, first_row())
            rows_ref[1:2, :] = gain1_ref[...]
            rows_ref[2:3, :] = gain2_ref[...]
            rows_ref[3:, :] = jnp.zeros((13, model), F32)
        kept.dx, kept.gains = c.run(input_back, 'input_back')
    self_counts = [2 * width, 2 * width + 16]

    def self_grads(i):
        terms = [([kept.dqkv[i]], [a0]), ([att[i]], [kept.g1_low])]
        return products(terms, [kept.gains], self_counts, 'self_grads')

    def ffn_out_step():
        values = [one.finish() for one in (sum_g, sum_u, sum_d1, sum_d2)]
        c = Call(1, length, order)
        c.whole(*values)
        c.out_whole((3, model, hidden_width), F32)

        def ffn_out(*refs):
            *ins, out_ref = refs
            half = hidden_width // 2
            for k in range(2):
                out_ref[k] = ins[k][...].astype(F32).T
                out_ref[2, :, k * half:(k + 1) * half] = ins[2 + k][...].astype(F32).T
        return c.run(ffn_out, 'ffn_out')[0]
    if groups == 2:
        sum_d1.other, sum_d2.other = down_grads(1)
    sum_d1.send()
    sum_d2.send()
    sum_d1.value, sum_d2.value = down_grads(0)
    ffn_back_step()
    if groups == 2:
        [sum_g.other] = gate_up(1, 0)
    sum_g.send()
    [sum_g.value] = gate_up(0, 0)
    sum_d1.step()
    if groups == 2:
        [sum_u.other] = gate_up(1, 1)
    sum_u.send()
    sum_d2.step()
    [sum_u.value] = gate_up(0, 1)
    self_back(0)
    sum_d1.step()
    if groups == 2:
        self_back(1)
    sum_d2.step()
    sum_g.step()
    if groups == 2:
        [sum_s.other] = side_grads(1)
    sum_s.send()
    [sum_s.value] = side_grads(0)
    sum_d1.step()
    input_back_step()
    if groups == 2:
        sum_q1.other, sum_q2.other = self_grads(1)
    sum_q1.send()
    sum_q2.send()
    sum_q1.value, sum_q2.value = self_grads(0)
    sum_d2.step()
    sum_u.step()
    sum_g.step()
    sum_s.step()
    sum_d1.step()
    sum_u.step()
    sum_q1.step()
    sum_d2.step()
    sum_g.step()
    sum_s.step()
    sum_q2.step()
    sum_u.step()
    kept.last = decoder_down()
    sum_q1.step()
    sum_g.step()
    sum_s.step()
    sum_q2.step()
    sum_u.step()
    sum_q1.step()
    kept.out = decoder_output(kept.last)
    kept.ffn = ffn_out_step()
    sum_q2.step()
    out_rows = from_rows(order.place(kept.out))
    dx_rows = from_rows(order.place(kept.dx))
    first, second, side = [one.finish() for one in (sum_q1, sum_q2, sum_s)]
    gain_total = second[2 * width:2 * width + 3].astype(F32)
    c = Call(1, length, order)
    c.whole(first, second, side)
    c.out_whole((6 * width, model), F32)

    def attn_out(first_ref, second_ref, side_ref, out_ref):
        for k, ref in enumerate((first_ref, second_ref, side_ref)):
            at = 2 * width * k
            out_ref[at:at + 2 * width, :] = ref[:2 * width, :].astype(F32)
    attn_grad = c.run(attn_out, 'attn_out')[0]
    attn_grad = attn_grad.reshape(6, width, model).transpose(0, 2, 1)
    return (out_rows[None], dx_rows[None], gain_total[None], attn_grad[None], kept.ffn[None])

def solution(mesh):
    in_specs = (P('section', 'dp', 'tensor', None), P('dp'), P('dp', 'tensor', None), P('section', None, None), P('section', None, None, 'tensor'), P('section', None, None, 'tensor'))
    out_specs = (P('section', 'dp', 'tensor', None), P('section', 'dp', 'tensor', None), P('section', None, None), P('section', None, None, 'tensor'), P('section', None, None, 'tensor'))
    return jax.shard_map(on_device, mesh=mesh, in_specs=in_specs, out_specs=out_specs, check_vma=False)
```

```python
from types import SimpleNamespace
import jax
import jax.numpy as jnp
from jax import lax
from jax.experimental import pallas as pl
from jax.experimental.pallas import tpu as pltpu
from jax.sharding import PartitionSpec as P
DH = 64
EPSILON = 1e-06
NEGATIVE = -1e+30
F32 = jnp.float32
BF16 = jnp.bfloat16
VMEM = 16 * 1024 * 1024
NN = (((1,), (0,)), ((), ()))
NT = (((1,), (1,)), ((), ()))
TN = (((0,), (0,)), ((), ()))

def mm(left, right, dims=NN):
    return lax.dot_general(left, right, dims, preferred_element_type=F32)

def factor_of(v):
    return lax.rsqrt(jnp.mean(v * v, axis=-1, keepdims=True) + EPSILON)

def normed(v, gain):
    return (v * factor_of(v) * gain).astype(BF16)

def normed_back(v, gain, u):
    factor = factor_of(v)
    scaled = u * gain
    grad_gain = jnp.sum(u * v * factor, axis=0, keepdims=True)
    inner = jnp.mean(scaled * v, axis=-1, keepdims=True)
    return (factor * scaled - v * (factor * factor * factor * inner), grad_gain)

def gelu_parts(v):
    c = 0.7978845608028654
    square = v * v
    t = jnp.tanh(v * (c + c * 0.044715 * square))
    half = 0.5 + 0.5 * t
    slope = half + v * (half * (1.0 - t)) * (c + 3.0 * c * 0.044715 * square)
    return (v * half, slope)

def causal_mask(enc, length):
    key_pos = lax.broadcasted_iota(jnp.int32, (length, length), 0)
    query_pos = lax.broadcasted_iota(jnp.int32, (length, length), 1)
    return key_pos <= query_pos + enc * length

def scores(q, k, allowed):
    s = mm(k, q, NT)
    return s if allowed is None else jnp.where(allowed, s, NEGATIVE)

def attend(q_ref, q0, kv_ref, k0, v0, out_ref, lse_ref, allowed, width):
    for h in range(width // DH):
        lo = h * DH
        q = q_ref[:, q0 + lo:q0 + lo + DH] * BF16(DH ** (-0.5))
        k = kv_ref[:, k0 + lo:k0 + lo + DH]
        v = kv_ref[:, v0 + lo:v0 + lo + DH]
        s = scores(q, k, allowed)
        top = jnp.max(s, axis=0, keepdims=True)
        e = jnp.exp(s - top)
        total = jnp.sum(e, axis=0, keepdims=True)
        o = mm(v.T, e.astype(BF16)) * (1.0 / total)
        out_ref[:, lo:lo + DH] = o.T.astype(BF16)
        lse_ref[h:h + 1, :] = top + jnp.log(total)

def attend_back(q_ref, q0, kv_ref, k0, v0, lse_ref, grad, dq_ref, dkv_ref, allowed, width):
    for h in range(width // DH):
        lo = h * DH
        q = q_ref[:, q0 + lo:q0 + lo + DH] * BF16(DH ** (-0.5))
        k = kv_ref[:, k0 + lo:k0 + lo + DH]
        v = kv_ref[:, v0 + lo:v0 + lo + DH]
        g = grad[:, lo:lo + DH]
        p = jnp.exp(scores(q, k, allowed) - lse_ref[h:h + 1, :])
        dp = mm(v, g, NT)
        delta = jnp.sum(p * dp, axis=0, keepdims=True)
        ds = (p * (dp - delta)).astype(BF16)
        dkv_ref[:, v0 + lo:v0 + lo + DH] = mm(p.astype(BF16), g).astype(BF16)
        dkv_ref[:, k0 + lo:k0 + lo + DH] = mm(ds, q).astype(BF16)
        dq = mm(k.T, ds) * DH ** (-0.5)
        dq_ref[:, q0 + lo:q0 + lo + DH] = dq.T.astype(BF16)

def ffn_back(a, g, weights, dgate_refs, dup_refs):
    part = None
    for (wg, wu, wd), dgate_ref, dup_ref in zip(weights, dgate_refs, dup_refs):
        value, slope = gelu_parts(mm(a, wg[...]))
        up = mm(a, wu[...])
        dh = mm(g, wd[...])
        dgate_ref[...] = (dh * up * slope).astype(BF16)
        dup_ref[...] = (dh * value).astype(BF16)
        here = mm(dgate_ref[...], wg[...], NT) + mm(dup_ref[...], wu[...], NT)
        part = here if part is None else part + here
    return part

def ffn_both(a, g, weights, hid_refs, dgate_refs, dup_refs):
    part = None
    for (wg, wu, wd), hid_ref, dgate_ref, dup_ref in zip(weights, hid_refs, dgate_refs, dup_refs):
        gate = mm(a, wg[...])
        up = mm(a, wu[...])
        dh = mm(g, wd[...])
        value, slope = gelu_parts(gate)
        hid_ref[...] = (value * up).astype(BF16)
        dgate_ref[...] = (dh * up * slope).astype(BF16)
        dup_ref[...] = (dh * value).astype(BF16)
        here = mm(dgate_ref[...], wg[...], NT) + mm(dup_ref[...], wu[...], NT)
        part = here if part is None else part + here
    return part

def after(value, *others):
    return lax.optimization_barrier((value,) + others)[0]
LAG = {'X': 2, 'A': 2, 'B': 2, 'R': 2, 'X0': 3}

class Order:

    def __init__(self):
        self.tokens = []

    def place(self, value):
        return after(value, *self.tokens) if self.tokens else value

    def done(self, value):
        self.tokens = [value]

    def need(self, *values):
        self.tokens = self.tokens + list(values)
COST = pl.CostEstimate(flops=1, bytes_accessed=1, transcendentals=0)
SMEM_SPEC = pl.BlockSpec(memory_space=pltpu.SMEM)

def whole_spec(spec):
    return spec if spec is SMEM_SPEC else pl.BlockSpec(memory_space=pltpu.VMEM)

class Call:

    def __init__(self, rows, length, order):
        self.rows, self.length, self.order = (rows, length, order)
        self.specs, self.args, self.out_specs, self.out_shapes = ([], [], [], [])
        self.in_views, self.out_views = ([], [])

    @property
    def views(self):
        return self.in_views + self.out_views

    def scalar(self, value):
        self.specs.append(SMEM_SPEC)
        self.args.append(value)
        self.in_views.append(None)

    def tokens(self, *values):
        for value in values:
            count = value.shape[0] // self.rows
            self.specs.append(pl.BlockSpec((count, value.shape[1]), lambda i: (i, 0)))
            self.args.append(value)
            self.in_views.append(None)

    def heads(self, *values):
        for value in values:
            self.specs.append(pl.BlockSpec((None,) + value.shape[1:], lambda i: (i, 0, 0)))
            self.args.append(value)
            self.in_views.append(0)

    def whole(self, *values):
        for value in values:
            block = None
            if isinstance(value, tuple):
                value, block, at = value
            if block is None:
                block, at = (value.shape, (0,) * value.ndim)
            self.specs.append(pl.BlockSpec(block, lambda i, at=at: at))
            self.args.append(value)
            view = tuple((k if size is None else pl.ds(k * size, size) for k, size in zip(at, block)))
            self.in_views.append(None if block == value.shape else view)

    def out_tokens(self, width, kind, count=None):
        count = self.length if count is None else count
        self.out_views.append(None)
        self.out_specs.append(pl.BlockSpec((count, width), lambda i: (i, 0)))
        self.out_shapes.append(jax.ShapeDtypeStruct((self.rows * count, width), kind))

    def out_heads(self, heads):
        self.out_views.append(0)
        self.out_specs.append(pl.BlockSpec((None, heads, self.length), lambda i: (i, 0, 0)))
        self.out_shapes.append(jax.ShapeDtypeStruct((self.rows, heads, self.length), F32))

    def out_whole(self, shape, kind):
        self.out_views.append(None)
        self.out_specs.append(pl.BlockSpec(shape, lambda i, n=len(shape): (0,) * n))
        self.out_shapes.append(jax.ShapeDtypeStruct(shape, kind))

    def narrowed(self, kernel):
        views = list(self.views)

        def inner(*refs):
            kernel(*[ref if view is None else ref.at[view] for ref, view in zip(refs, views)])
        return inner

    def run(self, kernel, name):
        first = next((k for k, v in enumerate(self.args) if v.dtype != jnp.int32))
        self.args[first] = self.order.place(self.args[first])
        more = {'grid': (self.rows,)}
        if self.rows == 1:
            more = {}
            self.specs = [whole_spec(spec) for spec in self.specs]
            self.out_specs = [whole_spec(spec) for spec in self.out_specs]
            kernel = self.narrowed(kernel)
        out = pl.pallas_call(kernel, in_specs=self.specs, out_specs=self.out_specs, out_shape=self.out_shapes, **more, compiler_params=pltpu.CompilerParams(vmem_limit_bytes=VMEM), cost_estimate=COST, name=name)(*self.args)
        self.order.done(out[0])
        return out

def accumulate(ref, value, first):
    if first is True:
        ref[...] = value
        return

    @pl.when(first)
    def _():
        ref[...] = value

    @pl.when(jnp.logical_not(first))
    def _():
        ref[...] += value

def on_device(layer_input, dec_lengths, out_cotangent, gains, attn_weights, ffn_weights):
    tensor = lax.axis_size('tensor')
    planes = lax.axis_size('dp')
    batch, part_len, model = layer_input.shape[1:]
    groups = 2 if tensor % 2 == 0 and batch % 2 == 0 else 1
    cores = tensor // groups
    rows = batch // groups
    length = part_len * tensor
    tokens = rows * length
    share = length // cores
    width = attn_weights.shape[3]
    hidden_width = ffn_weights.shape[3]
    heads = width // DH
    shares = range(groups)
    section = lax.axis_index('section')
    plane = lax.axis_index('dp')
    lane = lax.axis_index('tensor')
    group = lane // cores
    core = lane % cores
    is_enc = section == 0
    outer = (plane == 0) | (plane == planes - 1)
    place = jnp.stack([v.astype(jnp.int32) for v in (is_enc, core, outer, plane % 2, group)])
    group_route = [(t, (t + cores) % tensor) for t in range(tensor)]
    core_groups = [[g * cores + c for c in range(cores)] for g in range(groups)]
    next_plane = [(p, p ^ 1) for p in range(planes)]
    order = Order()

    def over_groups(value):
        return lax.ppermute(value, 'tensor', group_route)

    def decoder_only(value, axis, route):
        size = lax.axis_size(axis)
        return lax.ppermute(value, ('section', axis), [(size + a, size + b) for a, b in route])

    def encoder_only(value, axis, route):
        return lax.ppermute(value, ('section', axis), route)

    def core_route(step):
        return [(g * cores + (c + step) % cores, g * cores + c) for g in range(groups) for c in range(cores)]

    def core_swap(value):
        return [lax.ppermute(value, 'tensor', core_route(k)) for k in range(1, cores)]

    def core_sum(part):
        if cores <= 2:
            return [part] + core_swap(part)
        return [lax.psum(part, 'tensor', axis_index_groups=core_groups)]

    def pick(value, index, count):
        return lax.dynamic_slice_in_dim(value, index * count, count, 0)

    def move(value, axis, route, decoder):
        return decoder_only(value, axis, route) if decoder else lax.ppermute(value, axis, route)
    queues = {}

    def queued(link, value, transfer):
        lag = LAG.get(link, 0)
        line = queues.setdefault(link, [])
        if lag and len(line) >= lag:
            value = after(value, line[-lag])
        got = transfer(value)
        line.append(got)
        return got

    class Fetch:

        def __init__(self, own, at, count, *behind, assisted=True):
            self.halved = assisted and planes % 2 == 0 and (count % 32 == 0)
            if self.halved:
                count //= 2
                at = at + plane % 2 * count
            value = lax.dynamic_slice_in_dim(own, at, count, 0)
            if behind:
                value = after(value, *behind)
            self.direct = queued('X0', value, over_groups)

        def forward(self, placed=True):
            if self.halved:
                if placed:
                    self.direct = order.place(self.direct)
                    order.need(self.direct)
                self.passed = queued('Z0', self.direct, lambda v: lax.ppermute(v, 'dp', next_plane))

        def arrived(self):
            return self.passed if self.halved else self.direct

        def parts(self):
            return [self.direct, self.passed] if self.halved else [self.direct]

    def assemble(place_ref, refs, out_ref, halved):
        if len(refs) == 1:
            out_ref[...] = refs[0][...]
            return
        half = refs[0].shape[0]
        first = place_ref[3] * half if halved else 0
        second = half - first
        out_ref[pl.ds(pl.multiple_of(first, half), half), :] = refs[0][...]
        out_ref[pl.ds(pl.multiple_of(second, half), half), :] = refs[1][...]

    def to_rows(value, route_group, placed=False):
        if groups == 1:
            blocks = value[:, None]
        else:
            mine = pick(value, group, rows)
            got = early_cot if placed else route_group(pick(value, 1 - group, rows))
            if placed:
                got = order.place(got)
            first = group == 0
            blocks = jnp.stack([jnp.where(first, mine, got), jnp.where(first, got, mine)], 1)
        if cores == 2:
            got = core_swap(blocks)[0]
            low = core == 0
            blocks = jnp.stack([jnp.where(low, blocks, got), jnp.where(low, got, blocks)], 2)
        elif cores > 2:
            blocks = lax.all_gather(blocks, 'tensor', axis=2, axis_index_groups=core_groups)
        return blocks.reshape(tokens, model)

    def from_rows(value):
        blocks = value.reshape(rows, tensor, part_len, model)
        mine = lax.dynamic_index_in_dim(blocks, lane, 1, keepdims=False)
        if groups == 1:
            return mine
        got = over_groups(lax.dynamic_index_in_dim(blocks, (lane + cores) % tensor, 1, keepdims=False))
        first = group == 0
        return jnp.concatenate([jnp.where(first, mine, got), jnp.where(first, got, mine)], 0)

    def split(refs, *counts):
        at, out = (0, [])
        for count in counts:
            out.append(refs[at:at + count])
            at += count
        return out

    def call():
        return Call(rows, length, order)

    def first_row():
        return True if rows == 1 else pl.program_id(0) == 0
    attn_t = attn_weights[0].transpose(0, 2, 1).reshape(6 * width, model)
    ffn = ffn_weights[0]
    gain = gains[0]
    own_self = (attn_t, (4 * width, model), (0, 0))
    own_side = (attn_t, (2 * width, model), (2, 0))
    own_ffn = [(ffn, (None, model, hidden_width), (j, 0, 0)) for j in range(3)]
    w_self, w_ffn, w_dec, w_side = ([own_self], [own_ffn], [own_ffn], [own_side])
    x_parts = [pick(layer_input[0], group, rows)]
    if groups == 2:
        x_parts.append(queued('X0', pick(layer_input[0], 1 - group, rows), over_groups))
        flat = ffn.reshape(3 * model, hidden_width)
        behind = {'none': [], 'in': [x_parts[1]], 'slice': [pick(layer_input[0], 1 - group, rows)]}
        far_self = Fetch(attn_t, 0, 4 * width, *behind['slice'], assisted=True)
        far_pair = [Fetch(flat, 0, model)]
        far_pair.append(Fetch(flat, model, model, x_parts[1]))
        half = model // 2
        far_down = [ffn[2, :half], ffn[2, half:]]
        far_down[0] = after(far_down[0], far_pair[0].direct)
        far_down[1] = after(far_down[1], far_pair[0].direct)
        far_down = [queued('X0', v, lambda v: encoder_only(v, 'tensor', group_route)) for v in far_down]
    side_out = attn_t[4 * width:]
    side_out = after(side_out, x_parts[1])
    enc_side = lax.ppermute(side_out, 'section', [(0, 1)])
    x_parts = x_parts + [v for part in zip(*[core_swap(v) for v in x_parts]) for v in part]
    c = call()
    c.scalar(place)
    c.heads(*x_parts)
    c.whole(gain[0:1])
    c.out_tokens(model, BF16)
    c.out_tokens(model, BF16)

    def first_norm(place_ref, *refs):
        gain_ref, x_ref, a_ref = refs[-3:]
        for k, ref in enumerate(refs[:-3]):
            from_core = lax.rem(place_ref[1] + k // groups, cores)
            from_group = lax.rem(place_ref[4] + k % groups, groups)
            at = (from_group * cores + from_core) * part_len
            x_ref[pl.ds(pl.multiple_of(at, part_len), part_len), :] = ref[...]
        a_ref[...] = normed(x_ref[...].astype(F32), gain_ref[...])
    if groups == 2:
        far_self.forward(False)
        order.need(far_self.direct)
    x, a0 = c.run(first_norm, 'first_norm')
    cot = to_rows(out_cotangent, lambda v: decoder_only(v, 'tensor', group_route))
    row_ids = group * rows + jnp.arange(rows)
    live = jnp.arange(length)[None, :] < dec_lengths[row_ids][:, None]
    live = live.reshape(tokens, 1)
    gy = jnp.where(live, cot, BF16(0))
    early_cot = None

    def self_forward(i, part):
        pieces = far_self.parts() if i == 1 else [w_self[i]]
        made = i == 1 and len(pieces) > 1
        if i == 1 and (not made):
            w_self.append(pieces[0])
        c = call()
        c.scalar(place)
        c.tokens(a0)
        c.whole(*pieces)
        if part is not None:
            c.tokens(part)
        c.out_tokens(3 * width, BF16)
        c.out_tokens(width, BF16)
        c.out_heads(heads)
        c.out_tokens(model, BF16 if i == groups - 1 else F32)
        if made:
            c.out_whole((4 * width, model), BF16)

        def kernel(place_ref, a_ref, *refs):
            qkv_ref, att_ref, lse_ref, part_ref = refs[-5:-1] if made else refs[-4:]
            w_ref = refs[0]
            if made:
                w_ref = refs[-1]
                assemble(place_ref, refs[:len(pieces)], w_ref, far_self.halved)
            qkv_ref[...] = mm(a_ref[...], w_ref[:3 * width, :], NT).astype(BF16)
            allowed = causal_mask(place_ref[0], length)
            attend(qkv_ref, 0, qkv_ref, width, 2 * width, att_ref, lse_ref, allowed, width)
            out = mm(att_ref[...], w_ref[3 * width:, :])
            if part is not None:
                out = out + refs[len(pieces)][...]
            part_ref[...] = out.astype(part_ref.dtype)
        return c.run(kernel, 'self_forward')
    qkv, att, lse, part = ([], [], [], None)
    for i in shares:
        if i == 1:
            order.need(enc_side)
            order.need(gy)
            far_pair[0].forward()
            far_pair[1].forward()
        a, b, l, part, *rest = self_forward(i, part)
        w_self += rest
        qkv.append(a)
        att.append(b)
        lse.append(l)
    if groups == 2:
        pins = [] + [far_pair[0].arrived()] + []
        if pins:
            part = after(part, *pins)
    parts = core_sum(part)

    def total_of(refs):
        value = refs[0][...].astype(F32)
        for ref in refs[1:]:
            value = value + ref[...].astype(F32)
        return value

    def ffn_share(a, wg, wu, wd, hid_ref):
        value, _ = gelu_parts(mm(a, wg[...]))
        hid_ref[...] = (value * mm(a, wu[...])).astype(BF16)
        return mm(hid_ref[...], wd[...], NT)
    c = call()
    c.tokens(x, *parts)
    c.whole(gain[1:2], *w_ffn[0])
    c.out_tokens(model, F32)
    c.out_tokens(model, BF16)
    c.out_tokens(hidden_width, BF16)
    c.out_tokens(model, BF16 if groups == 1 else F32)

    def ffn_first(x_ref, *refs):
        count = len(parts)
        gain_ref, wg, wu, wd, x1_ref, a1_ref, hid_ref, part_ref = refs[count:]
        x1 = x_ref[...].astype(F32) + total_of(refs[:count])
        x1_ref[...] = x1
        a1_ref[...] = normed(x1, gain_ref[...])
        part_ref[...] = ffn_share(a1_ref[...], wg, wu, wd, hid_ref).astype(part_ref.dtype)
    x1, a1, hid, part = c.run(ffn_first, 'ffn_first')
    e_hid = [hid]
    if groups == 2:
        both_sides = decoder_only(jnp.concatenate([attn_t[4 * width:], enc_side], 0), 'tensor', group_route)
        pieces = [fetch.parts() for fetch in far_pair]
        c = call()
        c.scalar(place)
        c.tokens(a1, part)
        c.whole(*[v for got in pieces for v in got], *far_down)
        c.out_tokens(model, BF16)
        c.out_tokens(hidden_width, BF16)
        c.out_whole((2 * model, hidden_width), BF16)
        c.out_whole((model, hidden_width), BF16)

        def ffn_second(place_ref, a_ref, prev_ref, *refs):
            *piece_refs, down_refs, (part_ref, hid_ref, pair_ref, wd) = split(refs, *[len(got) for got in pieces], 2, 4)
            for k in range(2):
                w = pair_ref.at[k * model:(k + 1) * model]
                assemble(place_ref, piece_refs[k], w, far_pair[k].halved)
            for k, ref in enumerate(down_refs):
                wd[k * half:(k + 1) * half, :] = ref[...]
            ws = (pair_ref.at[:model], pair_ref.at[model:], wd)
            part_ref[...] = (prev_ref[...] + ffn_share(a_ref[...], *ws, hid_ref)).astype(BF16)
        part, hid, pair, far_down = c.run(ffn_second, 'ffn_second')
        far = [(pair, (model, hidden_width), (k, 0)) for k in range(2)]
        dec_far = decoder_only(ffn[2], 'tensor', group_route)
        w_dec = [own_ffn, far + [dec_far]]
        w_ffn.append(far + [far_down])
        e_hid.append(hid)
        part = after(part, both_sides)
    parts = core_sum(part)
    c = call()
    c.scalar(place)
    c.tokens(x1, *parts)
    c.whole(gain[2:3])
    c.out_tokens(model, F32)
    c.out_tokens(model, BF16)
    c.out_tokens(model, BF16, share)

    def memory_kernel(place_ref, x1_ref, *refs):
        gain_ref, y_ref, memory_ref, mine_ref = refs[-4:]
        y = x1_ref[...] + total_of(refs[:-4])
        y_ref[...] = y
        memory_ref[...] = normed(y, gain_ref[...])
        start = pl.multiple_of(place_ref[1] * share, share)
        mine_ref[...] = memory_ref[pl.ds(start, share), :]
    if groups == 2:
        both_sides = [(both_sides, (2 * width, model), (k, 0)) for k in range(2)]
    y, memory, mem_mine = c.run(memory_kernel, 'memory')
    mem_mine = lax.ppermute(mem_mine, 'section', [(0, 1)])
    mem = [mem_mine] + core_swap(mem_mine)
    w_side, w_enc = ([own_side], [enc_side])
    if groups == 2:
        w_side.append(both_sides[0])
        w_enc.append(both_sides[1])
    c = call()
    c.scalar(place)
    c.tokens(a1, *mem)
    c.whole(*w_side, *w_enc)
    for i in shares:
        c.out_tokens(width, BF16)
    for i in shares:
        c.out_tokens(2 * width, BF16)
    for i in shares:
        c.out_tokens(width, BF16)
    for i in shares:
        c.out_heads(heads)
    c.out_tokens(model, BF16)

    def cross_forward(place_ref, a_ref, *refs):
        mem_refs, side, enc, cq, kv, catt, clse, (part_ref,) = split(refs, cores, groups, groups, groups, groups, groups, groups, 1)
        out = None
        for i in shares:
            cq[i][...] = mm(a_ref[...], side[i][:width, :], NT).astype(BF16)
            for j, ref in enumerate(mem_refs):
                kv[i][j * share:(j + 1) * share, :] = mm(ref[...], enc[i][...], NT).astype(BF16)
            attend(cq[i], 0, kv[i], 0, width, catt[i], clse[i], None, width)
            here = mm(catt[i][...], side[i][width:, :])
            out = here if out is None else out + here
        part_ref[...] = out.astype(BF16)
    cq, kv, catt, clse, (part,) = split(c.run(cross_forward, 'cross_forward'), groups, groups, groups, groups, 1)
    if groups == 2:
        part = after(part, dec_far)
    parts = core_sum(part)
    c = call()
    c.tokens(x1, gy, *parts)
    c.whole(gain[2:3], *[w for ws in w_dec for w in ws])
    c.out_tokens(model, F32)
    c.out_tokens(model, BF16)
    for _ in range(3 * groups):
        c.out_tokens(hidden_width, BF16)
    c.out_tokens(model, BF16)

    def triples(refs):
        return [refs[3 * i:3 * i + 3] for i in shares]

    def dec_ffn(x1_ref, gy_ref, *refs):
        part_refs, (gain_ref,), ws, (x2_ref, a2_ref), hid, dgate, dup, (part_ref,) = split(refs, len(parts), 1, 3 * groups, 2, groups, groups, groups, 1)
        x2 = x1_ref[...] + total_of(part_refs)
        x2_ref[...] = x2
        a2_ref[...] = normed(x2, gain_ref[...])
        part_ref[...] = ffn_both(a2_ref[...], gy_ref[...], triples(ws), hid, dgate, dup).astype(BF16)
    (x2, a2), d_hid, d_gate, d_up, (part,) = split(c.run(dec_ffn, 'dec_ffn'), 2, groups, groups, groups, 1)
    parts = core_sum(part)
    c = call()
    c.tokens(x2, gy, *parts, *cq, *kv)
    c.heads(*clse)
    c.whole(gain[2:3], *w_side, *w_enc)
    c.out_tokens(model, F32)
    c.out_tokens(model, BF16)
    c.out_whole((1, model), F32)
    for i in shares:
        c.out_tokens(width, BF16)
    c.out_tokens(2 * width * groups, BF16)
    c.out_tokens(model, BF16)
    for j in range(cores):
        c.out_tokens(model, F32 if j == 0 else BF16, share)

    def cross_back(x2_ref, gy_ref, *refs):
        part_refs, cq_refs, kv_refs, lse_refs, (gain_ref,), side, enc, (g2_ref, low_ref, gain2_ref), dcq_refs, (dkv_ref, part_ref), mem_refs = split(refs, len(parts), groups, groups, groups, 1, groups, groups, 3, groups, 2, cores)
        dkv_refs = [dkv_ref.at[:, 2 * width * i:2 * width * (i + 1)] for i in shares]
        back, grad_gain = normed_back(x2_ref[...], gain_ref[...], total_of(part_refs))
        accumulate(gain2_ref, grad_gain, first_row())
        g2 = gy_ref[...].astype(F32) + back
        g2_ref[...] = g2
        low_ref[...] = g2.astype(BF16)
        out = None
        for i in shares:
            grad = mm(low_ref[...], side[i][width:, :], NT).astype(BF16)
            attend_back(cq_refs[i], 0, kv_refs[i], 0, width, lse_refs[i], grad, dcq_refs[i], dkv_refs[i], None, width)
            here = mm(dcq_refs[i][...], side[i][:width, :])
            out = here if out is None else out + here
        part_ref[...] = out.astype(BF16)
        for j, ref in enumerate(mem_refs):
            total = None
            for i in shares:
                here = mm(dkv_refs[i][j * share:(j + 1) * share, :], enc[i][...])
                total = here if total is None else total + here
            ref[...] = total.astype(ref.dtype)
    (g2, g2_low, dec_gain2), dcq, (dkv, part_dec), dmem = split(c.run(cross_back, 'cross_back'), 3, groups, 2, cores)
    mine = dmem[0]
    for step in range(1, cores):
        mine = mine + lax.ppermute(dmem[step], 'tensor', core_route(cores - step)).astype(F32)
    mine = mine.astype(BF16)
    order.done(mine)
    mine = lax.ppermute(mine, 'section', [(1, 0)])
    dmem = [mine] + core_swap(mine)
    kept = SimpleNamespace(dqkv=[])
    kept.dkv = lax.ppermute(dkv, 'section', [(1, 0)])
    chunk = 4 * width // 3

    def products(terms, tails, counts, name):
        sizes = [[len(values) for values in term] for term in terms]
        flat = [v for term in terms for values in term for v in values] + tails
        flat[0] = order.place(flat[0])

        def product(left_refs, right_refs):
            total = None
            for j, right in enumerate(right_refs):
                spans = [(left_refs[j][...], right[...])]
                for left, value in spans:
                    here = mm(left, value, TN)
                    total = here if total is None else total + here
            return total

        def kernel(place_ref, *refs):
            outs = refs[len(flat):]
            starts = [sum(counts[:k]) for k in range(len(counts))]

            def store(value, at):
                done = 0
                while done < value.shape[0]:
                    k = max((q for q in range(len(counts)) if starts[q] <= at + done))
                    inside = at + done - starts[k]
                    count = min(value.shape[0] - done, counts[k] - inside)
                    outs[k][inside:inside + count, :] = value[done:done + count].astype(BF16)
                    done += count
            used, at = (0, 0)
            for size in sizes:
                values = split(refs[used:], *size)
                used += sum(size)
                if len(size) == 2:
                    store(product(*values), at)
                else:

                    @pl.when(place_ref[0] == 1)
                    def _(values=values, at=at):
                        store(product(*values[:2]), at)

                    @pl.when(place_ref[0] == 0)
                    def _(values=values, at=at):
                        store(product(*values[2:]), at)
                at += values[0][0].shape[1]
            for tail in refs[used:len(flat)]:
                store(tail[...], at)
                at += tail.shape[0]
        out = pl.pallas_call(kernel, in_specs=[SMEM_SPEC] + [pl.BlockSpec(memory_space=pltpu.VMEM)] * len(flat), out_shape=[jax.ShapeDtypeStruct((count, model), BF16) for count in counts], compiler_params=pltpu.CompilerParams(vmem_limit_bytes=VMEM), cost_estimate=COST, name=name)(place, *flat)
        order.done(out[-1])
        return list(out)

    def add_kernel(value, got):

        def kernel(value_ref, got_ref, out_ref):
            total = value_ref[...].astype(F32) + got_ref[...].astype(F32)
            out_ref[...] = total.astype(BF16)
        c = Call(1, length, order)
        c.whole(value, got)
        c.out_whole(value.shape, BF16)
        return c.run(kernel, 'sum_step')[0]

    class Sum:

        def __init__(self):
            self.got, self.at = (None, 0)
            half = planes // 2
            self.moves = [('group', group_route)] if groups == 2 else []
            if planes % 2 == 0:
                for k in range(half - 1):
                    self.moves.append(('add', [(k, k + 1), (planes - 1 - k, planes - 2 - k)]))
                self.moves.append(('add', [(half - 1, half), (half, half - 1)]))
                for k in range(half - 1):
                    left, right = (half - 1 - k, half + k)
                    self.moves.append(('take', [(left, left - 1), (right, right + 1)]))

        def send(self):
            if groups == 2:
                self.got = queued('X', self.other, over_groups)

        def step(self):
            if self.at == len(self.moves):
                return
            kind, route = self.moves[self.at]
            if self.got is None:
                self.got = lax.ppermute(self.value, 'dp', route)
            names = 'XABR' if groups == 2 and planes == 4 else 'X' * 100
            last = self.at == len(self.moves) - 1
            if last and kind == 'take':
                got = self.got
                order.need(got)
            else:
                got = order.place(self.got)
            if kind == 'take':
                targets = [b for _, b in route]
                self.value = jnp.where((plane == targets[0]) | (plane == targets[1]), got, self.value)
            else:
                self.value = add_kernel(self.value, got)
            if not (last and kind == 'take'):
                order.done(self.value)
            self.at += 1
            if not last:
                route = self.moves[self.at][1]
                self.got = queued(names[self.at], self.value, lambda v: lax.ppermute(v, 'dp', route))

        def finish(self):
            while self.at < len(self.moves):
                self.step()
            if planes % 2 and planes > 1:
                self.value = lax.psum(self.value, 'dp')
            return self.value
    sum_d1, sum_d2, sum_g, sum_u, sum_s, sum_q1, sum_q2 = [Sum() for _ in range(7)]

    def side_grads(i):
        args = [order.place(memory), kept.dkv, dcq[i], a1, catt[i], g2_low]

        def kernel(place_ref, memory_ref, dkv_ref, dcq_ref, a1_ref, catt_ref, g2_ref, *out_refs):

            @pl.when(place_ref[0] == 1)
            def _():
                total = None
                for row in range(rows):
                    for j in range(cores):
                        at = row * length + lax.rem(place_ref[1] + j, cores) * share
                        right = memory_ref[pl.ds(pl.multiple_of(at, share), share), :]
                        start = row * length + j * share
                        left = dkv_ref[start:start + share, 2 * width * i:2 * width * (i + 1)]
                        here = mm(left, right, TN)
                        total = here if total is None else total + here
                out_refs[0][...] = total.astype(BF16)

            @pl.when(place_ref[0] == 0)
            def _():
                out_refs[0][:width, :] = mm(dcq_ref[...], a1_ref[...], TN).astype(BF16)
                out_refs[0][width:, :] = mm(catt_ref[...], g2_ref[...], TN).astype(BF16)
        out = pl.pallas_call(kernel, in_specs=[SMEM_SPEC] + [pl.BlockSpec(memory_space=pltpu.VMEM)] * len(args), out_shape=[jax.ShapeDtypeStruct((2 * width, model), BF16)], compiler_params=pltpu.CompilerParams(vmem_limit_bytes=VMEM), cost_estimate=COST, name='side_grads')(place, *args)
        order.done(out[-1])
        return out

    def decoder_down():
        c = call()
        c.tokens(*d_hid)
        c.whole(*[ws[2] for ws in w_dec])
        c.out_tokens(model, BF16)

        def dec_down(*refs):
            hid_refs, ws, (out_ref,) = split(refs, groups, groups, 1)
            total = None
            for hid_ref, w in zip(hid_refs, ws):
                here = mm(hid_ref[...], w[...], NT)
                total = here if total is None else total + here
            out_ref[...] = total.astype(BF16)
        return core_sum(c.run(dec_down, 'dec_down')[0])

    def decoder_output(last):
        c = call()
        c.scalar(place)
        c.tokens(memory, live.astype(F32), x2, *last)
        c.out_tokens(model, BF16)

        def output(place_ref, memory_ref, live_ref, x2_ref, *refs):
            total = (x2_ref[...] + total_of(refs[:-1])) * live_ref[...]
            refs[-1][...] = jnp.where(place_ref[0] == 1, memory_ref[...], total.astype(BF16))
        return c.run(output, 'output')[0]
    c = call()
    c.scalar(place)
    c.tokens(y, *dmem, gy, g2)
    c.whole(gain[2:3], dec_gain2)
    c.out_tokens(model, BF16)
    c.out_tokens(model, F32)
    c.out_whole((1, model), F32)

    def memory_back(place_ref, y_ref, *refs):
        dmem_refs, (gy_ref, g2_ref, gain_ref, old_gain, low_ref, g_ref, new_gain) = split(refs, cores, 7)

        @pl.when(place_ref[0] == 1)
        def _():
            for j, ref in enumerate(dmem_refs):
                at = lax.rem(place_ref[1] + j, cores)
                g_ref[pl.ds(pl.multiple_of(at * share, share), share), :] = ref[...].astype(F32)
            e_g, grad_gain = normed_back(y_ref[...], gain_ref[...], g_ref[...])
            accumulate(new_gain, grad_gain, first_row())
            g_ref[...] = e_g
            low_ref[...] = e_g.astype(BF16)

        @pl.when(place_ref[0] == 0)
        def _():
            low_ref[...] = gy_ref[...]
            g_ref[...] = g2_ref[...]
            new_gain[...] = old_gain[...]
    ffn_g, g_in, gain2 = c.run(memory_back, 'memory_back')

    def down_grads(i):
        terms = [([e_hid[i]], [ffn_g], [d_hid[i]], [ffn_g])]
        return products(terms, [], [hidden_width // 2] * 2, 'down_grads')
    kept.g_in = g_in

    def ffn_back_step():
        global_parts = encoder_ffn_back()
        kept.parts = core_sum(global_parts)

    def encoder_ffn_back():
        c = call()
        c.scalar(place)
        c.tokens(ffn_g, a1, part_dec)
        c.whole(*[w for ws in w_ffn for w in ws])
        c.out_tokens(model, BF16)
        for _ in range(2 * groups):
            c.out_tokens(hidden_width, BF16)

        def enc_ffn_back(place_ref, g_ref, a1_ref, old_part, *refs):
            ws, (part_ref,), dgate, dup = split(refs, 3 * groups, 1, groups, groups)

            @pl.when(place_ref[0] == 1)
            def _():
                part_ref[...] = ffn_back(a1_ref[...], g_ref[...], triples(ws), dgate, dup).astype(BF16)

            @pl.when(place_ref[0] == 0)
            def _():
                part_ref[...] = old_part[...]
        (part,), kept.gate, kept.up = split(c.run(enc_ffn_back, 'enc_ffn_back'), 1, groups, groups)

        def pair_grads(i):
            terms = [([e_gate[i]], [a1], [d_gate[i]], [a2]), ([e_up[i]], [a1], [d_up[i]], [a2])]
            return products(terms, [], [hidden_width] * 2, 'pair_grads')
        return part

    def gate_up(i, which):
        return products([([(kept.gate, kept.up)[which][i]], [a1], [(d_gate, d_up)[which][i]], [a2])], [], [hidden_width], 'pair_grads')

    def self_back(i):
        c = call()
        c.scalar(place)
        if i == 0:
            c.tokens(x1, kept.g_in, *kept.parts)
        else:
            c.tokens(kept.g1_low, kept.part)
        c.tokens(qkv[i])
        c.heads(lse[i])
        if i == 0:
            c.whole(gain[1:2])
        c.whole(w_self[i])
        if i == 0:
            c.out_tokens(model, F32)
            c.out_tokens(model, BF16)
            c.out_whole((1, model), F32)
        c.out_tokens(3 * width, BF16)
        c.out_tokens(model, BF16 if i == groups - 1 else F32)

        def kernel(place_ref, *refs):
            if i == 0:
                (x1_ref, g_ref), part_refs, (qkv_ref, lse_ref, gain_ref, w_ref), (g1_ref, low_ref, gain1_ref, d_ref, part_ref) = split(refs, 2, len(kept.parts), 4, 5)
                back, grad_gain = normed_back(x1_ref[...], gain_ref[...], total_of(part_refs))
                accumulate(gain1_ref, grad_gain, first_row())
                g1 = g_ref[...] + back
                g1_ref[...] = g1
                low_ref[...] = g1.astype(BF16)
            else:
                low_ref, prev_ref, qkv_ref, lse_ref, w_ref, d_ref, part_ref = refs
            allowed = causal_mask(place_ref[0], length)
            grad = mm(low_ref[...], w_ref[3 * width:, :], NT).astype(BF16)
            attend_back(qkv_ref, 0, qkv_ref, width, 2 * width, lse_ref, grad, d_ref, d_ref, allowed, width)
            out = mm(d_ref[...], w_ref[:3 * width, :])
            if i > 0:
                out = out + prev_ref[...]
            part_ref[...] = out.astype(part_ref.dtype)
        *first, d, kept.part = c.run(kernel, 'self_back')
        if i == 0:
            kept.g1, kept.g1_low, kept.gain1 = first
        kept.dqkv.append(d)
        if i == groups - 1:
            kept.parts = core_sum(kept.part)

    def input_back_step():
        c = call()
        c.tokens(x, kept.g1, *kept.parts)
        c.whole(gain[0:1], kept.gain1, gain2)
        c.out_tokens(model, BF16)
        c.out_whole((16, model), F32)

        def input_back(x_ref, g1_ref, *refs):
            gain_ref, gain1_ref, gain2_ref, dx_ref, rows_ref = refs[-5:]
            back, grad_gain = normed_back(x_ref[...].astype(F32), gain_ref[...], total_of(refs[:-5]))
            dx_ref[...] = (g1_ref[...] + back).astype(BF16)
            accumulate(rows_ref.at[0:1], grad_gain, first_row())
            rows_ref[1:2, :] = gain1_ref[...]
            rows_ref[2:3, :] = gain2_ref[...]
            rows_ref[3:, :] = jnp.zeros((13, model), F32)
        kept.dx, kept.gains = c.run(input_back, 'input_back')
    first_rows = 2 * width + 0
    self_counts = [first_rows, 4 * width + 16 - first_rows]

    def self_grads(i):
        terms = [([kept.dqkv[i]], [a0]), ([att[i]], [kept.g1_low])]
        return products(terms, [kept.gains], self_counts, 'self_grads')

    def ffn_out_step():
        values = [one.finish() for one in (sum_g, sum_u, sum_d1, sum_d2)]
        c = Call(1, length, order)
        c.whole(*values)
        c.out_whole((3, model, hidden_width), F32)

        def ffn_out(*refs):
            *ins, out_ref = refs
            half = hidden_width // 2
            for k in range(2):
                out_ref[k] = ins[k][...].astype(F32).T
                out_ref[2, :, k * half:(k + 1) * half] = ins[2 + k][...].astype(F32).T
        return c.run(ffn_out, 'ffn_out')[0]
    if groups == 2:
        sum_d1.other, sum_d2.other = down_grads(1)
    sum_d1.send()
    sum_d2.send()
    ffn_back_step()
    sum_d1.value, sum_d2.value = down_grads(0)
    if groups == 2:
        [sum_g.other] = gate_up(1, 0)
    sum_g.send()
    [sum_g.value] = gate_up(0, 0)
    sum_d1.step()
    if groups == 2:
        [sum_u.other] = gate_up(1, 1)
    sum_u.send()
    sum_d2.step()
    [sum_u.value] = gate_up(0, 1)
    self_back(0)
    sum_d1.step()
    if groups == 2:
        self_back(1)
    sum_d2.step()
    sum_g.step()
    if groups == 2:
        [sum_s.other] = side_grads(1)
    sum_s.send()
    [sum_s.value] = side_grads(0)
    sum_d1.step()
    input_back_step()
    if groups == 2:
        sum_q1.other, sum_q2.other = self_grads(1)
    sum_q1.send()
    sum_q2.send()
    sum_q1.value, sum_q2.value = self_grads(0)
    sum_d2.step()
    sum_u.step()
    sum_g.step()
    sum_s.step()
    sum_d1.step()
    sum_u.step()
    sum_q1.step()
    sum_d2.step()
    sum_g.step()
    sum_s.step()
    sum_q2.step()
    sum_u.step()
    sum_q1.step()
    kept.last = decoder_down()
    sum_g.step()
    sum_s.step()
    sum_q2.step()
    sum_u.step()
    sum_q1.step()
    kept.out = decoder_output(kept.last)
    kept.ffn = ffn_out_step()
    sum_q2.step()
    out_rows = from_rows(order.place(kept.out))
    dx_rows = from_rows(order.place(kept.dx))
    first, second, side = [one.finish() for one in (sum_q1, sum_q2, sum_s)]
    gain_total = second[4 * width - first_rows:4 * width - first_rows + 3].astype(F32)
    c = Call(1, length, order)
    c.whole(first, second, side)
    c.out_whole((6 * width, model), F32)

    def attn_out(first_ref, second_ref, side_ref, out_ref):
        out_ref[:first_rows, :] = first_ref[...].astype(F32)
        out_ref[first_rows:4 * width, :] = second_ref[:4 * width - first_rows, :].astype(F32)
        out_ref[4 * width:, :] = side_ref[...].astype(F32)
    attn_grad = c.run(attn_out, 'attn_out')[0]
    attn_grad = attn_grad.reshape(6, width, model).transpose(0, 2, 1)
    return (out_rows[None], dx_rows[None], gain_total[None], attn_grad[None], kept.ffn[None])

def solution(mesh):
    in_specs = (P('section', 'dp', 'tensor', None), P('dp'), P('dp', 'tensor', None), P('section', None, None), P('section', None, None, 'tensor'), P('section', None, None, 'tensor'))
    out_specs = (P('section', 'dp', 'tensor', None), P('section', 'dp', 'tensor', None), P('section', None, None), P('section', None, None, 'tensor'), P('section', None, None, 'tensor'))
    return jax.shard_map(on_device, mesh=mesh, in_specs=in_specs, out_specs=out_specs, check_vma=False)
```
